256 devices in a mesh: dp: 8 (over z_hi, y), proto: 32 (over z_lo, x, core).
Axes of the slice: x: 4, y: 4, z: 8 (z_hi: 2, z_lo: 4; z = z_hi * 4 + z_lo), core: 2. Of those that a mesh axis runs over, the one named last changes fastest.
Arguments:
- teacher_global: bfloat16 [1024, 2, 256], P(('dp', 'proto')), may hold values from -700 to 700
- queue: bfloat16 [3072, 256], P(('dp', 'proto')), may hold values from -700 to 700
- student: bfloat16 [1024, 10, 256], P(('dp', 'proto')), may hold values from -700 to 700
- prototypes: bfloat16 [131072, 256], P('proto'), may hold values from -700 to 700
Outputs:
- student_grad: float32 [1024, 10, 256], P(('dp', 'proto'))
- crop_loss: float32 [1024, 10], P(('dp', 'proto'))
The draws below stay inside these ranges and needn't reach their ends.
All inputs are finite; a program needn't handle non-finite values.
Results may differ from the reference program's by a relative error of at most 0.004.
Values may be sent and summed in bfloat16 or wider, within the bound.
No kernel may reach another device: no remote copies, remote signals or barrier semaphores. Data moves between devices by JAX's collectives and lax.ppermute only.
A program may use at most 128 MiB of HBM per device.

```python
import math
import jax
import jax.numpy as jnp
from jax import lax

B = 256
PROTOS = 131072
CROPS = 10
SINK_ITERS = 3
IMAGES = 1024
QUEUE = 3072
N_PROTO = 32


LATENT_DIMS = 4


RAMP_HEIGHT = 2.6


def image_latent(key):
    return jnp.clip(jax.random.normal(key, (IMAGES, 1, LATENT_DIMS), jnp.float32), -3.0, 3.0)


def build_rows(key, latent, lead_shape, mean_shift):
    amplitude = 2.0 * math.sqrt((B - LATENT_DIMS) / LATENT_DIMS)
    key_normal = jax.random.fold_in(key, 0)
    key_scale = jax.random.fold_in(key, 2)
    noise_shape = lead_shape + (B - LATENT_DIMS,)
    normal_part = jnp.clip(jax.random.normal(key_normal, noise_shape, jnp.float32), -4.0, 4.0)
    noise = normal_part
    signal = amplitude * (latent + mean_shift)
    values = jnp.concatenate([signal, noise], axis=-1)
    row_scale = jnp.exp(jax.random.uniform(key_scale, lead_shape + (1,), jnp.float32, 0.0, math.log(10.0)))
    return jnp.clip(values * row_scale, -700.0, 700.0)


def draw_teacher_global(key, part):
    latent = image_latent(key)
    key = jax.random.fold_in(key, 11)
    key_jitter, key_rows = jax.random.split(key)
    jitter = 0.3 * jnp.clip(jax.random.normal(key_jitter, (IMAGES, 2, LATENT_DIMS), jnp.float32), -3.0, 3.0)
    values = build_rows(key_rows, latent + jitter, (IMAGES, 2), 0.0)
    return values.astype(jnp.bfloat16)


def draw_student(key, part):
    latent = image_latent(key)
    key = jax.random.fold_in(key, 19)
    key_jitter, key_rows = jax.random.split(key)
    jitter = 0.6 * jnp.clip(jax.random.normal(key_jitter, (IMAGES, CROPS, LATENT_DIMS), jnp.float32), -3.0, 3.0)
    values = build_rows(key_rows, latent + jitter, (IMAGES, CROPS), 0.0)
    return values.astype(jnp.bfloat16)


def draw_queue(key, part):
    key = jax.random.fold_in(key, 13)
    key_latent, key_rows = jax.random.split(key)
    latent = jnp.clip(jax.random.normal(key_latent, (QUEUE, LATENT_DIMS), jnp.float32), -3.0, 3.0)
    values = build_rows(key_rows, latent, (QUEUE,), 0.0)
    return values.astype(jnp.bfloat16)


def draw_prototypes(key, part):
    key = jax.random.fold_in(key, 17)
    key_latent, key_rows = jax.random.split(key)
    latent = jnp.clip(jax.random.normal(key_latent, (PROTOS, LATENT_DIMS), jnp.float32), -3.0, 3.0)
    position = jnp.arange(PROTOS).astype(jnp.float32) / PROTOS
    first_dim = (jnp.arange(LATENT_DIMS) == 0).astype(jnp.float32)
    ramp = RAMP_HEIGHT * (2.0 * position[:, None] - 1.0) * first_dim[None, :]
    values = build_rows(key_rows, latent, (PROTOS,), ramp)
    return values.astype(jnp.bfloat16)


def setup_inputs(seed: int = 0) -> dict:
    seeds = jax.random.split(jax.random.key(seed), 5)
    teacher_global = draw_teacher_global(jax.random.fold_in(seeds[4], 71), 0)
    queue = draw_queue(jax.random.fold_in(seeds[4], 71), 0)
    student = draw_student(jax.random.fold_in(seeds[4], 71), 0)
    prototypes = draw_prototypes(jax.random.fold_in(seeds[4], 71), 0)
    return dict(teacher_global=teacher_global, queue=queue, student=student, prototypes=prototypes)


TEACHER_SOFTNESS = 0.07
STUDENT_SOFTNESS = 0.1
NORM_EPSILON = 1e-06

def unit_rows(values):
    values = values.astype(jnp.float32)
    return values * lax.rsqrt(lax.optimization_barrier(jnp.sum(values * values, axis=-1, keepdims=True)) + NORM_EPSILON)

def crop_weights(crop_count):
    crop_ids = jnp.arange(crop_count)
    not_first = (crop_ids != 0).astype(jnp.float32)
    not_second = (crop_ids != 1).astype(jnp.float32)
    return (not_first, not_second, not_first + not_second)

def reference(teacher_global, queue, student, prototypes):
    teach_rows = jnp.concatenate([teacher_global.reshape(IMAGES * 2, B), queue], axis=0)
    stud_rows = student.reshape(IMAGES * CROPS, B)
    teach_unit = unit_rows(teach_rows).astype(jnp.bfloat16)
    stud_unit = unit_rows(stud_rows)
    student_reduced = stud_unit.astype(jnp.bfloat16)
    block_size = PROTOS // N_PROTO
    proto_blocks = prototypes.reshape(N_PROTO, block_size, B)

    def teacher_exponent(protos_blk):
        unit_vector_block = unit_rows(protos_blk).astype(jnp.bfloat16)
        logit_block = jnp.dot(teach_unit, unit_vector_block.T, preferred_element_type=jnp.float32)
        return jnp.exp(logit_block / TEACHER_SOFTNESS)
    sample_scale = jnp.ones((teach_rows.shape[0],), jnp.float32)
    proto_scale = jnp.ones((N_PROTO, block_size), jnp.float32)
    for iteration in range(SINK_ITERS):

        def sweep_block(protos_blk, current=sample_scale):
            teacher_exponentials = teacher_exponent(protos_blk)
            scale_blk = 1.0 / jnp.dot(current, teacher_exponentials, precision=lax.Precision.HIGHEST)
            return (scale_blk, jnp.dot(teacher_exponentials, scale_blk, precision=lax.Precision.HIGHEST))
        proto_scale, partials = lax.map(sweep_block, proto_blocks)
        sample_scale = 1.0 / lax.optimization_barrier(jnp.sum(partials, axis=0))
    first_w, second_w, pair_count = crop_weights(CROPS)
    glob_scale = sample_scale[:IMAGES * 2].reshape(IMAGES, 2)
    global_unit_rows = teach_unit[:IMAGES * 2]
    stud_count = IMAGES * CROPS

    def column_block(running, inputs):
        grand_total_sum, cross_sum, attraction_term, repulsion_term = running
        protos_blk, scale_blk = inputs
        unit_vector_block = unit_rows(protos_blk).astype(jnp.bfloat16)
        exponent_block = jnp.exp(jnp.dot(global_unit_rows, unit_vector_block.T, preferred_element_type=jnp.float32) / TEACHER_SOFTNESS)
        exponent_block = exponent_block.reshape(IMAGES, 2, block_size)
        target = exponent_block * scale_blk * glob_scale[:, :, None]
        pooled = target[:, None, 0, :] * first_w[None, :, None] + target[:, None, 1, :] * second_w[None, :, None]
        pooled = pooled.reshape(stud_count, block_size)
        score_logits = jnp.dot(student_reduced, unit_vector_block.T, preferred_element_type=jnp.float32) / STUDENT_SOFTNESS
        weights = jnp.exp(score_logits)
        grand_total_sum = grand_total_sum + lax.optimization_barrier(jnp.sum(weights, axis=1))
        cross_sum = cross_sum + lax.optimization_barrier(jnp.sum(pooled * score_logits, axis=1))
        attraction_term = attraction_term + jnp.dot(weights.astype(jnp.bfloat16), unit_vector_block, preferred_element_type=jnp.float32)
        repulsion_term = repulsion_term + jnp.dot(pooled.astype(jnp.bfloat16), unit_vector_block, preferred_element_type=jnp.float32)
        return ((grand_total_sum, cross_sum, attraction_term, repulsion_term), None)
    start_state = (jnp.zeros((stud_count,), jnp.float32), jnp.zeros((stud_count,), jnp.float32), jnp.zeros((stud_count, B), jnp.float32), jnp.zeros((stud_count, B), jnp.float32))
    (grand_total_sum, cross_sum, attraction_term, repulsion_term), unused = lax.scan(column_block, start_state, (proto_blocks, proto_scale))
    pairwise_everything = jnp.tile(pair_count, IMAGES)
    gradient_unit_rows = (pairwise_everything[:, None] * attraction_term / grand_total_sum[:, None] - repulsion_term) / STUDENT_SOFTNESS
    crop_loss = pairwise_everything * jnp.log(grand_total_sum) - cross_sum
    stud_float = stud_rows.astype(jnp.float32)
    inv_norm = lax.rsqrt(lax.optimization_barrier(jnp.sum(stud_float * stud_float, axis=1, keepdims=True)) + NORM_EPSILON)
    inner_prod = lax.optimization_barrier(jnp.sum(stud_unit * gradient_unit_rows, axis=1, keepdims=True))
    student_grad = inv_norm * (gradient_unit_rows - stud_unit * inner_prod)
    return (student_grad.reshape(IMAGES, CROPS, B), crop_loss.reshape(IMAGES, CROPS))
```

```python
import functools
import math

import jax
import jax.numpy as jnp
from jax import lax
from jax.experimental import pallas as pl
from jax.experimental.pallas import tpu as pltpu
from jax.sharding import PartitionSpec as P

SINK_ITERS = 3
TEACHER_SOFTNESS = 0.07
STUDENT_SOFTNESS = 0.1
NORM_EPSILON = 1e-06
TEACHER_EXP2 = math.log2(math.e) / TEACHER_SOFTNESS
STUDENT_EXP2 = math.log2(math.e) / STUDENT_SOFTNESS

LANES = 128
SEND_ROWS = 64
BACK_ROWS = 56
VMEM_LIMIT = 56 * 1024 * 1024

f32 = jnp.float32
bf16 = jnp.bfloat16


def iota(shape, dim):
    return lax.broadcasted_iota(jnp.int32, shape, dim)


def unit(values):
    return values * lax.rsqrt(jnp.sum(values * values, axis=-1, keepdims=True) + NORM_EPSILON)


def params(**kw):
    return pltpu.CompilerParams(vmem_limit_bytes=VMEM_LIMIT, **kw)


def pack_kernel(images, crops, queue_rows, teacher_ref, queue_ref, student_ref, out_ref, rows_ref):
    stud = images * crops
    glob = images * 2
    rest = queue_rows - 8
    for i in range(images):
        rows_ref[i * crops : (i + 1) * crops, :] = unit(student_ref[i].astype(f32))
        rows_ref[stud + 2 * i : stud + 2 * i + 2, :] = unit(teacher_ref[i].astype(f32))
    units = unit(queue_ref[...].astype(f32))
    rows_ref[stud + glob : stud + glob + queue_rows, :] = units
    rows_ref[stud + glob + queue_rows : stud + glob + queue_rows + rest, :] = units[8:]
    packed = rows_ref[...].astype(bf16)
    for j in range(out_ref.shape[0]):
        out_ref[j] = packed


def gather_rows(rows_ref, start, stop):
    return rows_ref[...].astype(f32)[:, start:stop]


def teacher_kernel(stud, glob, gathered_ref, protos_ref, unit_ref, exp_ref, sums_ref, teach_ref):
    groups = gathered_ref.shape[0]
    width = gathered_ref.shape[2]
    steps, copies = pl.num_programs(0), sums_ref.shape[0]

    @pl.when(pl.program_id(0) == 0)
    def _():
        block = gathered_ref[...].astype(f32)
        g = block[:, stud : stud + glob].reshape(groups * glob, width)
        q = block[:, stud + glob : stud + glob + 8].reshape(groups * 8, width)
        r = block[:, stud + glob + 8 : stud + glob + 16].reshape(groups // 2, 2, 8, width)
        low = iota((groups // 2, 8, width), 1) < 4
        r = jnp.where(low, r[:, 0], r[:, 1]).reshape(groups * 4, width)
        teach_ref[...] = jnp.concatenate([g, q, r], axis=0).astype(bf16)

    protos = unit(protos_ref[...].astype(f32)).astype(bf16)
    unit_ref[...] = protos
    logits = lax.dot_general(
        teach_ref[...], protos, (((1,), (1,)), ((), ())), preferred_element_type=f32
    )
    exps = jnp.exp2(logits * TEACHER_EXP2)
    exp_ref[...] = exps.astype(bf16)
    sums = jnp.sum(exps, axis=0, keepdims=True)
    for j in range(copies):
        sums_ref[j] = sums


def student_kernel(stud, gathered_ref, unit_ref, attract_ref, total_ref, rows_ref, acc_ref, tot_ref):
    groups = gathered_ref.shape[0]
    width = gathered_ref.shape[2]
    step = pl.program_id(0)
    rows = groups * stud
    chunk = 256

    @pl.when(step == 0)
    def _():
        block = gathered_ref[...].astype(f32)[:, :stud]
        rows_ref[...] = block.reshape(rows, width).astype(bf16)
        acc_ref[...] = jnp.zeros_like(acc_ref)
        tot_ref[...] = jnp.zeros_like(tot_ref)

    protos = unit_ref[...]
    cols = protos.shape[0]
    for c in range(rows // chunk):
        here = slice(c * chunk, (c + 1) * chunk)
        logits = lax.dot_general(
            rows_ref[here, :], protos, (((1,), (1,)), ((), ())), preferred_element_type=f32
        )
        weights = jnp.exp2(logits * STUDENT_EXP2)
        part = weights[:, :LANES]
        for k in range(1, cols // LANES):
            part = part + weights[:, k * LANES : (k + 1) * LANES]
        tot_ref[here, :] += part
        acc_ref[here, :] += jnp.dot(weights.astype(bf16), protos, preferred_element_type=f32)

    @pl.when(step == pl.num_programs(0) - 1)
    def _():
        attract_ref[...] = acc_ref[...].reshape(groups, stud, width)
        total = jnp.sum(tot_ref[...], axis=1, keepdims=True).reshape(groups, stud, 1)
        eye = iota((groups, stud, LANES), 1) == iota((groups, stud, LANES), 2)
        total_ref[...] = jnp.sum(
            jnp.where(eye, jnp.broadcast_to(total, (groups, stud, LANES)), 0.0),
            axis=1,
            keepdims=True,
        )


def proto_scale_of(parts_ref):
    total = parts_ref[0]
    for j in range(1, parts_ref.shape[0]):
        total = total + parts_ref[j]
    return 1.0 / total


def col_kernel(parts_ref, exp_ref, out_ref):
    scale = proto_scale_of(parts_ref)
    rows, cols = exp_ref.shape
    lines = []
    for g in range(rows // LANES):
        acc = None
        for k in range(cols // LANES):
            lanes = slice(k * LANES, (k + 1) * LANES)
            term = exp_ref[g * LANES : (g + 1) * LANES, lanes].astype(f32) * scale[:, lanes]
            acc = term if acc is None else acc + term
        lines.append(jnp.sum(acc.T, axis=0, keepdims=True))
    lines.append(jnp.ones((8 - len(lines), LANES), f32))
    out = jnp.concatenate(lines, axis=0)
    for j in range(out_ref.shape[0]):
        out_ref[j] = out


def row_kernel(parts_ref, exp_ref, out_ref):
    rows, cols = exp_ref.shape
    scale = 1.0 / jnp.sum(parts_ref[...], axis=0)
    tall = [
        jnp.broadcast_to(scale[g : g + 1, :], (LANES, LANES)).T for g in range(rows // LANES)
    ]
    for k in range(cols // LANES):
        lanes = slice(k * LANES, (k + 1) * LANES)
        acc = None
        for g in range(rows // LANES):
            term = exp_ref[g * LANES : (g + 1) * LANES, lanes].astype(f32) * tall[g]
            acc = term if acc is None else acc + term
        line = jnp.sum(acc, axis=0, keepdims=True)
        for j in range(out_ref.shape[0]):
            out_ref[j, :, lanes] = line


def repel_kernel(stud, glob, parts_ref, exp_ref, unit_ref, attract_ref, total_ref, out_ref):
    groups = out_ref.shape[0]
    scale = proto_scale_of(parts_ref)
    rows, cols = exp_ref.shape
    width = unit_ref.shape[1]
    acc = jnp.zeros((rows, LANES), f32)
    repel = jnp.zeros((rows, width), f32)
    step = 512
    for start in range(0, cols, step):
        terms = exp_ref[:, start : start + step].astype(f32) * scale[:, start : start + step]
        for k in range(step // LANES):
            acc = acc + terms[:, k * LANES : (k + 1) * LANES]
        repel = repel + jnp.dot(
            terms.astype(bf16), unit_ref[start : start + step, :], preferred_element_type=f32
        )
    sums = jnp.sum(acc, axis=1, keepdims=True).reshape(groups, glob, 1)
    place = iota((groups, glob, LANES), 1) + stud == iota((groups, glob, LANES), 2)
    sums = jnp.sum(
        jnp.where(place, jnp.broadcast_to(sums, (groups, glob, LANES)), 0.0), axis=1, keepdims=True
    )
    repel = repel.reshape(groups, glob, width)
    scalars = total_ref[...] + sums
    high = scalars.astype(bf16).astype(f32)
    scalars = jnp.concatenate([high, scalars - high], axis=2)
    scalars = jnp.broadcast_to(scalars, (groups, 8, width))
    out_ref[...] = jnp.concatenate([attract_ref[...], repel, scalars], axis=1).astype(bf16)


def final_kernel(back_ref, student_ref, grad_ref, loss_ref, rows_ref):
    images, crops, width = student_ref.shape
    stud = images * crops
    rows_ref[...] = jnp.sum(back_ref[...].astype(f32), axis=0)
    last = stud + 2 * images
    line = rows_ref[last : last + 1, :]
    line = line[:, :LANES] + line[:, LANES:]
    crop = iota((crops, 1), 0)
    sub, lane = iota((crops, LANES), 0), iota((crops, LANES), 1)
    lane_row = iota((1, LANES), 1)
    pairs = jnp.where(crop < 2, 1.0, 2.0)
    lines = jnp.broadcast_to(line, (crops, LANES))
    for i in range(images):
        views = []
        for g in range(2):
            at = stud + 2 * i + g
            mass = jnp.sum(jnp.where(lane_row == at, line, 0.0), axis=1, keepdims=True)
            views.append(rows_ref[at : at + 1, :] / mass)
        repel = jnp.where(crop != 0, views[0], 0.0) + jnp.where(crop != 1, views[1], 0.0)
        total = jnp.sum(jnp.where(lane == sub + i * crops, lines, 0.0), axis=1, keepdims=True)
        values = student_ref[i].astype(f32)
        inv_norm = lax.rsqrt(jnp.sum(values * values, axis=1, keepdims=True) + NORM_EPSILON)
        own = values * inv_norm
        low = own.astype(bf16).astype(f32)
        attract = rows_ref[i * crops : (i + 1) * crops, :]
        grad_unit = (pairs * attract / total - repel) / STUDENT_SOFTNESS
        cross = jnp.sum(low * repel, axis=1, keepdims=True) / STUDENT_SOFTNESS
        loss = pairs * jnp.log(total) - cross
        inner = jnp.sum(own * grad_unit, axis=1, keepdims=True)
        grad_ref[i] = inv_norm * (grad_unit - own * inner)
        spread = jnp.where(sub == lane, jnp.broadcast_to(loss, (crops, LANES)), 0.0)
        loss_ref[i : i + 1, :] = jnp.sum(spread, axis=0, keepdims=True)[:, :crops]


def exchange(array, axis):
    return lax.all_to_all(array, axis, 0, 0, tiled=True)


def body(teacher_global, queue, student, prototypes):
    images, crops, width = student.shape
    queue_rows = queue.shape[0]
    groups, parts = lax.axis_size("proto"), lax.axis_size("dp")
    stud, glob = images * crops, images * 2
    teach_rows = groups * (glob + queue_rows)
    protos = prototypes.shape[0]
    shape = jax.ShapeDtypeStruct

    packed = pl.pallas_call(
        functools.partial(pack_kernel, images, crops, queue_rows),
        out_shape=shape((groups, SEND_ROWS, width), bf16),
        scratch_shapes=[pltpu.VMEM((SEND_ROWS, width), f32)],
        compiler_params=params(),
        name="pack_rows",
    )(teacher_global, queue, student)
    gathered = exchange(packed, "proto")

    block = 512
    all_rows = pl.BlockSpec((groups, SEND_ROWS, width), lambda i: (0, 0, 0))
    unit_protos, exps, row_parts = pl.pallas_call(
        functools.partial(teacher_kernel, stud, glob),
        grid=(protos // block,),
        in_specs=[all_rows, pl.BlockSpec((block, width), lambda i: (i, 0))],
        out_specs=[
            pl.BlockSpec((block, width), lambda i: (i, 0)),
            pl.BlockSpec((teach_rows, block), lambda i: (0, i)),
            pl.BlockSpec((parts, 1, block), lambda i: (0, 0, i)),
        ],
        out_shape=[
            shape((protos, width), bf16),
            shape((teach_rows, protos), bf16),
            shape((parts, 1, protos), f32),
        ],
        scratch_shapes=[pltpu.VMEM((teach_rows, width), bf16)],
        compiler_params=params(),
        name="teacher_exponentials",
    )(gathered, prototypes)

    block = 1024
    attract, total = pl.pallas_call(
        functools.partial(student_kernel, stud),
        grid=(protos // block,),
        in_specs=[all_rows, pl.BlockSpec((block, width), lambda i: (i, 0))],
        out_specs=[
            pl.BlockSpec((groups, stud, width), lambda i: (0, 0, 0)),
            pl.BlockSpec((groups, 1, LANES), lambda i: (0, 0, 0)),
        ],
        out_shape=[shape((groups, stud, width), f32), shape((groups, 1, LANES), f32)],
        scratch_shapes=[
            pltpu.VMEM((groups * stud, width), bf16),
            pltpu.VMEM((groups * stud, width), f32),
            pltpu.VMEM((groups * stud, LANES), f32),
        ],
        compiler_params=params(),
        name="student_attract",
    )(gathered, unit_protos)

    for iteration in range(SINK_ITERS - 1):
        row_parts = exchange(row_parts, "dp")
        col_parts = pl.pallas_call(
            col_kernel,
            out_shape=shape((groups, 8, LANES), f32),
            compiler_params=params(),
            name="sum_over_prototypes",
        )(row_parts, exps)
        col_parts = exchange(col_parts, "proto")
        row_parts = pl.pallas_call(
            row_kernel,
            out_shape=shape((parts, 1, protos), f32),
            compiler_params=params(),
            name="sum_over_rows",
        )(col_parts, exps)
    row_parts = exchange(row_parts, "dp")

    whole = lambda *dims: pl.BlockSpec(dims, lambda i: (0,) * len(dims))
    back = pl.pallas_call(
        functools.partial(repel_kernel, stud, glob),
        grid=(1,),
        in_specs=[
            whole(parts, 1, protos),
            whole(groups * glob, protos),
            whole(protos, width),
            whole(groups, stud, width),
            whole(groups, 1, LANES),
        ],
        out_specs=whole(groups, BACK_ROWS, width),
        out_shape=shape((groups, BACK_ROWS, width), bf16),
        compiler_params=params(),
        name="repel",
    )(row_parts, exps, unit_protos, attract, total)
    back = exchange(back, "proto")

    return pl.pallas_call(
        final_kernel,
        out_shape=[shape((images, crops, width), f32), shape((images, crops), f32)],
        scratch_shapes=[pltpu.VMEM((BACK_ROWS, width), f32)],
        compiler_params=params(),
        name="gradients",
    )(back, student)


def solution(mesh):
    in_specs = (
        P(("dp", "proto"), None, None),
        P(("dp", "proto"), None),
        P(("dp", "proto"), None, None),
        P("proto", None),
    )
    out_specs = (P(("dp", "proto"), None, None), P(("dp", "proto"), None))
    return jax.shard_map(body, mesh=mesh, in_specs=in_specs, out_specs=out_specs, check_vma=False)
```

```python
import functools
import math

import jax
import jax.numpy as jnp
from jax import lax
from jax.experimental import pallas as pl
from jax.experimental.pallas import tpu as pltpu
from jax.sharding import PartitionSpec as P

SINK_ITERS = 3
TEACHER_SOFTNESS = 0.07
STUDENT_SOFTNESS = 0.1
NORM_EPSILON = 1e-06
TEACHER_EXP2 = math.log2(math.e) / TEACHER_SOFTNESS
STUDENT_EXP2 = math.log2(math.e) / STUDENT_SOFTNESS

LANES = 128
MIB = 1024 * 1024

f32 = jnp.float32
bf16 = jnp.bfloat16
shape = jax.ShapeDtypeStruct


def iota(shape, dim):
    return lax.broadcasted_iota(jnp.int32, shape, dim)


def unit(values):
    return values * lax.rsqrt(jnp.sum(values * values, axis=-1, keepdims=True) + NORM_EPSILON)


def nt_dot(a, b):
    return lax.dot_general(a, b, (((1,), (1,)), ((), ())), preferred_element_type=f32)


def call(kernel, name, out_shape, flops=0, nbytes=0, exps=0, vmem=32, **kw):
    return pl.pallas_call(
        kernel,
        out_shape=out_shape,
        compiler_params=pltpu.CompilerParams(vmem_limit_bytes=vmem * MIB),
        cost_estimate=pl.CostEstimate(flops=flops, bytes_accessed=nbytes, transcendentals=exps),
        name=name,
        **kw,
    )


def in_vmem(array):
    return pltpu.with_memory_space_constraint(array, pltpu.VMEM)


def pack_kernel(student_ref, teacher_ref, queue_ref, out_ref, rows_ref):
    crops, images, _ = student_ref.shape
    queue_rows = queue_ref.shape[0]
    stud = crops * images
    for c in range(crops):
        rows_ref[c * images : (c + 1) * images, :] = unit(student_ref[c].astype(f32))
    for i in range(images):
        views = unit(teacher_ref[i].astype(f32))
        rows_ref[stud + i : stud + i + 1, :] = views[1:2]
        rows_ref[stud + images + i : stud + images + i + 1, :] = views[0:1]
    units = unit(queue_ref[...].astype(f32))
    at = stud + 2 * images
    rows_ref[at : at + queue_rows, :] = units
    rows_ref[at + queue_rows :, :] = units[8:]
    packed = rows_ref[...].astype(bf16)
    for j in range(out_ref.shape[0]):
        out_ref[j] = packed


def unit_kernel(protos_ref, out_ref):
    out_ref[...] = unit(protos_ref[...].astype(f32)).astype(bf16)


def by_core(core_ref, own, other):
    is_first = core_ref[0] == 0
    return jnp.where(is_first, own, other), jnp.where(is_first, other, own)


def teacher_kernel(stud, glob, core_ref, own_ref, other_ref, unit_ref, exp_ref, sums_ref):
    chips, _, width = own_ref.shape
    blocks = by_core(core_ref, own_ref[...].astype(f32)[:, stud:], other_ref[...].astype(f32)[:, stud:])
    block = jnp.concatenate(blocks, axis=0)
    groups = 2 * chips
    g = block[:, :glob].reshape(groups * glob, width)
    q = block[:, glob : glob + 8].reshape(groups * 8, width)
    r = block[:, glob + 8 :].reshape(chips, 2, 8, width)
    low = iota((chips, 8, width), 1) < 4
    r = jnp.where(low, r[:, 0], r[:, 1]).reshape(groups * 4, width)
    teach = jnp.concatenate([g, q, r], axis=0).astype(bf16)
    step = 256
    for start in range(0, unit_ref.shape[0], step):
        here = slice(start, start + step)
        exps = jnp.exp2(nt_dot(teach, unit_ref[here, :]) * TEACHER_EXP2)
        exp_ref[:, here] = exps.astype(bf16)
        sums = jnp.sum(exps, axis=0, keepdims=True)
        for j in range(sums_ref.shape[0]):
            sums_ref[j, :, here] = sums


def student_kernel(stud, core_ref, rows_ref, unit_ref, keep_ref, send_ref, total_ref, stud_ref, acc_ref, tot_ref):
    chips, _, width = rows_ref.shape
    step = pl.program_id(0)
    rows = chips * stud
    chunk = 128

    @pl.when(step == 0)
    def _():
        block = rows_ref[...].astype(f32)[:, :stud]
        stud_ref[...] = block.reshape(rows, width).astype(bf16)
        acc_ref[...] = jnp.zeros_like(acc_ref)
        tot_ref[...] = jnp.zeros_like(tot_ref)

    protos = unit_ref[...]
    cols = protos.shape[0]
    for c in range(rows // chunk):
        here = slice(c * chunk, (c + 1) * chunk)
        weights = jnp.exp2(nt_dot(stud_ref[here, :], protos) * STUDENT_EXP2)
        part = weights[:, :LANES]
        for k in range(1, cols // LANES):
            part = part + weights[:, k * LANES : (k + 1) * LANES]
        tot_ref[here, :] += part
        acc_ref[here, :] += jnp.dot(weights.astype(bf16), protos, preferred_element_type=f32)

    @pl.when(step == pl.num_programs(0) - 1)
    def _():
        attract = acc_ref[...].reshape(chips, stud, width)
        is_first = core_ref[0] == 0
        low, high = attract[:, :, :LANES], attract[:, :, LANES:]
        keep_ref[...] = jnp.where(is_first, low, high)
        send_ref[...] = jnp.where(is_first, high, low).astype(bf16)
        total = jnp.sum(tot_ref[...], axis=1, keepdims=True).reshape(chips, stud, 1)
        eye = iota((chips, stud, LANES), 1) == iota((chips, stud, LANES), 2)
        total_ref[...] = jnp.sum(
            jnp.where(eye, jnp.broadcast_to(total, (chips, stud, LANES)), 0.0),
            axis=1,
            keepdims=True,
        )


def proto_scale_of(parts_ref):
    total = parts_ref[0]
    for j in range(1, parts_ref.shape[0]):
        total = total + parts_ref[j]
    return 1.0 / total


def col_kernel(parts_ref, exp_ref, out_ref):
    scale = proto_scale_of(parts_ref)
    rows, cols = exp_ref.shape
    lines = []
    for g in range(rows // LANES):
        acc = None
        for k in range(cols // LANES):
            lanes = slice(k * LANES, (k + 1) * LANES)
            term = exp_ref[g * LANES : (g + 1) * LANES, lanes].astype(f32) * scale[:, lanes]
            acc = term if acc is None else acc + term
        lines.append(jnp.sum(acc.T, axis=0, keepdims=True))
    lines.append(jnp.ones((8 - len(lines), LANES), f32))
    out = jnp.concatenate(lines, axis=0)
    for j in range(out_ref.shape[0]):
        out_ref[j] = out


def row_kernel(parts_ref, exp_ref, out_ref):
    rows, cols = exp_ref.shape
    scale = 1.0 / jnp.sum(parts_ref[...], axis=0)
    tall = [
        jnp.broadcast_to(scale[g : g + 1, :], (LANES, LANES)).T for g in range(rows // LANES)
    ]
    for k in range(cols // LANES):
        lanes = slice(k * LANES, (k + 1) * LANES)
        acc = None
        for g in range(rows // LANES):
            term = exp_ref[g * LANES : (g + 1) * LANES, lanes].astype(f32) * tall[g]
            acc = term if acc is None else acc + term
        line = jnp.sum(acc, axis=0, keepdims=True)
        for j in range(out_ref.shape[0]):
            out_ref[j, :, lanes] = line


def repel_kernel(
    core_ref, parts_ref, exp_ref, unit_ref, keep_own, keep_other, got_own, got_other, tot_own, tot_other, out_ref
):
    chips, stud, _ = keep_own.shape
    glob = 8
    rows = 2 * chips * glob
    scale = proto_scale_of(parts_ref)
    cols, width = unit_ref.shape
    acc = jnp.zeros((rows, LANES), f32)
    repel = jnp.zeros((rows, width), f32)
    step = 512
    for start in range(0, cols, step):
        here = slice(start, start + step)
        terms = exp_ref[:rows, here].astype(f32) * scale[:, here]
        for k in range(step // LANES):
            acc = acc + terms[:, k * LANES : (k + 1) * LANES]
        repel = repel + jnp.dot(terms.astype(bf16), unit_ref[here, :], preferred_element_type=f32)
    sums = jnp.sum(acc, axis=1, keepdims=True).reshape(2, chips, glob, 1)
    repel = repel.reshape(2, chips, glob, width)
    attract = by_core(
        core_ref, keep_own[...] + got_own[...].astype(f32), keep_other[...] + got_other[...].astype(f32)
    )
    totals = by_core(core_ref, tot_own[...], tot_other[...])
    dims = (chips, glob, LANES)
    place = iota(dims, 1) + stud == iota(dims, 2)
    for core in range(2):
        mass = jnp.where(place, jnp.broadcast_to(sums[core], dims), 0.0)
        scalars = totals[core] + jnp.sum(mass, axis=1, keepdims=True)
        high = scalars.astype(bf16).astype(f32)
        scalars = jnp.where(iota(dims, 1) == 0, high, scalars - high)
        parts = [attract[core], repel[core][:, :, :LANES], repel[core][:, :, LANES:], scalars]
        out_ref[:, core] = jnp.concatenate(parts, axis=1).astype(bf16)


def final_kernel(back_ref, student_ref, grad_ref, loss_ref, rows_ref):
    crops, images, width = student_ref.shape
    stud = crops * images
    for c in range(crops):
        rows_ref[c * images : (c + 1) * images, :] = student_ref[c].astype(f32)
    values = rows_ref[...]
    back = jnp.sum(back_ref[...].astype(f32), axis=0)
    attract = jnp.concatenate([back[0, :stud], back[1, :stud]], axis=1)
    back = back[0, stud:] + back[1, stud:]
    line = back[16:17] + back[17:18]
    sub, lane = iota((stud, LANES), 0), iota((stud, LANES), 1)
    lines = jnp.broadcast_to(line, (stud, LANES))
    total = jnp.sum(jnp.where(lane == sub, lines, 0.0), axis=1, keepdims=True)
    mass = jnp.sum(jnp.where(lane == sub + stud, lines, 0.0)[:8], axis=1, keepdims=True)
    views = jnp.concatenate([back[:8], back[8:16]], axis=1) / mass
    both = views + jnp.concatenate([views[images:], views[:images]], axis=0)
    repel = jnp.concatenate([views] + [both] * (stud // 8 - 1), axis=0)
    pairs = jnp.where(iota((stud, 1), 0) < 2 * images, 1.0, 2.0)
    inv_norm = lax.rsqrt(jnp.sum(values * values, axis=1, keepdims=True) + NORM_EPSILON)
    own = values * inv_norm
    low = own.astype(bf16).astype(f32)
    grad_unit = (pairs * attract / total - repel) / STUDENT_SOFTNESS
    cross = jnp.sum(low * repel, axis=1, keepdims=True) / STUDENT_SOFTNESS
    loss = pairs * jnp.log(total) - cross
    inner = jnp.sum(own * grad_unit, axis=1, keepdims=True)
    grad = inv_norm * (grad_unit - own * inner)
    for c in range(crops):
        grad_ref[c] = grad[c * images : (c + 1) * images]
    wide = jnp.broadcast_to(loss, (stud, LANES))
    for i in range(images):
        spread = jnp.where(sub == lane * images + i, wide, 0.0)
        loss_ref[i : i + 1, :] = jnp.sum(spread, axis=0, keepdims=True)[:, :crops]


def exchange(array, axis, **kw):
    return lax.all_to_all(array, axis, 0, 0, tiled=True, **kw)


def body(teacher_global, queue, student, prototypes):
    images, crops, width = student.shape
    queue_rows = queue.shape[0]
    groups, parts = lax.axis_size("proto"), lax.axis_size("dp")
    chips = groups // 2
    stud, glob = images * crops, images * 2
    teach_rows = groups * (glob + queue_rows)
    protos = prototypes.shape[0]
    student = jnp.transpose(student, (1, 0, 2))
    core = jnp.reshape(lax.axis_index("proto") % 2, (1,))
    scalar = pl.BlockSpec(memory_space=pltpu.SMEM)
    vmem = pl.BlockSpec(memory_space=pltpu.VMEM)

    def swap(array):
        return lax.ppermute(array, "proto", [(j, j ^ 1) for j in range(groups)])

    send_rows = stud + glob + queue_rows + 4
    packed = call(
        pack_kernel,
        "pack_rows",
        shape((chips, send_rows, width), bf16),
        scratch_shapes=[pltpu.VMEM((send_rows, width), f32)],
    )(student, teacher_global, queue)
    same_core = [list(range(c, groups, 2)) for c in range(2)]
    own_rows = exchange(packed, "proto", axis_index_groups=same_core)
    other_rows = swap(own_rows)
    unit_protos = call(
        unit_kernel,
        "unit_prototypes",
        shape((protos, width), bf16),
        grid=(4,),
        in_specs=[pl.BlockSpec((protos // 4, width), lambda i: (i, 0))],
        out_specs=pl.BlockSpec((protos // 4, width), lambda i: (i, 0)),
        flops=3 * protos * width,
        nbytes=4 * protos * width,
    )(prototypes)

    exps, row_parts = call(
        functools.partial(teacher_kernel, stud, glob),
        "teacher_exponentials",
        [pltpu.VMEM((teach_rows, protos), bf16), shape((parts, 1, protos), f32)],
        in_specs=[scalar, vmem, vmem, vmem],
        flops=2 * teach_rows * protos * width,
        nbytes=2 * teach_rows * protos,
        exps=teach_rows * protos,
    )(core, own_rows, other_rows, unit_protos)
    exps = in_vmem(exps)

    def students(rows):
        block = 1024
        fixed = lambda *dims: pl.BlockSpec(dims, lambda i: (0,) * len(dims))
        return call(
            functools.partial(student_kernel, stud),
            "student_attract",
            [
                shape((chips, stud, LANES), f32),
                shape((chips, stud, LANES), bf16),
                shape((chips, 1, LANES), f32),
            ],
            grid=(protos // block,),
            in_specs=[
                scalar,
                fixed(chips, send_rows, width),
                pl.BlockSpec((block, width), lambda i: (i, 0)),
            ],
            out_specs=[
                fixed(chips, stud, LANES),
                fixed(chips, stud, LANES),
                fixed(chips, 1, LANES),
            ],
            scratch_shapes=[
                pltpu.VMEM((chips * stud, width), bf16),
                pltpu.VMEM((chips * stud, width), f32),
                pltpu.VMEM((chips * stud, LANES), f32),
            ],
            flops=4 * chips * stud * protos * width,
            nbytes=2 * protos * width,
            exps=chips * stud * protos,
        )(core, rows, unit_protos)

    student_parts = []
    for rows in (own_rows, other_rows):
        row_parts, student_part = lax.optimization_barrier((exchange(row_parts, "dp"), students(rows)))
        student_parts.append(student_part)
        col_parts = call(
            col_kernel,
            "sum_over_prototypes",
            shape((groups, 8, LANES), f32),
            flops=2 * teach_rows * protos,
            nbytes=2 * teach_rows * protos,
        )(row_parts, exps)
        col_parts = exchange(col_parts, "proto")
        row_parts = call(
            row_kernel,
            "sum_over_rows",
            shape((parts, 1, protos), f32),
            flops=2 * teach_rows * protos,
            nbytes=2 * teach_rows * protos,
        )(col_parts, exps)
    row_parts = exchange(row_parts, "dp")

    (keep_own, send_own, tot_own), (keep_other, send_other, tot_other) = student_parts
    got_other, got_own = swap(send_own), swap(send_other)
    back = call(
        repel_kernel,
        "repel",
        shape((chips, 2, 64, LANES), bf16),
        in_specs=[scalar] + [vmem] * 9,
        flops=2 * groups * glob * protos * width,
        nbytes=2 * protos * width,
    )(core, row_parts, exps, unit_protos, keep_own, keep_other, got_own, got_other, tot_own, tot_other)
    back = exchange(back.reshape(groups, 64, LANES), "proto").reshape(chips, 2, 64, LANES)

    grad, loss = call(
        final_kernel,
        "gradients",
        [shape((crops, images, width), f32), shape((images, crops), f32)],
        scratch_shapes=[pltpu.VMEM((stud, width), f32)],
    )(back, student)
    return jnp.transpose(grad, (1, 0, 2)), loss


def solution(mesh):
    in_specs = (
        P(("dp", "proto"), None, None),
        P(("dp", "proto"), None),
        P(("dp", "proto"), None, None),
        P("proto", None),
    )
    out_specs = (P(("dp", "proto"), None, None), P(("dp", "proto"), None))
    return jax.shard_map(body, mesh=mesh, in_specs=in_specs, out_specs=out_specs, check_vma=False)
```

```python
import functools
import math

import jax
import jax.numpy as jnp
from jax import lax
from jax.experimental import pallas as pl
from jax.experimental.pallas import tpu as pltpu
from jax.sharding import PartitionSpec as P

SINK_ITERS = 3
TEACHER_SOFTNESS = 0.07
STUDENT_SOFTNESS = 0.1
NORM_EPSILON = 1e-06
TEACHER_EXP2 = math.log2(math.e) / TEACHER_SOFTNESS
STUDENT_EXP2 = math.log2(math.e) / STUDENT_SOFTNESS

LANES = 128
MIB = 1024 * 1024

f32 = jnp.float32
bf16 = jnp.bfloat16
shape = jax.ShapeDtypeStruct


def iota(shape, dim):
    return lax.broadcasted_iota(jnp.int32, shape, dim)


def unit(values):
    return values * lax.rsqrt(jnp.sum(values * values, axis=-1, keepdims=True) + NORM_EPSILON)


def nt_dot(a, b):
    return lax.dot_general(a, b, (((1,), (1,)), ((), ())), preferred_element_type=f32)


def call(kernel, name, out_shape, flops=0, nbytes=0, exps=0, vmem=32, **kw):
    return pl.pallas_call(
        kernel,
        out_shape=out_shape,
        compiler_params=pltpu.CompilerParams(vmem_limit_bytes=vmem * MIB),
        cost_estimate=pl.CostEstimate(flops=flops, bytes_accessed=nbytes, transcendentals=exps),
        name=name,
        **kw,
    )


def in_vmem(array):
    return pltpu.with_memory_space_constraint(array, pltpu.VMEM)


def pack_kernel(student_ref, teacher_ref, queue_ref, out_ref, rows_ref):
    crops, images, _ = student_ref.shape
    queue_rows = queue_ref.shape[0]
    stud = crops * images
    for c in range(crops):
        rows_ref[c * images : (c + 1) * images, :] = unit(student_ref[c].astype(f32))
    for i in range(images):
        views = unit(teacher_ref[i].astype(f32))
        rows_ref[stud + i : stud + i + 1, :] = views[1:2]
        rows_ref[stud + images + i : stud + images + i + 1, :] = views[0:1]
    units = unit(queue_ref[...].astype(f32))
    at = stud + 2 * images
    rows_ref[at : at + queue_rows, :] = units
    rows_ref[at + queue_rows :, :] = units[8:]
    packed = rows_ref[...].astype(bf16)
    for j in range(out_ref.shape[0]):
        out_ref[j] = packed


def unit_kernel(protos_ref, out_ref):
    out_ref[...] = unit(protos_ref[...].astype(f32)).astype(bf16)


def by_core(core_ref, own, other):
    is_first = core_ref[0] == 0
    return jnp.where(is_first, own, other), jnp.where(is_first, other, own)


def teacher_kernel(stud, glob, core_ref, own_ref, other_ref, unit_ref, exp_ref, sums_ref):
    chips, _, width = own_ref.shape
    blocks = by_core(core_ref, own_ref[...].astype(f32)[:, stud:], other_ref[...].astype(f32)[:, stud:])
    block = jnp.concatenate(blocks, axis=0)
    groups = 2 * chips
    g = block[:, :glob].reshape(groups * glob, width)
    q = block[:, glob : glob + 8].reshape(groups * 8, width)
    r = block[:, glob + 8 :].reshape(chips, 2, 8, width)
    low = iota((chips, 8, width), 1) < 4
    r = jnp.where(low, r[:, 0], r[:, 1]).reshape(groups * 4, width)
    teach = jnp.concatenate([g, q, r], axis=0).astype(bf16)
    step = 256
    for start in range(0, unit_ref.shape[0], step):
        here = slice(start, start + step)
        exps = jnp.exp2(nt_dot(teach, unit_ref[here, :]) * TEACHER_EXP2)
        exp_ref[:, here] = exps.astype(bf16)
        sums_ref[0, :, here] = jnp.sum(exps, axis=0, keepdims=True)


def student_kernel(
    stud, core_ref, own_ref, other_ref, unit_ref, keep_ref, send_ref, total_ref, stud_ref, acc_ref, tot_ref
):
    chips, _, width = own_ref.shape
    rows = chips * stud
    for h, rows_ref in enumerate((own_ref, other_ref)):
        block = rows_ref[...].astype(f32)[:, :stud]
        stud_ref[h * rows : (h + 1) * rows, :] = block.reshape(rows, width).astype(bf16)
    step = 512
    chunk = rows
    for start in range(0, unit_ref.shape[0], step):
        protos = unit_ref[start : start + step, :]
        for c in range(2 * rows // chunk):
            here = slice(c * chunk, (c + 1) * chunk)
            weights = jnp.exp2(nt_dot(stud_ref[here, :], protos) * STUDENT_EXP2)
            part = weights[:, :LANES]
            for k in range(1, step // LANES):
                part = part + weights[:, k * LANES : (k + 1) * LANES]
            term = jnp.dot(weights.astype(bf16), protos, preferred_element_type=f32)
            if start == 0:
                tot_ref[here, :] = part
                acc_ref[here, :] = term
            else:
                tot_ref[here, :] += part
                acc_ref[here, :] += term
    is_first = core_ref[0] == 0
    for h in range(2):
        here = slice(h * rows, (h + 1) * rows)
        attract = acc_ref[here, :].reshape(chips, stud, width)
        low, high = attract[:, :, :LANES], attract[:, :, LANES:]
        keep_ref[h] = jnp.where(is_first, low, high)
        send_ref[h] = jnp.where(is_first, high, low).astype(bf16)
        total = jnp.sum(tot_ref[here, :], axis=1, keepdims=True).reshape(chips, stud, 1)
        eye = iota((chips, stud, LANES), 1) == iota((chips, stud, LANES), 2)
        total_ref[h] = jnp.sum(
            jnp.where(eye, jnp.broadcast_to(total, (chips, stud, LANES)), 0.0),
            axis=1,
            keepdims=True,
        )


def pair_kernel(mine_ref, got_ref, out_ref):
    total = mine_ref[0] + got_ref[0]
    for j in range(out_ref.shape[0]):
        out_ref[j] = total


def proto_scale_of(parts_ref):
    total = parts_ref[0]
    for j in range(1, parts_ref.shape[0]):
        total = total + parts_ref[j]
    return 1.0 / total


def col_kernel(parts_ref, exp_ref, out_ref):
    scale = proto_scale_of(parts_ref)
    rows, cols = exp_ref.shape
    lines = []
    for g in range(rows // LANES):
        acc = None
        for k in range(cols // LANES):
            lanes = slice(k * LANES, (k + 1) * LANES)
            term = exp_ref[g * LANES : (g + 1) * LANES, lanes].astype(f32) * scale[:, lanes]
            acc = term if acc is None else acc + term
        lines.append(jnp.sum(acc.T, axis=0, keepdims=True))
    lines.append(jnp.ones((8 - len(lines), LANES), f32))
    out = jnp.concatenate(lines, axis=0)
    for j in range(out_ref.shape[0]):
        out_ref[j] = out


def row_kernel(parts_ref, exp_ref, out_ref):
    rows, cols = exp_ref.shape
    scale = 1.0 / jnp.sum(parts_ref[...], axis=0)
    acc = None
    for g in range(rows // LANES):
        tall = jnp.broadcast_to(scale[g : g + 1, :], (LANES, LANES)).T
        for t in range(0, LANES, 16):
            wide = jnp.concatenate([tall[t : t + 16]] * (cols // LANES), axis=1)
            term = exp_ref[g * LANES + t : g * LANES + t + 16, :].astype(f32) * wide
            term = term[:8] + term[8:]
            acc = term if acc is None else acc + term
    line = jnp.sum(acc, axis=0, keepdims=True)
    for j in range(out_ref.shape[0]):
        out_ref[j] = line


def repel_kernel(
    core_ref, parts_ref, exp_ref, unit_ref, keep_ref, got_ref, total_ref, out_ref
):
    _, chips, stud, _ = keep_ref.shape
    glob = 8
    rows = 2 * chips * glob
    scale = proto_scale_of(parts_ref)
    cols, width = unit_ref.shape
    acc = jnp.zeros((rows, LANES), f32)
    repel = jnp.zeros((rows, width), f32)
    step = 512
    for start in range(0, cols, step):
        here = slice(start, start + step)
        terms = exp_ref[:rows, here].astype(f32) * scale[:, here]
        for k in range(step // LANES):
            acc = acc + terms[:, k * LANES : (k + 1) * LANES]
        repel = repel + jnp.dot(terms.astype(bf16), unit_ref[here, :], preferred_element_type=f32)
    sums = jnp.sum(acc, axis=1, keepdims=True).reshape(2, chips, glob, 1)
    repel = repel.reshape(2, chips, glob, width)
    attract = by_core(
        core_ref, keep_ref[0] + got_ref[1].astype(f32), keep_ref[1] + got_ref[0].astype(f32)
    )
    totals = by_core(core_ref, total_ref[0], total_ref[1])
    dims = (chips, glob, LANES)
    place = iota(dims, 1) + stud == iota(dims, 2)
    for core in range(2):
        mass = jnp.where(place, jnp.broadcast_to(sums[core], dims), 0.0)
        scalars = totals[core] + jnp.sum(mass, axis=1, keepdims=True)
        high = scalars.astype(bf16).astype(f32)
        scalars = jnp.where(iota(dims, 1) == 0, high, scalars - high)
        parts = [attract[core], repel[core][:, :, :LANES], repel[core][:, :, LANES:], scalars]
        out_ref[:, core] = jnp.concatenate(parts, axis=1).astype(bf16)


def final_kernel(back_ref, student_ref, grad_ref, loss_ref, rows_ref):
    crops, images, width = student_ref.shape
    stud = crops * images
    for c in range(crops):
        rows_ref[c * images : (c + 1) * images, :] = student_ref[c].astype(f32)
    values = rows_ref[...]
    back = jnp.sum(back_ref[...].astype(f32), axis=0)
    attract = jnp.concatenate([back[0, :stud], back[1, :stud]], axis=1)
    back = back[0, stud:] + back[1, stud:]
    line = back[16:17] + back[17:18]
    sub, lane = iota((stud, LANES), 0), iota((stud, LANES), 1)
    lines = jnp.broadcast_to(line, (stud, LANES))
    total = jnp.sum(jnp.where(lane == sub, lines, 0.0), axis=1, keepdims=True)
    mass = jnp.sum(jnp.where(lane == sub + stud, lines, 0.0)[:8], axis=1, keepdims=True)
    views = jnp.concatenate([back[:8], back[8:16]], axis=1) / mass
    both = views + jnp.concatenate([views[images:], views[:images]], axis=0)
    repel = jnp.concatenate([views] + [both] * (stud // 8 - 1), axis=0)
    pairs = jnp.where(iota((stud, 1), 0) < 2 * images, 1.0, 2.0)
    inv_norm = lax.rsqrt(jnp.sum(values * values, axis=1, keepdims=True) + NORM_EPSILON)
    own = values * inv_norm
    low = own.astype(bf16).astype(f32)
    grad_unit = (pairs * attract / total - repel) / STUDENT_SOFTNESS
    cross = jnp.sum(low * repel, axis=1, keepdims=True) / STUDENT_SOFTNESS
    loss = pairs * jnp.log(total) - cross
    inner = jnp.sum(own * grad_unit, axis=1, keepdims=True)
    grad = inv_norm * (grad_unit - own * inner)
    for c in range(crops):
        grad_ref[c] = grad[c * images : (c + 1) * images]
    wide = jnp.broadcast_to(loss, (stud, LANES))
    for i in range(images):
        spread = jnp.where(sub == lane * images + i, wide, 0.0)
        loss_ref[i : i + 1, :] = jnp.sum(spread, axis=0, keepdims=True)[:, :crops]


def exchange(array, axis, **kw):
    return lax.all_to_all(array, axis, 0, 0, tiled=True, **kw)


def body(teacher_global, queue, student, prototypes):
    images, crops, width = student.shape
    queue_rows = queue.shape[0]
    groups, parts = lax.axis_size("proto"), lax.axis_size("dp")
    chips = groups // 2
    stud, glob = images * crops, images * 2
    teach_rows = groups * (glob + queue_rows)
    protos = prototypes.shape[0]
    student = jnp.transpose(student, (1, 0, 2))
    core = jnp.reshape(lax.axis_index("proto") % 2, (1,))
    scalar = pl.BlockSpec(memory_space=pltpu.SMEM)
    vmem = pl.BlockSpec(memory_space=pltpu.VMEM)

    def swap(array):
        return lax.ppermute(array, "proto", [(j, j ^ 1) for j in range(groups)])

    send_rows = stud + glob + queue_rows + 4
    packed = call(
        pack_kernel,
        "pack_rows",
        shape((chips, send_rows, width), bf16),
        scratch_shapes=[pltpu.VMEM((send_rows, width), f32)],
    )(*(pltpu.with_memory_space_constraint(a, pltpu.HBM) for a in (student, teacher_global, queue)))
    same_core = [list(range(c, groups, 2)) for c in range(2)]
    own_rows = exchange(packed, "proto", axis_index_groups=same_core)
    other_rows = swap(own_rows)
    unit_protos = call(
        unit_kernel,
        "unit_prototypes",
        shape((protos, width), bf16),
        grid=(4,),
        in_specs=[pl.BlockSpec((protos // 4, width), lambda i: (i, 0))],
        out_specs=pl.BlockSpec((protos // 4, width), lambda i: (i, 0)),
        flops=3 * protos * width,
        nbytes=4 * protos * width,
    )(prototypes)

    exps, row_parts = call(
        functools.partial(teacher_kernel, stud, glob),
        "teacher_exponentials",
        [pltpu.VMEM((teach_rows, protos), bf16), shape((1, 1, protos), f32)],
        in_specs=[scalar, vmem, vmem, vmem],
        flops=2 * teach_rows * protos * width,
        nbytes=2 * teach_rows * protos,
        exps=teach_rows * protos,
    )(core, own_rows, other_rows, unit_protos)
    exps = in_vmem(exps)

    half = parts // 2
    got_sums = lax.ppermute(row_parts, "dp", [(j, (j + half) % parts) for j in range(parts)])
    all_rows = 2 * chips * stud
    keep, send, total = call(
        functools.partial(student_kernel, stud),
        "student_attract",
        [
            shape((2, chips, stud, LANES), f32),
            shape((2, chips, stud, LANES), bf16),
            shape((2, chips, 1, LANES), f32),
        ],
        in_specs=[scalar, vmem, vmem, vmem],
        scratch_shapes=[
            pltpu.VMEM((all_rows, width), bf16),
            pltpu.VMEM((all_rows, width), f32),
            pltpu.VMEM((all_rows, LANES), f32),
        ],
        flops=4 * all_rows * protos * width,
        nbytes=2 * protos * width,
        exps=all_rows * protos,
    )(core, own_rows, other_rows, unit_protos)
    got_sums, keep, send, total = lax.optimization_barrier((got_sums, keep, send, total))
    row_parts = call(pair_kernel, "add_halves", shape((half, 1, protos), f32))(row_parts, got_sums)
    halves = [list(range(half)), list(range(half, parts))]
    row_parts = exchange(row_parts, "dp", axis_index_groups=halves)

    for iteration in range(SINK_ITERS - 1):
        col_parts = call(
            col_kernel,
            "sum_over_prototypes",
            shape((groups, 8, LANES), f32),
            flops=2 * teach_rows * protos,
            nbytes=2 * teach_rows * protos,
        )(row_parts, exps)
        col_parts = exchange(col_parts, "proto")
        if iteration == 0:
            col_parts, send = lax.optimization_barrier((col_parts, send))
            got = swap(send)
        row_parts = call(
            row_kernel,
            "sum_over_rows",
            shape((parts, 1, protos), f32),
            flops=2 * teach_rows * protos,
            nbytes=2 * teach_rows * protos,
        )(col_parts, exps)
        if iteration == 0:
            row_parts, got = lax.optimization_barrier((row_parts, got))
        row_parts = exchange(row_parts, "dp")

    back = call(
        repel_kernel,
        "repel",
        shape((chips, 2, 64, LANES), bf16),
        in_specs=[scalar] + [vmem] * 6,
        flops=2 * groups * glob * protos * width,
        nbytes=2 * protos * width,
    )(core, row_parts, exps, unit_protos, keep, got, total)
    back = exchange(back.reshape(groups, 64, LANES), "proto").reshape(chips, 2, 64, LANES)

    grad, loss = call(
        final_kernel,
        "gradients",
        [shape((crops, images, width), f32), shape((images, crops), f32)],
        scratch_shapes=[pltpu.VMEM((stud, width), f32)],
    )(back, student)
    return jnp.transpose(grad, (1, 0, 2)), loss


def solution(mesh):
    in_specs = (
        P(("dp", "proto"), None, None),
        P(("dp", "proto"), None),
        P(("dp", "proto"), None, None),
        P("proto", None),
    )
    out_specs = (P(("dp", "proto"), None, None), P(("dp", "proto"), None))
    return jax.shard_map(body, mesh=mesh, in_specs=in_specs, out_specs=out_specs, check_vma=False)
```

```python
import functools
import math

import jax
import jax.numpy as jnp
from jax import lax
from jax.experimental import pallas as pl
from jax.experimental.pallas import tpu as pltpu
from jax.sharding import PartitionSpec as P

SINK_ITERS = 3
TEACHER_SOFTNESS = 0.07
STUDENT_SOFTNESS = 0.1
NORM_EPSILON = 1e-06
TEACHER_EXP2 = math.log2(math.e) / TEACHER_SOFTNESS
STUDENT_EXP2 = math.log2(math.e) / STUDENT_SOFTNESS

LANES = 128
MIB = 1024 * 1024

f32 = jnp.float32
bf16 = jnp.bfloat16
shape = jax.ShapeDtypeStruct


def iota(shape, dim):
    return lax.broadcasted_iota(jnp.int32, shape, dim)


def unit(values):
    return values * lax.rsqrt(jnp.sum(values * values, axis=-1, keepdims=True) + NORM_EPSILON)


def nt_dot(a, b):
    return lax.dot_general(a, b, (((1,), (1,)), ((), ())), preferred_element_type=f32)


def call(kernel, name, out_shape, flops=0, nbytes=0, exps=0, vmem=32, **kw):
    return pl.pallas_call(
        kernel,
        out_shape=out_shape,
        compiler_params=pltpu.CompilerParams(vmem_limit_bytes=vmem * MIB),
        cost_estimate=pl.CostEstimate(flops=flops, bytes_accessed=nbytes, transcendentals=exps),
        name=name,
        **kw,
    )


def in_vmem(array):
    return pltpu.with_memory_space_constraint(array, pltpu.VMEM)


def in_hbm(array):
    return pltpu.with_memory_space_constraint(array, pltpu.HBM)


def pack_kernel(student_ref, teacher_ref, queue_ref, out_ref, rows_ref):
    crops, images, _ = student_ref.shape
    queue_rows = queue_ref.shape[0]
    stud = crops * images
    for c in range(crops):
        rows_ref[c * images : (c + 1) * images, :] = unit(student_ref[c].astype(f32))
    for i in range(images):
        views = unit(teacher_ref[i].astype(f32))
        rows_ref[stud + i : stud + i + 1, :] = views[1:2]
        rows_ref[stud + images + i : stud + images + i + 1, :] = views[0:1]
    units = unit(queue_ref[...].astype(f32))
    at = stud + 2 * images
    rows_ref[at : at + queue_rows, :] = units
    rows_ref[at + queue_rows :, :] = units[8:]
    packed = rows_ref[...].astype(bf16)
    for j in range(out_ref.shape[0]):
        out_ref[j] = packed


def unit_kernel(protos_ref, out_ref):
    out_ref[...] = unit(protos_ref[...].astype(f32)).astype(bf16)


def by_core(core_ref, own, other):
    is_first = core_ref[0] == 0
    return jnp.where(is_first, own, other), jnp.where(is_first, other, own)


def teacher_kernel(stud, glob, core_ref, own_ref, other_ref, unit_ref, exp_ref, sums_ref):
    chips, _, width = own_ref.shape
    blocks = by_core(core_ref, own_ref[...].astype(f32)[:, stud:], other_ref[...].astype(f32)[:, stud:])
    block = jnp.concatenate(blocks, axis=0)
    groups = 2 * chips
    g = block[:, :glob].reshape(groups * glob, width)
    q = block[:, glob : glob + 8].reshape(groups * 8, width)
    r = block[:, glob + 8 :].reshape(chips, 2, 8, width)
    low = iota((chips, 8, width), 1) < 4
    r = jnp.where(low, r[:, 0], r[:, 1]).reshape(groups * 4, width)
    teach = jnp.concatenate([g, q, r], axis=0).astype(bf16)
    step = 256
    for start in range(0, unit_ref.shape[0], step):
        here = slice(start, start + step)
        exps = jnp.exp2(nt_dot(teach, unit_ref[here, :]) * TEACHER_EXP2)
        exp_ref[:, here] = exps.astype(bf16)
        sums_ref[0, :, here] = jnp.sum(exps, axis=0, keepdims=True)


def student_kernel(
    stud, core_ref, own_ref, other_ref, unit_ref, keep_ref, send_ref, total_ref, stud_ref, acc_ref, tot_ref
):
    chips, _, width = own_ref.shape
    rows = chips * stud
    for h, rows_ref in enumerate((own_ref, other_ref)):
        block = rows_ref[...].astype(f32)[:, :stud]
        stud_ref[h * rows : (h + 1) * rows, :] = block.reshape(rows, width).astype(bf16)
    step = 512
    chunk = rows
    for start in range(0, unit_ref.shape[0], step):
        protos = unit_ref[start : start + step, :]
        for c in range(2 * rows // chunk):
            here = slice(c * chunk, (c + 1) * chunk)
            weights = jnp.exp2(nt_dot(stud_ref[here, :], protos) * STUDENT_EXP2)
            part = weights[:, :LANES]
            for k in range(1, step // LANES):
                part = part + weights[:, k * LANES : (k + 1) * LANES]
            term = jnp.dot(weights.astype(bf16), protos, preferred_element_type=f32)
            if start == 0:
                tot_ref[here, :] = part
                acc_ref[here, :] = term
            else:
                tot_ref[here, :] += part
                acc_ref[here, :] += term
    is_first = core_ref[0] == 0
    for h in range(2):
        here = slice(h * rows, (h + 1) * rows)
        attract = acc_ref[here, :].reshape(chips, stud, width)
        low, high = attract[:, :, :LANES], attract[:, :, LANES:]
        keep_ref[h] = jnp.where(is_first, low, high)
        send_ref[h] = jnp.where(is_first, high, low).astype(bf16)
        total = jnp.sum(tot_ref[here, :], axis=1, keepdims=True).reshape(chips, stud, 1)
        eye = iota((chips, stud, LANES), 1) == iota((chips, stud, LANES), 2)
        total_ref[h] = jnp.sum(
            jnp.where(eye, jnp.broadcast_to(total, (chips, stud, LANES)), 0.0),
            axis=1,
            keepdims=True,
        )


def pair_kernel(mine_ref, got_ref, out_ref):
    total = mine_ref[0] + got_ref[0]
    for j in range(out_ref.shape[0]):
        out_ref[j] = total


def proto_scale_of(parts_ref):
    total = parts_ref[0]
    for j in range(1, parts_ref.shape[0]):
        total = total + parts_ref[j]
    return 1.0 / total


def col_kernel(parts_ref, exp_ref, out_ref):
    scale = proto_scale_of(parts_ref)
    rows, cols = exp_ref.shape
    lines = []
    for g in range(rows // LANES):
        acc = None
        for k in range(cols // LANES):
            lanes = slice(k * LANES, (k + 1) * LANES)
            term = exp_ref[g * LANES : (g + 1) * LANES, lanes].astype(f32) * scale[:, lanes]
            acc = term if acc is None else acc + term
        lines.append(jnp.sum(acc.T, axis=0, keepdims=True))
    out = jnp.concatenate(lines, axis=1)
    for j in range(out_ref.shape[0]):
        out_ref[j] = out


def row_kernel(parts_ref, exp_ref, out_ref):
    rows, cols = exp_ref.shape
    scale = 1.0 / jnp.sum(parts_ref[...], axis=0)
    acc = None
    for g in range(rows // LANES):
        tall = jnp.broadcast_to(scale[:, g * LANES : (g + 1) * LANES], (LANES, LANES)).T
        for t in range(0, LANES, 16):
            wide = jnp.concatenate([tall[t : t + 16]] * (cols // LANES), axis=1)
            term = exp_ref[g * LANES + t : g * LANES + t + 16, :].astype(f32) * wide
            term = term[:8] + term[8:]
            acc = term if acc is None else acc + term
    line = jnp.sum(acc, axis=0, keepdims=True)
    for j in range(out_ref.shape[0]):
        out_ref[j] = line


def repel_kernel(
    core_ref, parts_ref, exp_ref, unit_ref, keep_ref, got_ref, total_ref, out_ref
):
    _, chips, stud, _ = keep_ref.shape
    glob = 8
    rows = 2 * chips * glob
    scale = proto_scale_of(parts_ref)
    cols, width = unit_ref.shape
    acc = jnp.zeros((rows, LANES), f32)
    repel = jnp.zeros((rows, width), f32)
    step = 512
    for start in range(0, cols, step):
        here = slice(start, start + step)
        terms = exp_ref[:rows, here].astype(f32) * scale[:, here]
        for k in range(step // LANES):
            acc = acc + terms[:, k * LANES : (k + 1) * LANES]
        repel = repel + jnp.dot(terms.astype(bf16), unit_ref[here, :], preferred_element_type=f32)
    sums = jnp.sum(acc, axis=1, keepdims=True).reshape(2, chips, glob, 1)
    repel = repel.reshape(2, chips, glob, width)
    attract = by_core(
        core_ref, keep_ref[0] + got_ref[1].astype(f32), keep_ref[1] + got_ref[0].astype(f32)
    )
    totals = by_core(core_ref, total_ref[0], total_ref[1])
    dims = (chips, glob, LANES)
    place = iota(dims, 1) + stud == iota(dims, 2)
    for core in range(2):
        mass = jnp.where(place, jnp.broadcast_to(sums[core], dims), 0.0)
        scalars = totals[core] + jnp.sum(mass, axis=1, keepdims=True)
        high = scalars.astype(bf16).astype(f32)
        scalars = jnp.where(iota(dims, 1) == 0, high, scalars - high)
        parts = [attract[core], repel[core][:, :, :LANES], repel[core][:, :, LANES:], scalars]
        out_ref[:, core] = jnp.concatenate(parts, axis=1).astype(bf16)


def final_kernel(back_ref, student_ref, grad_ref, loss_ref, rows_ref):
    crops, images, width = student_ref.shape
    stud = crops * images
    for c in range(crops):
        rows_ref[c * images : (c + 1) * images, :] = student_ref[c].astype(f32)
    values = rows_ref[...]
    back = jnp.sum(back_ref[...].astype(f32), axis=0)
    attract = jnp.concatenate([back[0, :stud], back[1, :stud]], axis=1)
    back = back[0, stud:] + back[1, stud:]
    line = back[16:17] + back[17:18]
    sub, lane = iota((stud, LANES), 0), iota((stud, LANES), 1)
    lines = jnp.broadcast_to(line, (stud, LANES))
    total = jnp.sum(jnp.where(lane == sub, lines, 0.0), axis=1, keepdims=True)
    mass = jnp.sum(jnp.where(lane == sub + stud, lines, 0.0)[:8], axis=1, keepdims=True)
    views = jnp.concatenate([back[:8], back[8:16]], axis=1) / mass
    both = views + jnp.concatenate([views[images:], views[:images]], axis=0)
    repel = jnp.concatenate([views] + [both] * (stud // 8 - 1), axis=0)
    pairs = jnp.where(iota((stud, 1), 0) < 2 * images, 1.0, 2.0)
    inv_norm = lax.rsqrt(jnp.sum(values * values, axis=1, keepdims=True) + NORM_EPSILON)
    own = values * inv_norm
    low = own.astype(bf16).astype(f32)
    grad_unit = (pairs * attract / total - repel) / STUDENT_SOFTNESS
    cross = jnp.sum(low * repel, axis=1, keepdims=True) / STUDENT_SOFTNESS
    loss = pairs * jnp.log(total) - cross
    inner = jnp.sum(own * grad_unit, axis=1, keepdims=True)
    grad = inv_norm * (grad_unit - own * inner)
    for c in range(crops):
        grad_ref[c] = grad[c * images : (c + 1) * images]
    wide = jnp.broadcast_to(loss, (stud, LANES))
    for i in range(images):
        spread = jnp.where(sub == lane * images + i, wide, 0.0)
        loss_ref[i : i + 1, :] = jnp.sum(spread, axis=0, keepdims=True)[:, :crops]


def exchange(array, axis, **kw):
    return lax.all_to_all(array, axis, 0, 0, tiled=True, **kw)


def body(teacher_global, queue, student, prototypes):
    images, crops, width = student.shape
    queue_rows = queue.shape[0]
    groups, parts = lax.axis_size("proto"), lax.axis_size("dp")
    chips = groups // 2
    stud, glob = images * crops, images * 2
    teach_rows = groups * (glob + queue_rows)
    protos = prototypes.shape[0]
    student = jnp.transpose(student, (1, 0, 2))
    core = jnp.reshape(lax.axis_index("proto") % 2, (1,))
    scalar = pl.BlockSpec(memory_space=pltpu.SMEM)
    vmem = pl.BlockSpec(memory_space=pltpu.VMEM)

    def swap(array):
        return lax.ppermute(array, "proto", [(j, j ^ 1) for j in range(groups)])

    send_rows = stud + glob + queue_rows + 4
    packed = call(
        pack_kernel,
        "pack_rows",
        shape((chips, send_rows, width), bf16),
        scratch_shapes=[pltpu.VMEM((send_rows, width), f32)],
    )(*map(in_hbm, (student, teacher_global, queue)))
    same_core = [list(range(c, groups, 2)) for c in range(2)]
    own_rows = exchange(packed, "proto", axis_index_groups=same_core)
    other_rows = swap(own_rows)
    unit_protos = call(
        unit_kernel,
        "unit_prototypes",
        shape((protos, width), bf16),
        grid=(4,),
        in_specs=[pl.BlockSpec((protos // 4, width), lambda i: (i, 0))],
        out_specs=pl.BlockSpec((protos // 4, width), lambda i: (i, 0)),
        flops=3 * protos * width,
        nbytes=4 * protos * width,
    )(in_hbm(prototypes))

    exps, row_parts = call(
        functools.partial(teacher_kernel, stud, glob),
        "teacher_exponentials",
        [pltpu.VMEM((teach_rows, protos), bf16), shape((1, 1, protos), f32)],
        in_specs=[scalar, vmem, vmem, vmem],
        flops=2 * teach_rows * protos * width,
        nbytes=2 * teach_rows * protos,
        exps=teach_rows * protos,
    )(core, own_rows, other_rows, unit_protos)
    exps = in_vmem(exps)

    half = parts // 2
    got_sums = lax.ppermute(row_parts, "dp", [(j, (j + half) % parts) for j in range(parts)])
    all_rows = 2 * chips * stud
    keep, send, total = call(
        functools.partial(student_kernel, stud),
        "student_attract",
        [
            shape((2, chips, stud, LANES), f32),
            shape((2, chips, stud, LANES), bf16),
            shape((2, chips, 1, LANES), f32),
        ],
        in_specs=[scalar, vmem, vmem, vmem],
        scratch_shapes=[
            pltpu.VMEM((all_rows, width), bf16),
            pltpu.VMEM((all_rows, width), f32),
            pltpu.VMEM((all_rows, LANES), f32),
        ],
        flops=4 * all_rows * protos * width,
        nbytes=2 * protos * width,
        exps=all_rows * protos,
    )(core, own_rows, other_rows, unit_protos)
    got_sums, keep, send, total = lax.optimization_barrier((got_sums, keep, send, total))
    row_parts = call(pair_kernel, "add_halves", shape((half, 1, protos), f32))(row_parts, got_sums)
    halves = [list(range(half)), list(range(half, parts))]
    row_parts = exchange(row_parts, "dp", axis_index_groups=halves)

    for iteration in range(SINK_ITERS - 1):
        col_parts = call(
            col_kernel,
            "sum_over_prototypes",
            shape((groups, 1, teach_rows), f32),
            flops=2 * teach_rows * protos,
            nbytes=2 * teach_rows * protos,
        )(row_parts, exps)
        col_parts = exchange(col_parts, "proto")
        if iteration == 0:
            col_parts, send = lax.optimization_barrier((col_parts, send))
            got = swap(send)
        row_parts = call(
            row_kernel,
            "sum_over_rows",
            shape((parts, 1, protos), f32),
            flops=2 * teach_rows * protos,
            nbytes=2 * teach_rows * protos,
        )(col_parts, exps)
        if iteration == 0:
            row_parts, got = lax.optimization_barrier((row_parts, got))
        row_parts = exchange(row_parts, "dp")

    back = call(
        repel_kernel,
        "repel",
        shape((chips, 2, 64, LANES), bf16),
        in_specs=[scalar] + [vmem] * 6,
        flops=2 * groups * glob * protos * width,
        nbytes=2 * protos * width,
    )(core, row_parts, exps, unit_protos, keep, got, total)
    back = exchange(back.reshape(groups, 64, LANES), "proto").reshape(chips, 2, 64, LANES)

    grad, loss = call(
        final_kernel,
        "gradients",
        [shape((crops, images, width), f32), shape((images, crops), f32)],
        scratch_shapes=[pltpu.VMEM((stud, width), f32)],
    )(back, student)
    return jnp.transpose(grad, (1, 0, 2)), loss


def solution(mesh):
    in_specs = (
        P(("dp", "proto"), None, None),
        P(("dp", "proto"), None),
        P(("dp", "proto"), None, None),
        P("proto", None),
    )
    out_specs = (P(("dp", "proto"), None, None), P(("dp", "proto"), None))
    return jax.shard_map(body, mesh=mesh, in_specs=in_specs, out_specs=out_specs, check_vma=False)
```

```python
import functools
import math

import jax
import jax.numpy as jnp
from jax import lax
from jax.experimental import pallas as pl
from jax.experimental.pallas import tpu as pltpu
from jax.sharding import PartitionSpec as P

SINK_ITERS = 3
TEACHER_SOFTNESS = 0.07
STUDENT_SOFTNESS = 0.1
NORM_EPSILON = 1e-06
TEACHER_EXP2 = math.log2(math.e) / TEACHER_SOFTNESS
STUDENT_EXP2 = math.log2(math.e) / STUDENT_SOFTNESS

LANES = 128
MIB = 1024 * 1024

f32 = jnp.float32
bf16 = jnp.bfloat16
shape = jax.ShapeDtypeStruct


def iota(shape, dim):
    return lax.broadcasted_iota(jnp.int32, shape, dim)


def unit(values):
    return values * lax.rsqrt(jnp.sum(values * values, axis=-1, keepdims=True) + NORM_EPSILON)


def nt_dot(a, b):
    return lax.dot_general(a, b, (((1,), (1,)), ((), ())), preferred_element_type=f32)


def call(kernel, name, out_shape, flops=0, nbytes=0, exps=0, vmem=32, **kw):
    return pl.pallas_call(
        kernel,
        out_shape=out_shape,
        compiler_params=pltpu.CompilerParams(vmem_limit_bytes=vmem * MIB),
        cost_estimate=pl.CostEstimate(flops=flops, bytes_accessed=nbytes, transcendentals=exps),
        name=name,
        **kw,
    )


def in_vmem(array):
    return pltpu.with_memory_space_constraint(array, pltpu.VMEM)


def in_hbm(array):
    return pltpu.with_memory_space_constraint(array, pltpu.HBM)


def pack_kernel(student_ref, teacher_ref, queue_ref, out_ref, rows_ref):
    crops, images, _ = student_ref.shape
    queue_rows = queue_ref.shape[0]
    stud = crops * images
    for c in range(crops):
        rows_ref[c * images : (c + 1) * images, :] = unit(student_ref[c].astype(f32))
    for i in range(images):
        views = unit(teacher_ref[i].astype(f32))
        rows_ref[stud + i : stud + i + 1, :] = views[1:2]
        rows_ref[stud + images + i : stud + images + i + 1, :] = views[0:1]
    units = unit(queue_ref[...].astype(f32))
    at = stud + 2 * images
    rows_ref[at : at + queue_rows, :] = units
    rows_ref[at + queue_rows :, :] = units[8:]
    packed = rows_ref[...].astype(bf16)
    for j in range(out_ref.shape[0]):
        out_ref[j] = packed


def unit_kernel(protos_ref, out_ref):
    out_ref[...] = unit(protos_ref[...].astype(f32)).astype(bf16)


def by_core(core_ref, own, other):
    is_first = core_ref[0] == 0
    return jnp.where(is_first, own, other), jnp.where(is_first, other, own)


def teacher_kernel(stud, glob, core_ref, own_ref, other_ref, unit_ref, exp_ref, sums_ref):
    chips, _, width = own_ref.shape
    blocks = by_core(core_ref, own_ref[...].astype(f32)[:, stud:], other_ref[...].astype(f32)[:, stud:])
    block = jnp.concatenate(blocks, axis=0)
    groups = 2 * chips
    g = block[:, :glob].reshape(groups * glob, width)
    q = block[:, glob : glob + 8].reshape(groups * 8, width)
    r = block[:, glob + 8 :].reshape(chips, 2, 8, width)
    low = iota((chips, 8, width), 1) < 4
    r = jnp.where(low, r[:, 0], r[:, 1]).reshape(groups * 4, width)
    teach = jnp.concatenate([g, q, r], axis=0).astype(bf16)
    step = 256
    for start in range(0, unit_ref.shape[0], step):
        here = slice(start, start + step)
        exps = jnp.exp2(nt_dot(teach, unit_ref[here, :]) * TEACHER_EXP2)
        exp_ref[:, here] = exps.astype(bf16)
        sums_ref[0, :, here] = jnp.sum(exps, axis=0, keepdims=True)


def student_kernel(
    stud, core_ref, own_ref, other_ref, unit_ref, keep_ref, send_ref, total_ref, stud_ref, acc_ref, tot_ref
):
    chips, _, width = own_ref.shape
    rows = chips * stud
    for h, rows_ref in enumerate((own_ref, other_ref)):
        block = rows_ref[...].astype(f32)[:, :stud]
        stud_ref[h * rows : (h + 1) * rows, :] = block.reshape(rows, width).astype(bf16)
    step = 512
    chunk = rows
    for start in range(0, unit_ref.shape[0], step):
        protos = unit_ref[start : start + step, :]
        for c in range(2 * rows // chunk):
            here = slice(c * chunk, (c + 1) * chunk)
            weights = jnp.exp2(nt_dot(stud_ref[here, :], protos) * STUDENT_EXP2)
            part = weights[:, :LANES]
            for k in range(1, step // LANES):
                part = part + weights[:, k * LANES : (k + 1) * LANES]
            term = jnp.dot(weights.astype(bf16), protos, preferred_element_type=f32)
            if start == 0:
                tot_ref[here, :] = part
                acc_ref[here, :] = term
            else:
                tot_ref[here, :] += part
                acc_ref[here, :] += term
    is_first = core_ref[0] == 0
    for h in range(2):
        here = slice(h * rows, (h + 1) * rows)
        attract = acc_ref[here, :].reshape(chips, stud, width)
        low, high = attract[:, :, :LANES], attract[:, :, LANES:]
        keep_ref[h] = jnp.where(is_first, low, high)
        send_ref[h] = jnp.where(is_first, high, low).astype(bf16)
        total = jnp.sum(tot_ref[here, :], axis=1, keepdims=True).reshape(chips, stud, 1)
        eye = iota((chips, stud, LANES), 1) == iota((chips, stud, LANES), 2)
        total_ref[h] = jnp.sum(
            jnp.where(eye, jnp.broadcast_to(total, (chips, stud, LANES)), 0.0),
            axis=1,
            keepdims=True,
        )


def pair_kernel(mine_ref, got_ref, out_ref):
    total = mine_ref[0] + got_ref[0]
    for j in range(out_ref.shape[0]):
        out_ref[j] = total


def proto_scale_of(parts_ref):
    total = parts_ref[0]
    for j in range(1, parts_ref.shape[0]):
        total = total + parts_ref[j]
    return 1.0 / total


def col_kernel(parts_ref, exp_ref, out_ref):
    scale = proto_scale_of(parts_ref)
    rows, cols = exp_ref.shape
    lines = []
    for g in range(rows // LANES):
        acc = None
        for k in range(cols // LANES):
            lanes = slice(k * LANES, (k + 1) * LANES)
            term = exp_ref[g * LANES : (g + 1) * LANES, lanes].astype(f32) * scale[:, lanes]
            acc = term if acc is None else acc + term
        lines.append(jnp.sum(acc.T, axis=0, keepdims=True))
    out = jnp.concatenate(lines, axis=1)
    for j in range(out_ref.shape[0]):
        out_ref[j] = out


def row_kernel(parts_ref, exp_ref, out_ref):
    rows, cols = exp_ref.shape
    scale = 1.0 / jnp.sum(parts_ref[...], axis=0)
    acc = None
    for g in range(rows // LANES):
        tall = jnp.broadcast_to(scale[:, g * LANES : (g + 1) * LANES], (LANES, LANES)).T
        for t in range(0, LANES, 16):
            wide = jnp.concatenate([tall[t : t + 16]] * (cols // LANES), axis=1)
            term = exp_ref[g * LANES + t : g * LANES + t + 16, :].astype(f32) * wide
            term = term[:8] + term[8:]
            acc = term if acc is None else acc + term
    line = jnp.sum(acc, axis=0, keepdims=True)
    for j in range(out_ref.shape[0]):
        out_ref[j] = line


def repel_kernel(
    core_ref, parts_ref, exp_ref, unit_ref, keep_ref, got_ref, total_ref, out_ref
):
    _, chips, stud, _ = keep_ref.shape
    glob = 8
    rows = 2 * chips * glob
    scale = proto_scale_of(parts_ref)
    cols, width = unit_ref.shape
    acc = jnp.zeros((rows, LANES), f32)
    repel = jnp.zeros((rows, width), f32)
    step = 512
    for start in range(0, cols, step):
        here = slice(start, start + step)
        terms = exp_ref[:rows, here].astype(f32) * scale[:, here]
        for k in range(step // LANES):
            acc = acc + terms[:, k * LANES : (k + 1) * LANES]
        repel = repel + jnp.dot(terms.astype(bf16), unit_ref[here, :], preferred_element_type=f32)
    sums = jnp.sum(acc, axis=1, keepdims=True).reshape(2, chips, glob, 1)
    repel = repel.reshape(2, chips, glob, width)
    attract = by_core(
        core_ref, keep_ref[0] + got_ref[1].astype(f32), keep_ref[1] + got_ref[0].astype(f32)
    )
    totals = by_core(core_ref, total_ref[0], total_ref[1])
    dims = (chips, glob, LANES)
    place = iota(dims, 1) + stud == iota(dims, 2)
    for core in range(2):
        mass = jnp.where(place, jnp.broadcast_to(sums[core], dims), 0.0)
        scalars = totals[core] + jnp.sum(mass, axis=1, keepdims=True)
        high = scalars.astype(bf16).astype(f32)
        scalars = jnp.where(iota(dims, 1) == 0, high, scalars - high)
        parts = [attract[core], repel[core][:, :, :LANES], repel[core][:, :, LANES:], scalars]
        out_ref[:, core] = jnp.concatenate(parts, axis=1).astype(bf16)


def final_kernel(back_ref, student_ref, grad_ref, loss_ref, rows_ref):
    crops, images, width = student_ref.shape
    stud = crops * images
    for c in range(crops):
        rows_ref[c * images : (c + 1) * images, :] = student_ref[c].astype(f32)
    values = rows_ref[...]
    back = jnp.sum(back_ref[...].astype(f32), axis=0)
    attract = jnp.concatenate([back[0, :stud], back[1, :stud]], axis=1)
    back = back[0, stud:] + back[1, stud:]
    line = back[16:17] + back[17:18]
    sub, lane = iota((stud, LANES), 0), iota((stud, LANES), 1)
    lines = jnp.broadcast_to(line, (stud, LANES))
    total = jnp.sum(jnp.where(lane == sub, lines, 0.0), axis=1, keepdims=True)
    mass = jnp.sum(jnp.where(lane == sub + stud, lines, 0.0)[:8], axis=1, keepdims=True)
    views = jnp.concatenate([back[:8], back[8:16]], axis=1) / mass
    both = views + jnp.concatenate([views[images:], views[:images]], axis=0)
    repel = jnp.concatenate([views] + [both] * (stud // 8 - 1), axis=0)
    pairs = jnp.where(iota((stud, 1), 0) < 2 * images, 1.0, 2.0)
    inv_norm = lax.rsqrt(jnp.sum(values * values, axis=1, keepdims=True) + NORM_EPSILON)
    own = values * inv_norm
    low = own.astype(bf16).astype(f32)
    grad_unit = (pairs * attract / total - repel) / STUDENT_SOFTNESS
    cross = jnp.sum(low * repel, axis=1, keepdims=True) / STUDENT_SOFTNESS
    loss = pairs * jnp.log(total) - cross
    inner = jnp.sum(own * grad_unit, axis=1, keepdims=True)
    grad = inv_norm * (grad_unit - own * inner)
    for c in range(crops):
        grad_ref[c] = grad[c * images : (c + 1) * images]
    wide = jnp.broadcast_to(loss, (stud, LANES))
    for i in range(images):
        spread = jnp.where(sub == lane * images + i, wide, 0.0)
        loss_ref[i : i + 1, :] = jnp.sum(spread, axis=0, keepdims=True)[:, :crops]


def exchange(array, axis, **kw):
    return lax.all_to_all(array, axis, 0, 0, tiled=True, **kw)


def body(teacher_global, queue, student, prototypes):
    images, crops, width = student.shape
    queue_rows = queue.shape[0]
    groups, parts = lax.axis_size("proto"), lax.axis_size("dp")
    chips = groups // 2
    stud, glob = images * crops, images * 2
    teach_rows = groups * (glob + queue_rows)
    protos = prototypes.shape[0]
    student = jnp.transpose(student, (1, 0, 2))
    core = jnp.reshape(lax.axis_index("proto") % 2, (1,))
    scalar = pl.BlockSpec(memory_space=pltpu.SMEM)
    vmem = pl.BlockSpec(memory_space=pltpu.VMEM)

    def swap(array):
        return lax.ppermute(array, "proto", [(j, j ^ 1) for j in range(groups)])

    send_rows = stud + glob + queue_rows + 4
    packed = call(
        pack_kernel,
        "pack_rows",
        shape((chips, send_rows, width), bf16),
        scratch_shapes=[pltpu.VMEM((send_rows, width), f32)],
    )(*map(in_hbm, (student, teacher_global, queue)))
    same_core = [list(range(c, groups, 2)) for c in range(2)]
    own_rows = exchange(packed, "proto", axis_index_groups=same_core)
    unit_protos = call(
        unit_kernel,
        "unit_prototypes",
        shape((protos, width), bf16),
        grid=(4,),
        in_specs=[pl.BlockSpec((protos // 4, width), lambda i: (i, 0))],
        out_specs=pl.BlockSpec((protos // 4, width), lambda i: (i, 0)),
        flops=3 * protos * width,
        nbytes=4 * protos * width,
    )(prototypes)

    own_rows, unit_protos = lax.optimization_barrier((own_rows, unit_protos))
    other_rows = swap(own_rows)

    exps, row_parts = call(
        functools.partial(teacher_kernel, stud, glob),
        "teacher_exponentials",
        [pltpu.VMEM((teach_rows, protos), bf16), shape((1, 1, protos), f32)],
        in_specs=[scalar, vmem, vmem, vmem],
        flops=2 * teach_rows * protos * width,
        nbytes=2 * teach_rows * protos,
        exps=teach_rows * protos,
    )(core, own_rows, other_rows, unit_protos)
    exps = in_vmem(exps)

    half = parts // 2
    got_sums = lax.ppermute(row_parts, "dp", [(j, (j + half) % parts) for j in range(parts)])
    all_rows = 2 * chips * stud
    keep, send, total = call(
        functools.partial(student_kernel, stud),
        "student_attract",
        [
            shape((2, chips, stud, LANES), f32),
            shape((2, chips, stud, LANES), bf16),
            shape((2, chips, 1, LANES), f32),
        ],
        in_specs=[scalar, vmem, vmem, vmem],
        scratch_shapes=[
            pltpu.VMEM((all_rows, width), bf16),
            pltpu.VMEM((all_rows, width), f32),
            pltpu.VMEM((all_rows, LANES), f32),
        ],
        flops=4 * all_rows * protos * width,
        nbytes=2 * protos * width,
        exps=all_rows * protos,
    )(core, own_rows, other_rows, unit_protos)
    got_sums, keep, send, total = lax.optimization_barrier((got_sums, keep, send, total))
    row_parts = call(pair_kernel, "add_halves", shape((half, 1, protos), f32))(row_parts, got_sums)
    halves = [list(range(half)), list(range(half, parts))]
    row_parts = exchange(row_parts, "dp", axis_index_groups=halves)

    for iteration in range(SINK_ITERS - 1):
        col_parts = call(
            col_kernel,
            "sum_over_prototypes",
            shape((groups, 1, teach_rows), f32),
            flops=2 * teach_rows * protos,
            nbytes=2 * teach_rows * protos,
        )(row_parts, exps)
        col_parts = exchange(col_parts, "proto")
        if iteration == 0:
            col_parts, send = lax.optimization_barrier((col_parts, send))
            got = swap(send)
        row_parts = call(
            row_kernel,
            "sum_over_rows",
            shape((parts, 1, protos), f32),
            flops=2 * teach_rows * protos,
            nbytes=2 * teach_rows * protos,
        )(col_parts, exps)
        if iteration == 0:
            row_parts, got = lax.optimization_barrier((row_parts, got))
        row_parts = exchange(row_parts, "dp")

    back = call(
        repel_kernel,
        "repel",
        shape((chips, 2, 64, LANES), bf16),
        in_specs=[scalar] + [vmem] * 6,
        flops=2 * groups * glob * protos * width,
        nbytes=2 * protos * width,
    )(core, row_parts, exps, unit_protos, keep, got, total)
    back = exchange(back.reshape(groups, 64, LANES), "proto").reshape(chips, 2, 64, LANES)

    grad, loss = call(
        final_kernel,
        "gradients",
        [shape((crops, images, width), f32), shape((images, crops), f32)],
        scratch_shapes=[pltpu.VMEM((stud, width), f32)],
    )(back, student)
    return jnp.transpose(grad, (1, 0, 2)), loss


def solution(mesh):
    in_specs = (
        P(("dp", "proto"), None, None),
        P(("dp", "proto"), None),
        P(("dp", "proto"), None, None),
        P("proto", None),
    )
    out_specs = (P(("dp", "proto"), None, None), P(("dp", "proto"), None))
    return jax.shard_map(body, mesh=mesh, in_specs=in_specs, out_specs=out_specs, check_vma=False)
```

```python
import functools
import math

import jax
import jax.numpy as jnp
from jax import lax
from jax.experimental import pallas as pl
from jax.experimental.pallas import tpu as pltpu
from jax.sharding import PartitionSpec as P

SINK_ITERS = 3
TEACHER_SOFTNESS = 0.07
STUDENT_SOFTNESS = 0.1
NORM_EPSILON = 1e-06
TEACHER_EXP2 = math.log2(math.e) / TEACHER_SOFTNESS
STUDENT_EXP2 = math.log2(math.e) / STUDENT_SOFTNESS

LANES = 128
MIB = 1024 * 1024

f32 = jnp.float32
bf16 = jnp.bfloat16
shape = jax.ShapeDtypeStruct


def iota(shape, dim):
    return lax.broadcasted_iota(jnp.int32, shape, dim)


def unit(values):
    return values * lax.rsqrt(jnp.sum(values * values, axis=-1, keepdims=True) + NORM_EPSILON)


def nt_dot(a, b):
    return lax.dot_general(a, b, (((1,), (1,)), ((), ())), preferred_element_type=f32)


def call(kernel, name, out_shape, flops=0, nbytes=0, exps=0, vmem=32, **kw):
    return pl.pallas_call(
        kernel,
        out_shape=out_shape,
        compiler_params=pltpu.CompilerParams(vmem_limit_bytes=vmem * MIB),
        cost_estimate=pl.CostEstimate(flops=flops, bytes_accessed=nbytes, transcendentals=exps),
        name=name,
        **kw,
    )


def in_vmem(array):
    return pltpu.with_memory_space_constraint(array, pltpu.VMEM)


def in_hbm(array):
    return pltpu.with_memory_space_constraint(array, pltpu.HBM)


def pack_kernel(student_ref, teacher_ref, queue_ref, out_ref, rows_ref):
    crops, images, width = student_ref.shape
    stud, glob = crops * images, 2 * images
    half = width // 2

    def put(at, rows, height, values):
        rows_ref[at + rows : at + rows + values.shape[0], :] = values[:, :half]
        rows_ref[at + height + rows : at + height + rows + values.shape[0], :] = values[:, half:]

    for c in range(crops):
        put(0, c * images, stud, unit(student_ref[c].astype(f32)))
    at = 2 * stud
    for i in range(images):
        views = unit(teacher_ref[i].astype(f32))
        put(at, i, glob, views[1:2])
        put(at, images + i, glob, views[0:1])
    units = unit(queue_ref[...].astype(f32))
    at = at + 2 * glob
    put(at, 0, 8, units[:8])
    put(at + 16, 0, 4, units[8:])
    packed = rows_ref[...].astype(bf16)
    for j in range(out_ref.shape[0]):
        out_ref[j] = packed


def wide(low, high):
    return jnp.concatenate([low, high], axis=-1)


def unit_kernel(protos_ref, out_ref, raw_ref, sems):
    parts = sems.shape[0]
    rows = raw_ref.shape[0] // parts
    copies = []
    for j in range(parts):
        here = pl.ds(j * rows, rows)
        copies.append(pltpu.make_async_copy(protos_ref.at[here], raw_ref.at[here], sems.at[j]))
        copies[j].start()
    for j in range(parts):
        copies[j].wait()
        here = slice(j * rows, (j + 1) * rows)
        out_ref[here, :] = unit(raw_ref[here, :].astype(f32)).astype(bf16)


def by_core(core_ref, own, other):
    is_first = core_ref[0] == 0
    return jnp.where(is_first, own, other), jnp.where(is_first, other, own)


def teacher_kernel(stud, glob, core_ref, own_ref, other_ref, unit_ref, exp_ref, sums_ref):
    chips, _, half = own_ref.shape
    width = 2 * half
    at = 2 * stud
    blocks = by_core(core_ref, own_ref[...].astype(f32)[:, at:], other_ref[...].astype(f32)[:, at:])
    block = jnp.concatenate(blocks, axis=0)
    groups = 2 * chips
    at = 2 * glob
    g = wide(block[:, :glob], block[:, glob:at]).reshape(groups * glob, width)
    q = wide(block[:, at : at + 8], block[:, at + 8 : at + 16]).reshape(groups * 8, width)
    r = block[:, at + 16 :].reshape(chips, 2, 8, half)
    turned = jnp.concatenate([r[:, :, 4:], r[:, :, :4]], axis=2)
    top = iota((chips, 8, half), 1) < 4
    r = wide(jnp.where(top, r[:, 0], turned[:, 1]), jnp.where(top, turned[:, 0], r[:, 1]))
    r = r.reshape(groups * 4, width)
    teach = jnp.concatenate([g, q, r], axis=0).astype(bf16)
    step = 256
    for start in range(0, unit_ref.shape[0], step):
        here = slice(start, start + step)
        exps = jnp.exp2(nt_dot(teach, unit_ref[here, :]) * TEACHER_EXP2)
        exp_ref[:, here] = exps.astype(bf16)
        sums = jnp.sum(exps, axis=0, keepdims=True)
        for k in range(step // LANES):
            at = start // LANES + k
            sums_ref[at : at + 1, :] = sums[:, k * LANES : (k + 1) * LANES]


def student_kernel(
    stud, core_ref, own_ref, other_ref, unit_ref, keep_ref, send_ref, total_ref, stud_ref, acc_ref, tot_ref
):
    chips, _, half = own_ref.shape
    width = 2 * half
    rows = chips * stud
    for h, rows_ref in enumerate((own_ref, other_ref)):
        block = rows_ref[...].astype(f32)[:, : 2 * stud]
        block = wide(block[:, :stud], block[:, stud:])
        stud_ref[h * rows : (h + 1) * rows, :] = block.reshape(rows, width).astype(bf16)
    step = 512
    chunk = rows
    for start in range(0, unit_ref.shape[0], step):
        protos = unit_ref[start : start + step, :]
        for c in range(2 * rows // chunk):
            here = slice(c * chunk, (c + 1) * chunk)
            weights = jnp.exp2(nt_dot(stud_ref[here, :], protos) * STUDENT_EXP2)
            part = weights[:, :LANES]
            for k in range(1, step // LANES):
                part = part + weights[:, k * LANES : (k + 1) * LANES]
            term = jnp.dot(weights.astype(bf16), protos, preferred_element_type=f32)
            if start == 0:
                tot_ref[here, :] = part
                acc_ref[here, :] = term
            else:
                tot_ref[here, :] += part
                acc_ref[here, :] += term
    is_first = core_ref[0] == 0
    for h in range(2):
        here = slice(h * rows, (h + 1) * rows)
        attract = acc_ref[here, :].reshape(chips, stud, width)
        low, high = attract[:, :, :LANES], attract[:, :, LANES:]
        keep_ref[h] = jnp.where(is_first, low, high)
        send_ref[h] = jnp.where(is_first, high, low).astype(bf16)
        total = jnp.sum(tot_ref[here, :], axis=1, keepdims=True).reshape(chips, stud, 1)
        eye = iota((chips, stud, LANES), 1) == iota((chips, stud, LANES), 2)
        total_ref[h] = jnp.sum(
            jnp.where(eye, jnp.broadcast_to(total, (chips, stud, LANES)), 0.0),
            axis=1,
            keepdims=True,
        )


def pair_kernel(mine_ref, got_ref, out_ref):
    total = mine_ref[...] + got_ref[...]
    for j in range(out_ref.shape[0]):
        out_ref[j] = total


def proto_scale_of(parts_ref):
    total = parts_ref[0].astype(f32)
    for j in range(1, parts_ref.shape[0]):
        total = total + parts_ref[j].astype(f32)
    scale = 1.0 / total
    return jnp.concatenate([scale[k : k + 1, :] for k in range(scale.shape[0])], axis=1)


def col_kernel(parts_ref, exp_ref, out_ref):
    scale = proto_scale_of(parts_ref)
    rows, cols = exp_ref.shape
    lines = []
    for g in range(rows // LANES):
        acc = None
        for k in range(cols // LANES):
            lanes = slice(k * LANES, (k + 1) * LANES)
            term = exp_ref[g * LANES : (g + 1) * LANES, lanes].astype(f32) * scale[:, lanes]
            acc = term if acc is None else acc + term
        lines.append(jnp.sum(acc.T, axis=0, keepdims=True))
    out = jnp.concatenate(lines, axis=1)
    for j in range(out_ref.shape[0]):
        out_ref[j] = out


def row_kernel(parts_ref, exp_ref, out_ref, line_ref):
    rows, cols = exp_ref.shape
    scale = 1.0 / jnp.sum(parts_ref[...], axis=0)
    acc = None
    for g in range(rows // LANES):
        tall = jnp.broadcast_to(scale[:, g * LANES : (g + 1) * LANES], (LANES, LANES)).T
        for t in range(0, LANES, 16):
            scales = jnp.concatenate([tall[t : t + 16]] * (cols // LANES), axis=1)
            term = exp_ref[g * LANES + t : g * LANES + t + 16, :].astype(f32) * scales
            term = term[:8] + term[8:]
            acc = term if acc is None else acc + term
    line = jnp.sum(acc, axis=0, keepdims=True)
    for k in range(cols // LANES):
        line_ref[k : k + 1, :] = line[:, k * LANES : (k + 1) * LANES]
    sums = line_ref[...].astype(bf16)
    for j in range(out_ref.shape[0]):
        out_ref[j] = sums


def repel_kernel(
    core_ref, parts_ref, exp_ref, unit_ref, keep_ref, got_ref, total_ref, out_ref
):
    _, chips, stud, _ = keep_ref.shape
    glob = 8
    rows = 2 * chips * glob
    scale = proto_scale_of(parts_ref)
    cols, width = unit_ref.shape
    acc = jnp.zeros((rows, LANES), f32)
    repel = jnp.zeros((rows, width), f32)
    step = 512
    for start in range(0, cols, step):
        here = slice(start, start + step)
        terms = exp_ref[:rows, here].astype(f32) * scale[:, here]
        for k in range(step // LANES):
            acc = acc + terms[:, k * LANES : (k + 1) * LANES]
        repel = repel + jnp.dot(terms.astype(bf16), unit_ref[here, :], preferred_element_type=f32)
    sums = jnp.sum(acc, axis=1, keepdims=True).reshape(2, chips, glob, 1)
    repel = repel.reshape(2, chips, glob, width)
    attract = by_core(
        core_ref, keep_ref[0] + got_ref[1].astype(f32), keep_ref[1] + got_ref[0].astype(f32)
    )
    totals = by_core(core_ref, total_ref[0], total_ref[1])
    dims = (chips, glob, LANES)
    place = iota(dims, 1) + stud == iota(dims, 2)
    for core in range(2):
        mass = jnp.where(place, jnp.broadcast_to(sums[core], dims), 0.0)
        scalars = totals[core] + jnp.sum(mass, axis=1, keepdims=True)
        high = scalars.astype(bf16).astype(f32)
        scalars = jnp.where(iota(dims, 1) == 0, high, scalars - high)
        parts = [attract[core], repel[core][:, :, :LANES], repel[core][:, :, LANES:], scalars]
        out_ref[:, core] = jnp.concatenate(parts, axis=1).astype(bf16)


def final_kernel(back_ref, student_ref, grad_ref, loss_ref, rows_ref):
    crops, images, width = student_ref.shape
    stud = crops * images
    for c in range(crops):
        rows_ref[c * images : (c + 1) * images, :] = student_ref[c].astype(f32)
    values = rows_ref[...]
    back = jnp.sum(back_ref[...].astype(f32), axis=0)
    attract = jnp.concatenate([back[0, :stud], back[1, :stud]], axis=1)
    back = back[0, stud:] + back[1, stud:]
    line = back[16:17] + back[17:18]
    sub, lane = iota((stud, LANES), 0), iota((stud, LANES), 1)
    lines = jnp.broadcast_to(line, (stud, LANES))
    total = jnp.sum(jnp.where(lane == sub, lines, 0.0), axis=1, keepdims=True)
    mass = jnp.sum(jnp.where(lane == sub + stud, lines, 0.0)[:8], axis=1, keepdims=True)
    views = jnp.concatenate([back[:8], back[8:16]], axis=1) / mass
    both = views + jnp.concatenate([views[images:], views[:images]], axis=0)
    repel = jnp.concatenate([views] + [both] * (stud // 8 - 1), axis=0)
    pairs = jnp.where(iota((stud, 1), 0) < 2 * images, 1.0, 2.0)
    inv_norm = lax.rsqrt(jnp.sum(values * values, axis=1, keepdims=True) + NORM_EPSILON)
    own = values * inv_norm
    low = own.astype(bf16).astype(f32)
    grad_unit = (pairs * attract / total - repel) / STUDENT_SOFTNESS
    cross = jnp.sum(low * repel, axis=1, keepdims=True) / STUDENT_SOFTNESS
    loss = pairs * jnp.log(total) - cross
    inner = jnp.sum(own * grad_unit, axis=1, keepdims=True)
    grad = inv_norm * (grad_unit - own * inner)
    for c in range(crops):
        grad_ref[c] = grad[c * images : (c + 1) * images]
    wide = jnp.broadcast_to(loss, (stud, LANES))
    for i in range(images):
        spread = jnp.where(sub == lane * images + i, wide, 0.0)
        loss_ref[i : i + 1, :] = jnp.sum(spread, axis=0, keepdims=True)[:, :crops]


def exchange(array, axis, **kw):
    return lax.all_to_all(array, axis, 0, 0, tiled=True, **kw)


def body(teacher_global, queue, student, prototypes):
    images, crops, width = student.shape
    queue_rows = queue.shape[0]
    groups, parts = lax.axis_size("proto"), lax.axis_size("dp")
    chips = groups // 2
    stud, glob = images * crops, images * 2
    teach_rows = groups * (glob + queue_rows)
    protos = prototypes.shape[0]
    student = jnp.transpose(student, (1, 0, 2))
    core = jnp.reshape(lax.axis_index("proto") % 2, (1,))
    scalar = pl.BlockSpec(memory_space=pltpu.SMEM)
    vmem = pl.BlockSpec(memory_space=pltpu.VMEM)

    def swap(array):
        return lax.ppermute(array, "proto", [(j, j ^ 1) for j in range(groups)])

    send_rows = 2 * (stud + glob + queue_rows)
    packed = call(
        pack_kernel,
        "pack_rows",
        shape((chips, send_rows, LANES), bf16),
        scratch_shapes=[pltpu.VMEM((send_rows, LANES), f32)],
    )(*map(in_hbm, (student, teacher_global, queue)))
    same_core = [list(range(c, groups, 2)) for c in range(2)]
    own_rows = exchange(packed, "proto", axis_index_groups=same_core)
    other_rows = swap(own_rows)
    unit_protos = call(
        unit_kernel,
        "unit_prototypes",
        shape((protos, width), bf16),
        in_specs=[pl.BlockSpec(memory_space=pl.ANY)],
        scratch_shapes=[pltpu.VMEM((protos, width), bf16), pltpu.SemaphoreType.DMA((8,))],
        flops=3 * protos * width,
        nbytes=4 * protos * width,
    )(in_hbm(prototypes))

    exps, row_parts = call(
        functools.partial(teacher_kernel, stud, glob),
        "teacher_exponentials",
        [pltpu.VMEM((teach_rows, protos), bf16), shape((protos // LANES, LANES), f32)],
        in_specs=[scalar, vmem, vmem, vmem],
        flops=2 * teach_rows * protos * width,
        nbytes=2 * teach_rows * protos,
        exps=teach_rows * protos,
    )(core, own_rows, other_rows, unit_protos)
    exps = in_vmem(exps)

    half = parts // 2
    got_sums = lax.ppermute(row_parts, "dp", [(j, (j + half) % parts) for j in range(parts)])
    all_rows = 2 * chips * stud
    keep, send, total = call(
        functools.partial(student_kernel, stud),
        "student_attract",
        [
            shape((2, chips, stud, LANES), f32),
            shape((2, chips, stud, LANES), bf16),
            shape((2, chips, 1, LANES), f32),
        ],
        in_specs=[scalar, vmem, vmem, vmem],
        scratch_shapes=[
            pltpu.VMEM((all_rows, width), bf16),
            pltpu.VMEM((all_rows, width), f32),
            pltpu.VMEM((all_rows, LANES), f32),
        ],
        flops=4 * all_rows * protos * width,
        nbytes=2 * protos * width,
        exps=all_rows * protos,
    )(core, own_rows, other_rows, unit_protos)
    got_sums, keep, send, total = lax.optimization_barrier((got_sums, keep, send, total))
    row_parts = call(pair_kernel, "add_halves", shape((half, protos // LANES, LANES), f32))(row_parts, got_sums)
    halves = [list(range(half)), list(range(half, parts))]
    row_parts = exchange(row_parts, "dp", axis_index_groups=halves)

    for iteration in range(SINK_ITERS - 1):
        col_parts = call(
            col_kernel,
            "sum_over_prototypes",
            shape((groups, 1, teach_rows), f32),
            flops=2 * teach_rows * protos,
            nbytes=2 * teach_rows * protos,
        )(row_parts, exps)
        col_parts = exchange(col_parts, "proto")
        if iteration == 0:
            col_parts, send = lax.optimization_barrier((col_parts, send))
            got = swap(send)
        row_parts = call(
            row_kernel,
            "sum_over_rows",
            shape((parts, protos // LANES, LANES), bf16),
            scratch_shapes=[pltpu.VMEM((protos // LANES, LANES), f32)],
            flops=2 * teach_rows * protos,
            nbytes=2 * teach_rows * protos,
        )(col_parts, exps)
        if iteration == 0:
            row_parts, got = lax.optimization_barrier((row_parts, got))
        row_parts = exchange(row_parts, "dp")

    back = call(
        repel_kernel,
        "repel",
        shape((chips, 2, 64, LANES), bf16),
        in_specs=[scalar] + [vmem] * 6,
        flops=2 * groups * glob * protos * width,
        nbytes=2 * protos * width,
    )(core, row_parts, exps, unit_protos, keep, got, total)
    back = exchange(back.reshape(groups, 64, LANES), "proto").reshape(chips, 2, 64, LANES)

    grad, loss = call(
        final_kernel,
        "gradients",
        [shape((crops, images, width), f32), shape((images, crops), f32)],
        scratch_shapes=[pltpu.VMEM((stud, width), f32)],
    )(back, student)
    return jnp.transpose(grad, (1, 0, 2)), loss


def solution(mesh):
    in_specs = (
        P(("dp", "proto"), None, None),
        P(("dp", "proto"), None),
        P(("dp", "proto"), None, None),
        P("proto", None),
    )
    out_specs = (P(("dp", "proto"), None, None), P(("dp", "proto"), None))
    return jax.shard_map(body, mesh=mesh, in_specs=in_specs, out_specs=out_specs, check_vma=False)
```

```python
import functools
import math

import jax
import jax.numpy as jnp
from jax import lax
from jax.experimental import pallas as pl
from jax.experimental.pallas import tpu as pltpu
from jax.sharding import PartitionSpec as P

SINK_ITERS = 3
TEACHER_SOFTNESS = 0.07
STUDENT_SOFTNESS = 0.1
NORM_EPSILON = 1e-06
TEACHER_EXP2 = math.log2(math.e) / TEACHER_SOFTNESS
STUDENT_EXP2 = math.log2(math.e) / STUDENT_SOFTNESS

LANES = 128
MIB = 1024 * 1024

f32 = jnp.float32
bf16 = jnp.bfloat16
shape = jax.ShapeDtypeStruct


def iota(shape, dim):
    return lax.broadcasted_iota(jnp.int32, shape, dim)


def unit(values):
    return values * lax.rsqrt(jnp.sum(values * values, axis=-1, keepdims=True) + NORM_EPSILON)


def nt_dot(a, b):
    return lax.dot_general(a, b, (((1,), (1,)), ((), ())), preferred_element_type=f32)


def call(kernel, name, out_shape, flops=0, nbytes=0, exps=0, vmem=32, **kw):
    return pl.pallas_call(
        kernel,
        out_shape=out_shape,
        compiler_params=pltpu.CompilerParams(vmem_limit_bytes=vmem * MIB),
        cost_estimate=pl.CostEstimate(flops=flops, bytes_accessed=nbytes, transcendentals=exps),
        name=name,
        **kw,
    )


def in_vmem(array):
    return pltpu.with_memory_space_constraint(array, pltpu.VMEM)


def in_hbm(array):
    return pltpu.with_memory_space_constraint(array, pltpu.HBM)


def pack_kernel(student_ref, teacher_ref, queue_ref, out_ref, rows_ref):
    crops, images, width = student_ref.shape
    stud, glob = crops * images, 2 * images
    half = width // 2

    def put(at, rows, height, values):
        rows_ref[at + rows : at + rows + values.shape[0], :] = values[:, :half]
        rows_ref[at + height + rows : at + height + rows + values.shape[0], :] = values[:, half:]

    for c in range(crops):
        put(0, c * images, stud, unit(student_ref[c].astype(f32)))
    at = 2 * stud
    for i in range(images):
        views = unit(teacher_ref[i].astype(f32))
        put(at, i, glob, views[1:2])
        put(at, images + i, glob, views[0:1])
    units = unit(queue_ref[...].astype(f32))
    at = at + 2 * glob
    put(at, 0, 8, units[:8])
    put(at + 16, 0, 4, units[8:])
    packed = rows_ref[...].astype(bf16)
    for j in range(out_ref.shape[0]):
        out_ref[j] = packed


def wide(low, high):
    return jnp.concatenate([low, high], axis=-1)


def unit_kernel(protos_ref, out_ref, raw_ref, sems):
    parts = sems.shape[0]
    rows = raw_ref.shape[0] // parts
    copies = []
    for j in range(parts):
        here = pl.ds(j * rows, rows)
        copies.append(pltpu.make_async_copy(protos_ref.at[here], raw_ref.at[here], sems.at[j]))
        copies[j].start()
    for j in range(parts):
        copies[j].wait()
        here = slice(j * rows, (j + 1) * rows)
        out_ref[here, :] = unit(raw_ref[here, :].astype(f32)).astype(bf16)


def by_core(core_ref, own, other):
    is_first = core_ref[0] == 0
    return jnp.where(is_first, own, other), jnp.where(is_first, other, own)


def teacher_kernel(stud, glob, core_ref, own_ref, other_ref, unit_ref, exp_ref, sums_ref):
    chips, _, half = own_ref.shape
    width = 2 * half
    at = 2 * stud
    blocks = by_core(core_ref, own_ref[...].astype(f32)[:, at:], other_ref[...].astype(f32)[:, at:])
    block = jnp.concatenate(blocks, axis=0)
    groups = 2 * chips
    at = 2 * glob
    g = wide(block[:, :glob], block[:, glob:at]).reshape(groups * glob, width)
    q = wide(block[:, at : at + 8], block[:, at + 8 : at + 16]).reshape(groups * 8, width)
    r = block[:, at + 16 :].reshape(chips, 2, 8, half)
    turned = jnp.concatenate([r[:, :, 4:], r[:, :, :4]], axis=2)
    top = iota((chips, 8, half), 1) < 4
    r = wide(jnp.where(top, r[:, 0], turned[:, 1]), jnp.where(top, turned[:, 0], r[:, 1]))
    r = r.reshape(groups * 4, width)
    teach = jnp.concatenate([g, q, r], axis=0).astype(bf16)
    step = 256
    for start in range(0, unit_ref.shape[0], step):
        here = slice(start, start + step)
        exps = jnp.exp2(nt_dot(teach, unit_ref[here, :]) * TEACHER_EXP2)
        exp_ref[:, here] = exps.astype(bf16)
        sums = jnp.sum(exps, axis=0, keepdims=True)
        for k in range(step // LANES):
            at = start // LANES + k
            sums_ref[at : at + 1, :] = sums[:, k * LANES : (k + 1) * LANES]


def other_core_kernel(stud, glob, own_ref, unit_ref, exp_ref):
    chips, _, half = own_ref.shape
    at = 2 * stud
    block = own_ref[...].astype(f32)[:, at : at + 2 * glob]
    teach = wide(block[:, :glob], block[:, glob:]).reshape(chips * glob, 2 * half).astype(bf16)
    step = 512
    for start in range(0, unit_ref.shape[0], step):
        here = slice(start, start + step)
        exp_ref[:, here] = jnp.exp2(nt_dot(teach, unit_ref[here, :]) * TEACHER_EXP2).astype(bf16)


def add_students(stud, own_ref, unit_ref, stud_ref, acc_ref, tot_ref, start_acc, start_tot):
    chips, _, half = own_ref.shape
    block = own_ref[...].astype(f32)[:, : 2 * stud]
    block = wide(block[:, :stud], block[:, stud:])
    stud_ref[...] = block.reshape(chips * stud, 2 * half).astype(bf16)
    step = 512
    for start in range(0, unit_ref.shape[0], step):
        protos = unit_ref[start : start + step, :]
        weights = jnp.exp2(nt_dot(stud_ref[...], protos) * STUDENT_EXP2)
        part = weights[:, :LANES]
        for k in range(1, step // LANES):
            part = part + weights[:, k * LANES : (k + 1) * LANES]
        term = jnp.dot(weights.astype(bf16), protos, preferred_element_type=f32)
        if start == 0 and start_acc is None:
            tot_ref[...] = part
            acc_ref[...] = term
        elif start == 0:
            tot_ref[...] = start_tot[...] + part
            acc_ref[...] = start_acc[...] + term
        else:
            tot_ref[...] += part
            acc_ref[...] += term


def student_own_kernel(stud, own_ref, unit_ref, acc_ref, tot_ref, stud_ref):
    add_students(stud, own_ref, unit_ref, stud_ref, acc_ref, tot_ref, None, None)


def student_other_kernel(
    stud, own_ref, unit_ref, start_acc, start_tot, attract_ref, total_ref, stud_ref, acc_ref, tot_ref
):
    add_students(stud, own_ref, unit_ref, stud_ref, acc_ref, tot_ref, start_acc, start_tot)
    chips = own_ref.shape[0]
    attract = acc_ref[...].reshape(chips, stud, 2 * LANES)
    attract = jnp.concatenate([attract[:, :, :LANES], attract[:, :, LANES:]], axis=1)
    attract_ref[...] = attract.astype(bf16)
    total = jnp.sum(tot_ref[...], axis=1, keepdims=True).reshape(chips, stud, 1)
    eye = iota((chips, stud, LANES), 1) == iota((chips, stud, LANES), 2)
    total_ref[...] = jnp.sum(
        jnp.where(eye, jnp.broadcast_to(total, (chips, stud, LANES)), 0.0), axis=1, keepdims=True
    )


def pair_kernel(mine_ref, got_ref, out_ref):
    total = mine_ref[...] + got_ref[...]
    for j in range(out_ref.shape[0]):
        out_ref[j] = total


def proto_scale_of(parts_ref):
    total = parts_ref[0].astype(f32)
    for j in range(1, parts_ref.shape[0]):
        total = total + parts_ref[j].astype(f32)
    scale = 1.0 / total
    return jnp.concatenate([scale[k : k + 1, :] for k in range(scale.shape[0])], axis=1)


def col_kernel(parts_ref, exp_ref, out_ref):
    scale = proto_scale_of(parts_ref)
    rows, cols = exp_ref.shape
    lines = []
    for g in range(rows // LANES):
        acc = None
        for k in range(cols // LANES):
            lanes = slice(k * LANES, (k + 1) * LANES)
            term = exp_ref[g * LANES : (g + 1) * LANES, lanes].astype(f32) * scale[:, lanes]
            acc = term if acc is None else acc + term
        lines.append(jnp.sum(acc.T, axis=0, keepdims=True))
    out = jnp.concatenate(lines, axis=1)
    for j in range(out_ref.shape[0]):
        out_ref[j] = out


def row_kernel(parts_ref, exp_ref, out_ref, line_ref):
    rows, cols = exp_ref.shape
    scale = 1.0 / jnp.sum(parts_ref[...], axis=0)
    acc = None
    for g in range(rows // LANES):
        tall = jnp.broadcast_to(scale[:, g * LANES : (g + 1) * LANES], (LANES, LANES)).T
        for t in range(0, LANES, 16):
            scales = jnp.concatenate([tall[t : t + 16]] * (cols // LANES), axis=1)
            term = exp_ref[g * LANES + t : g * LANES + t + 16, :].astype(f32) * scales
            term = term[:8] + term[8:]
            acc = term if acc is None else acc + term
    line = jnp.sum(acc, axis=0, keepdims=True)
    for k in range(cols // LANES):
        line_ref[k : k + 1, :] = line[:, k * LANES : (k + 1) * LANES]
    sums = line_ref[...].astype(bf16)
    for j in range(out_ref.shape[0]):
        out_ref[j] = sums


def add_repel(parts_ref, exps_of, unit_ref, repel, mass):
    scale = proto_scale_of(parts_ref)
    step = 512
    for start in range(0, unit_ref.shape[0], step):
        here = slice(start, start + step)
        terms = exps_of(here).astype(f32) * scale[:, here]
        for k in range(step // LANES):
            mass = mass + terms[:, k * LANES : (k + 1) * LANES]
        repel = repel + jnp.dot(terms.astype(bf16), unit_ref[here, :], preferred_element_type=f32)
    return repel, mass


def repel_own_kernel(core_ref, parts_ref, exp_ref, unit_ref, repel_ref, mass_ref):
    rows = repel_ref.shape[0]
    mine = pl.ds(pl.multiple_of(core_ref[0] * rows, rows), rows)
    repel_ref[...], mass_ref[...] = add_repel(
        parts_ref,
        lambda here: exp_ref[mine, here],
        unit_ref,
        jnp.zeros(repel_ref.shape, f32),
        jnp.zeros(mass_ref.shape, f32),
    )


def repel_other_kernel(
    stud, parts_ref, exp_ref, unit_ref, repel_ref, mass_ref, attract_ref, total_ref, out_ref
):
    repel, mass = add_repel(
        parts_ref, lambda here: exp_ref[:, here], unit_ref, repel_ref[...], mass_ref[...]
    )
    chips = attract_ref.shape[0]
    glob = repel.shape[0] // chips
    repel = repel.reshape(chips, glob, 2 * LANES)
    dims = (chips, glob, LANES)
    place = iota(dims, 1) + stud == iota(dims, 2)
    mass = jnp.sum(mass, axis=1, keepdims=True).reshape(chips, glob, 1)
    mass = jnp.where(place, jnp.broadcast_to(mass, dims), 0.0)
    scalars = total_ref[...] + jnp.sum(mass, axis=1, keepdims=True)
    high = scalars.astype(bf16).astype(f32)
    scalars = jnp.where(iota(dims, 1) == 0, high, scalars - high)
    parts = [attract_ref[...].astype(f32), repel[:, :, :LANES], repel[:, :, LANES:], scalars]
    out_ref[...] = jnp.concatenate(parts, axis=1).astype(bf16)


def final_kernel(back_ref, student_ref, grad_ref, loss_ref, rows_ref):
    crops, images, width = student_ref.shape
    stud = crops * images
    for c in range(crops):
        rows_ref[c * images : (c + 1) * images, :] = student_ref[c].astype(f32)
    values = rows_ref[...]
    back = jnp.sum(back_ref[...].astype(f32), axis=0)
    attract = wide(back[:stud], back[stud : 2 * stud])
    back = back[2 * stud :]
    line = back[16:17] + back[17:18]
    sub, lane = iota((stud, LANES), 0), iota((stud, LANES), 1)
    lines = jnp.broadcast_to(line, (stud, LANES))
    total = jnp.sum(jnp.where(lane == sub, lines, 0.0), axis=1, keepdims=True)
    mass = jnp.sum(jnp.where(lane == sub + stud, lines, 0.0)[:8], axis=1, keepdims=True)
    views = wide(back[:8], back[8:16]) / mass
    both = views + jnp.concatenate([views[images:], views[:images]], axis=0)
    repel = jnp.concatenate([views] + [both] * (stud // 8 - 1), axis=0)
    pairs = jnp.where(iota((stud, 1), 0) < 2 * images, 1.0, 2.0)
    inv_norm = lax.rsqrt(jnp.sum(values * values, axis=1, keepdims=True) + NORM_EPSILON)
    own = values * inv_norm
    low = own.astype(bf16).astype(f32)
    grad_unit = (pairs * attract / total - repel) / STUDENT_SOFTNESS
    cross = jnp.sum(low * repel, axis=1, keepdims=True) / STUDENT_SOFTNESS
    loss = pairs * jnp.log(total) - cross
    inner = jnp.sum(own * grad_unit, axis=1, keepdims=True)
    grad = inv_norm * (grad_unit - own * inner)
    for c in range(crops):
        grad_ref[c] = grad[c * images : (c + 1) * images]
    spreads = jnp.broadcast_to(loss, (stud, LANES))
    for i in range(images):
        spread = jnp.where(sub == lane * images + i, spreads, 0.0)
        loss_ref[i : i + 1, :] = jnp.sum(spread, axis=0, keepdims=True)[:, :crops]


def exchange(array, axis, **kw):
    return lax.all_to_all(array, axis, 0, 0, tiled=True, **kw)


def body(teacher_global, queue, student, prototypes):
    images, crops, width = student.shape
    queue_rows = queue.shape[0]
    groups, parts = lax.axis_size("proto"), lax.axis_size("dp")
    chips = groups // 2
    stud, glob = images * crops, images * 2
    teach_rows = groups * (glob + queue_rows)
    protos = prototypes.shape[0]
    student = jnp.transpose(student, (1, 0, 2))
    core = jnp.reshape(lax.axis_index("proto") % 2, (1,))
    scalar = pl.BlockSpec(memory_space=pltpu.SMEM)
    vmem = pl.BlockSpec(memory_space=pltpu.VMEM)

    def swap(array):
        return lax.ppermute(array, "proto", [(j, j ^ 1) for j in range(groups)])

    send_rows = 2 * (stud + glob + queue_rows)
    packed = call(
        pack_kernel,
        "pack_rows",
        shape((chips, send_rows, LANES), bf16),
        scratch_shapes=[pltpu.VMEM((send_rows, LANES), f32)],
    )(*map(in_hbm, (student, teacher_global, queue)))
    same_core = [list(range(c, groups, 2)) for c in range(2)]
    own_rows = exchange(packed, "proto", axis_index_groups=same_core)
    other_rows = swap(own_rows)
    own_rows, prototypes = lax.optimization_barrier((own_rows, prototypes))
    unit_protos = call(
        unit_kernel,
        "unit_prototypes",
        shape((protos, width), bf16),
        in_specs=[pl.BlockSpec(memory_space=pl.ANY)],
        scratch_shapes=[pltpu.VMEM((protos, width), bf16), pltpu.SemaphoreType.DMA((8,))],
        flops=3 * protos * width,
        nbytes=4 * protos * width,
    )(in_hbm(prototypes))

    other_rows, unit_protos = lax.optimization_barrier((other_rows, unit_protos))
    other_protos = swap(unit_protos)
    exps, row_parts = call(
        functools.partial(teacher_kernel, stud, glob),
        "teacher_exponentials",
        [pltpu.VMEM((teach_rows, protos), bf16), shape((protos // LANES, LANES), f32)],
        in_specs=[scalar, vmem, vmem, vmem],
        flops=2 * teach_rows * protos * width,
        nbytes=2 * teach_rows * protos,
        exps=teach_rows * protos,
    )(core, own_rows, other_rows, unit_protos)
    exps = in_vmem(exps)

    row_parts, own_rows = lax.optimization_barrier((row_parts, own_rows))
    half = parts // 2
    got_sums = lax.ppermute(row_parts, "dp", [(j, (j + half) % parts) for j in range(parts)])
    own_students = chips * stud
    work = dict(
        flops=4 * own_students * protos * width,
        nbytes=2 * protos * width,
        exps=own_students * protos,
    )
    rows_scratch = pltpu.VMEM((own_students, width), bf16)
    acc, tot = call(
        functools.partial(student_own_kernel, stud),
        "students_own_core",
        [shape((own_students, width), f32), shape((own_students, LANES), f32)],
        scratch_shapes=[rows_scratch],
        **work,
    )(own_rows, unit_protos)
    attract, total = call(
        functools.partial(student_other_kernel, stud),
        "students_other_core",
        [shape((chips, 2 * stud, LANES), bf16), shape((chips, 1, LANES), f32)],
        scratch_shapes=[
            rows_scratch,
            pltpu.VMEM((own_students, width), f32),
            pltpu.VMEM((own_students, LANES), f32),
        ],
        **work,
    )(own_rows, other_protos, acc, tot)
    own_glob = chips * glob
    other_exps = call(
        functools.partial(other_core_kernel, stud, glob),
        "teacher_other_core",
        pltpu.VMEM((own_glob, protos), bf16),
        flops=2 * own_glob * protos * width,
        nbytes=2 * protos * width,
        exps=own_glob * protos,
    )(own_rows, other_protos)
    got_sums, attract, total, other_exps = lax.optimization_barrier(
        (got_sums, attract, total, other_exps)
    )
    other_exps = in_vmem(other_exps)
    row_parts = call(pair_kernel, "add_halves", shape((half, protos // LANES, LANES), f32))(row_parts, got_sums)
    halves = [list(range(half)), list(range(half, parts))]
    row_parts = exchange(row_parts, "dp", axis_index_groups=halves)

    for iteration in range(SINK_ITERS - 1):
        col_parts = call(
            col_kernel,
            "sum_over_prototypes",
            shape((groups, 1, teach_rows), f32),
            flops=2 * teach_rows * protos,
            nbytes=2 * teach_rows * protos,
        )(row_parts, exps)
        col_parts = exchange(col_parts, "proto")
        row_parts = call(
            row_kernel,
            "sum_over_rows",
            shape((parts, protos // LANES, LANES), bf16),
            scratch_shapes=[pltpu.VMEM((protos // LANES, LANES), f32)],
            flops=2 * teach_rows * protos,
            nbytes=2 * teach_rows * protos,
        )(col_parts, exps)
        row_parts = exchange(row_parts, "dp")

    other_parts = swap(row_parts)
    work = dict(flops=2 * own_glob * protos * width, nbytes=4 * protos * width)
    repel, mass = call(
        repel_own_kernel,
        "repel_own_core",
        [shape((own_glob, width), f32), shape((own_glob, LANES), f32)],
        in_specs=[scalar] + [vmem] * 3,
        **work,
    )(core, row_parts, exps, unit_protos)
    back = call(
        functools.partial(repel_other_kernel, stud),
        "repel_other_core",
        shape((chips, 2 * stud + 2 * glob + 8, LANES), bf16),
        **work,
    )(other_parts, other_exps, other_protos, repel, mass, attract, total)
    back = exchange(back, "proto", axis_index_groups=same_core)

    grad, loss = call(
        final_kernel,
        "gradients",
        [shape((crops, images, width), f32), shape((images, crops), f32)],
        scratch_shapes=[pltpu.VMEM((stud, width), f32)],
    )(back, student)
    return jnp.transpose(grad, (1, 0, 2)), loss


def solution(mesh):
    in_specs = (
        P(("dp", "proto"), None, None),
        P(("dp", "proto"), None),
        P(("dp", "proto"), None, None),
        P("proto", None),
    )
    out_specs = (P(("dp", "proto"), None, None), P(("dp", "proto"), None))
    return jax.shard_map(body, mesh=mesh, in_specs=in_specs, out_specs=out_specs, check_vma=False)
```

```python
import functools
import math

import jax
import jax.numpy as jnp
from jax import lax
from jax.experimental import pallas as pl
from jax.experimental.pallas import tpu as pltpu
from jax.sharding import PartitionSpec as P

SINK_ITERS = 3
TEACHER_SOFTNESS = 0.07
STUDENT_SOFTNESS = 0.1
NORM_EPSILON = 1e-06
TEACHER_EXP2 = math.log2(math.e) / TEACHER_SOFTNESS
STUDENT_EXP2 = math.log2(math.e) / STUDENT_SOFTNESS

LANES = 128
MIB = 1024 * 1024

f32 = jnp.float32
bf16 = jnp.bfloat16
shape = jax.ShapeDtypeStruct


def iota(shape, dim):
    return lax.broadcasted_iota(jnp.int32, shape, dim)


def unit(values):
    return values * lax.rsqrt(jnp.sum(values * values, axis=-1, keepdims=True) + NORM_EPSILON)


def nt_dot(a, b):
    return lax.dot_general(a, b, (((1,), (1,)), ((), ())), preferred_element_type=f32)


def call(kernel, name, out_shape, flops=0, nbytes=0, exps=0, vmem=16, **kw):
    return pl.pallas_call(
        kernel,
        out_shape=out_shape,
        compiler_params=pltpu.CompilerParams(vmem_limit_bytes=vmem * MIB),
        cost_estimate=pl.CostEstimate(flops=flops, bytes_accessed=nbytes, transcendentals=exps),
        name=name,
        **kw,
    )


def in_vmem(array):
    return pltpu.with_memory_space_constraint(array, pltpu.VMEM)


def in_hbm(array):
    return pltpu.with_memory_space_constraint(array, pltpu.HBM)


def pack_kernel(student_ref, teacher_ref, queue_ref, out_ref, rows_ref):
    crops, images, width = student_ref.shape
    stud, glob = crops * images, 2 * images
    half = width // 2

    def put(at, rows, height, values):
        rows_ref[at + rows : at + rows + values.shape[0], :] = values[:, :half]
        rows_ref[at + height + rows : at + height + rows + values.shape[0], :] = values[:, half:]

    for c in range(crops):
        put(0, c * images, stud, unit(student_ref[c].astype(f32)))
    at = 2 * stud
    for i in range(images):
        views = unit(teacher_ref[i].astype(f32))
        put(at, i, glob, views[1:2])
        put(at, images + i, glob, views[0:1])
    units = unit(queue_ref[...].astype(f32))
    at = at + 2 * glob
    put(at, 0, 8, units[:8])
    put(at + 16, 0, 4, units[8:])
    packed = rows_ref[...].astype(bf16)
    for j in range(out_ref.shape[0]):
        out_ref[j] = packed


def wide(low, high):
    return jnp.concatenate([low, high], axis=-1)


def unit_kernel(protos_ref, out_ref, raw_ref, sems):
    parts = sems.shape[0]
    rows = raw_ref.shape[0] // parts
    copies = []
    for j in range(parts):
        here = pl.ds(j * rows, rows)
        copies.append(pltpu.make_async_copy(protos_ref.at[here], raw_ref.at[here], sems.at[j]))
        copies[j].start()
    for j in range(parts):
        copies[j].wait()
        here = slice(j * rows, (j + 1) * rows)
        out_ref[here, :] = unit(raw_ref[here, :].astype(f32)).astype(bf16)


def by_core(core_ref, own, other):
    is_first = core_ref[0] == 0
    return jnp.where(is_first, own, other), jnp.where(is_first, other, own)


def teacher_kernel(stud, glob, core_ref, own_ref, other_ref, unit_ref, exp_ref, sums_ref):
    chips, _, half = own_ref.shape
    width = 2 * half
    at = 2 * stud
    blocks = by_core(core_ref, own_ref[...].astype(f32)[:, at:], other_ref[...].astype(f32)[:, at:])
    block = jnp.concatenate(blocks, axis=0)
    groups = 2 * chips
    at = 2 * glob
    g = wide(block[:, :glob], block[:, glob:at]).reshape(groups * glob, width)
    q = wide(block[:, at : at + 8], block[:, at + 8 : at + 16]).reshape(groups * 8, width)
    r = block[:, at + 16 :].reshape(chips, 2, 8, half)
    turned = jnp.concatenate([r[:, :, 4:], r[:, :, :4]], axis=2)
    top = iota((chips, 8, half), 1) < 4
    r = wide(jnp.where(top, r[:, 0], turned[:, 1]), jnp.where(top, turned[:, 0], r[:, 1]))
    r = r.reshape(groups * 4, width)
    teach = jnp.concatenate([g, q, r], axis=0).astype(bf16)
    step = 256
    for start in range(0, unit_ref.shape[0], step):
        here = slice(start, start + step)
        exps = jnp.exp2(nt_dot(teach, unit_ref[here, :]) * TEACHER_EXP2)
        exp_ref[:, here] = exps.astype(bf16)
        sums = jnp.sum(exps, axis=0, keepdims=True)
        for k in range(step // LANES):
            at = start // LANES + k
            sums_ref[at : at + 1, :] = sums[:, k * LANES : (k + 1) * LANES]


def other_core_kernel(stud, glob, own_ref, unit_ref, exp_ref):
    chips, _, half = own_ref.shape
    at = 2 * stud
    block = own_ref[...].astype(f32)[:, at : at + 2 * glob]
    teach = wide(block[:, :glob], block[:, glob:]).reshape(chips * glob, 2 * half).astype(bf16)
    step = 512
    for start in range(0, unit_ref.shape[0], step):
        here = slice(start, start + step)
        exp_ref[:, here] = jnp.exp2(nt_dot(teach, unit_ref[here, :]) * TEACHER_EXP2).astype(bf16)


def add_students(stud, own_ref, unit_ref, stud_ref, acc_ref, tot_ref, start_acc, start_tot):
    chips, _, half = own_ref.shape
    block = own_ref[...].astype(f32)[:, : 2 * stud]
    block = wide(block[:, :stud], block[:, stud:])
    stud_ref[...] = block.reshape(chips * stud, 2 * half).astype(bf16)
    step = 512
    for start in range(0, unit_ref.shape[0], step):
        protos = unit_ref[start : start + step, :]
        weights = jnp.exp2(nt_dot(stud_ref[...], protos) * STUDENT_EXP2)
        part = weights[:, :LANES]
        for k in range(1, step // LANES):
            part = part + weights[:, k * LANES : (k + 1) * LANES]
        term = jnp.dot(weights.astype(bf16), protos, preferred_element_type=f32)
        if start == 0 and start_acc is None:
            tot_ref[...] = part
            acc_ref[...] = term
        elif start == 0:
            tot_ref[...] = start_tot[...] + part
            acc_ref[...] = start_acc[...] + term
        else:
            tot_ref[...] += part
            acc_ref[...] += term


def student_own_kernel(stud, own_ref, unit_ref, acc_ref, tot_ref, stud_ref):
    add_students(stud, own_ref, unit_ref, stud_ref, acc_ref, tot_ref, None, None)


def student_other_kernel(
    stud, own_ref, unit_ref, start_acc, start_tot, attract_ref, total_ref, stud_ref, acc_ref, tot_ref
):
    add_students(stud, own_ref, unit_ref, stud_ref, acc_ref, tot_ref, start_acc, start_tot)
    chips = own_ref.shape[0]
    attract = acc_ref[...].reshape(chips, stud, 2 * LANES)
    attract = jnp.concatenate([attract[:, :, :LANES], attract[:, :, LANES:]], axis=1)
    attract_ref[...] = attract.astype(bf16)
    total = jnp.sum(tot_ref[...], axis=1, keepdims=True).reshape(chips, stud, 1)
    eye = iota((chips, stud, LANES), 1) == iota((chips, stud, LANES), 2)
    total_ref[...] = jnp.sum(
        jnp.where(eye, jnp.broadcast_to(total, (chips, stud, LANES)), 0.0), axis=1, keepdims=True
    )


def pair_kernel(mine_ref, got_ref, out_ref):
    total = mine_ref[...] + got_ref[...]
    for j in range(out_ref.shape[0]):
        out_ref[j] = total


def proto_scale_of(parts_ref):
    total = parts_ref[0].astype(f32)
    for j in range(1, parts_ref.shape[0]):
        total = total + parts_ref[j].astype(f32)
    scale = 1.0 / total
    return jnp.concatenate([scale[k : k + 1, :] for k in range(scale.shape[0])], axis=1)


def col_kernel(parts_ref, exp_ref, out_ref):
    scale = proto_scale_of(parts_ref)
    rows, cols = exp_ref.shape
    lines = []
    for g in range(rows // LANES):
        acc = None
        for k in range(cols // LANES):
            lanes = slice(k * LANES, (k + 1) * LANES)
            term = exp_ref[g * LANES : (g + 1) * LANES, lanes].astype(f32) * scale[:, lanes]
            acc = term if acc is None else acc + term
        lines.append(jnp.sum(acc.T, axis=0, keepdims=True))
    out = jnp.concatenate(lines, axis=1)
    for j in range(out_ref.shape[0]):
        out_ref[j] = out


def row_kernel(parts_ref, exp_ref, out_ref, line_ref):
    rows, cols = exp_ref.shape
    scale = 1.0 / jnp.sum(parts_ref[...], axis=0)
    acc = None
    for g in range(rows // LANES):
        tall = jnp.broadcast_to(scale[:, g * LANES : (g + 1) * LANES], (LANES, LANES)).T
        for t in range(0, LANES, 16):
            scales = jnp.concatenate([tall[t : t + 16]] * (cols // LANES), axis=1)
            term = exp_ref[g * LANES + t : g * LANES + t + 16, :].astype(f32) * scales
            term = term[:8] + term[8:]
            acc = term if acc is None else acc + term
    line = jnp.sum(acc, axis=0, keepdims=True)
    for k in range(cols // LANES):
        line_ref[k : k + 1, :] = line[:, k * LANES : (k + 1) * LANES]
    sums = line_ref[...].astype(bf16)
    for j in range(out_ref.shape[0]):
        out_ref[j] = sums


def add_repel(parts_ref, exps_of, unit_ref, repel, mass):
    scale = proto_scale_of(parts_ref)
    step = 512
    for start in range(0, unit_ref.shape[0], step):
        here = slice(start, start + step)
        terms = exps_of(here).astype(f32) * scale[:, here]
        for k in range(step // LANES):
            mass = mass + terms[:, k * LANES : (k + 1) * LANES]
        repel = repel + jnp.dot(terms.astype(bf16), unit_ref[here, :], preferred_element_type=f32)
    return repel, mass


def repel_own_kernel(core_ref, parts_ref, exp_ref, unit_ref, repel_ref, mass_ref):
    rows = repel_ref.shape[0]
    mine = pl.ds(pl.multiple_of(core_ref[0] * rows, rows), rows)
    repel_ref[...], mass_ref[...] = add_repel(
        parts_ref,
        lambda here: exp_ref[mine, here],
        unit_ref,
        jnp.zeros(repel_ref.shape, f32),
        jnp.zeros(mass_ref.shape, f32),
    )


def repel_other_kernel(
    stud, parts_ref, exp_ref, unit_ref, repel_ref, mass_ref, attract_ref, total_ref, out_ref
):
    repel, mass = add_repel(
        parts_ref, lambda here: exp_ref[:, here], unit_ref, repel_ref[...], mass_ref[...]
    )
    chips = attract_ref.shape[0]
    glob = repel.shape[0] // chips
    repel = repel.reshape(chips, glob, 2 * LANES)
    dims = (chips, glob, LANES)
    place = iota(dims, 1) + stud == iota(dims, 2)
    mass = jnp.sum(mass, axis=1, keepdims=True).reshape(chips, glob, 1)
    mass = jnp.where(place, jnp.broadcast_to(mass, dims), 0.0)
    scalars = total_ref[...] + jnp.sum(mass, axis=1, keepdims=True)
    high = scalars.astype(bf16).astype(f32)
    scalars = jnp.where(iota(dims, 1) == 0, high, scalars - high)
    parts = [attract_ref[...].astype(f32), repel[:, :, :LANES], repel[:, :, LANES:], scalars]
    out_ref[...] = jnp.concatenate(parts, axis=1).astype(bf16)


def final_kernel(back_ref, student_ref, grad_ref, loss_ref, rows_ref):
    crops, images, width = student_ref.shape
    stud = crops * images
    for c in range(crops):
        rows_ref[c * images : (c + 1) * images, :] = student_ref[c].astype(f32)
    values = rows_ref[...]
    back = jnp.sum(back_ref[...].astype(f32), axis=0)
    attract = wide(back[:stud], back[stud : 2 * stud])
    back = back[2 * stud :]
    line = back[16:17] + back[17:18]
    sub, lane = iota((stud, LANES), 0), iota((stud, LANES), 1)
    lines = jnp.broadcast_to(line, (stud, LANES))
    total = jnp.sum(jnp.where(lane == sub, lines, 0.0), axis=1, keepdims=True)
    mass = jnp.sum(jnp.where(lane == sub + stud, lines, 0.0)[:8], axis=1, keepdims=True)
    views = wide(back[:8], back[8:16]) / mass
    both = views + jnp.concatenate([views[images:], views[:images]], axis=0)
    repel = jnp.concatenate([views] + [both] * (stud // 8 - 1), axis=0)
    pairs = jnp.where(iota((stud, 1), 0) < 2 * images, 1.0, 2.0)
    inv_norm = lax.rsqrt(jnp.sum(values * values, axis=1, keepdims=True) + NORM_EPSILON)
    own = values * inv_norm
    low = own.astype(bf16).astype(f32)
    grad_unit = (pairs * attract / total - repel) / STUDENT_SOFTNESS
    cross = jnp.sum(low * repel, axis=1, keepdims=True) / STUDENT_SOFTNESS
    loss = pairs * jnp.log(total) - cross
    inner = jnp.sum(own * grad_unit, axis=1, keepdims=True)
    grad = inv_norm * (grad_unit - own * inner)
    for c in range(crops):
        grad_ref[c] = grad[c * images : (c + 1) * images]
    spreads = jnp.broadcast_to(loss, (stud, LANES))
    for i in range(images):
        spread = jnp.where(sub == lane * images + i, spreads, 0.0)
        loss_ref[i : i + 1, :] = jnp.sum(spread, axis=0, keepdims=True)[:, :crops]


def exchange(array, axis, **kw):
    return lax.all_to_all(array, axis, 0, 0, tiled=True, **kw)


def body(teacher_global, queue, student, prototypes):
    images, crops, width = student.shape
    queue_rows = queue.shape[0]
    groups, parts = lax.axis_size("proto"), lax.axis_size("dp")
    chips = groups // 2
    stud, glob = images * crops, images * 2
    teach_rows = groups * (glob + queue_rows)
    protos = prototypes.shape[0]
    student = jnp.transpose(student, (1, 0, 2))
    core = jnp.reshape(lax.axis_index("proto") & 1, (1,))
    core, student = lax.optimization_barrier((core, student))
    scalar = pl.BlockSpec(memory_space=pltpu.SMEM)
    vmem = pl.BlockSpec(memory_space=pltpu.VMEM)

    def swap(array):
        return lax.ppermute(array, "proto", [(j, j ^ 1) for j in range(groups)])

    send_rows = 2 * (stud + glob + queue_rows)
    packed = call(
        pack_kernel,
        "pack_rows",
        shape((chips, send_rows, LANES), bf16),
        scratch_shapes=[pltpu.VMEM((send_rows, LANES), f32)],
    )(*map(in_hbm, (student, teacher_global, queue)))
    same_core = [list(range(c, groups, 2)) for c in range(2)]
    own_rows = exchange(packed, "proto", axis_index_groups=same_core)
    other_rows = swap(own_rows)
    own_rows, prototypes = lax.optimization_barrier((own_rows, prototypes))
    unit_protos = call(
        unit_kernel,
        "unit_prototypes",
        shape((protos, width), bf16),
        in_specs=[pl.BlockSpec(memory_space=pl.ANY)],
        scratch_shapes=[pltpu.VMEM((protos, width), bf16), pltpu.SemaphoreType.DMA((8,))],
        flops=3 * protos * width,
        nbytes=4 * protos * width,
    )(in_hbm(prototypes))

    other_rows, unit_protos = lax.optimization_barrier((other_rows, unit_protos))
    other_protos = swap(unit_protos)
    exps, row_parts = call(
        functools.partial(teacher_kernel, stud, glob),
        "teacher_exponentials",
        [pltpu.VMEM((teach_rows, protos), bf16), shape((protos // LANES, LANES), f32)],
        in_specs=[scalar, vmem, vmem, vmem],
        flops=2 * teach_rows * protos * width,
        nbytes=2 * teach_rows * protos,
        exps=teach_rows * protos,
    )(core, own_rows, other_rows, unit_protos)
    exps = in_vmem(exps)

    row_parts, own_rows = lax.optimization_barrier((row_parts, own_rows))
    half = parts // 2
    got_sums = lax.ppermute(row_parts, "dp", [(j, (j + half) % parts) for j in range(parts)])
    own_students = chips * stud
    work = dict(
        flops=4 * own_students * protos * width,
        nbytes=2 * protos * width,
        exps=own_students * protos,
    )
    rows_scratch = pltpu.VMEM((own_students, width), bf16)
    acc, tot = call(
        functools.partial(student_own_kernel, stud),
        "students_own_core",
        [shape((own_students, width), f32), shape((own_students, LANES), f32)],
        scratch_shapes=[rows_scratch],
        **work,
    )(own_rows, unit_protos)
    attract, total = call(
        functools.partial(student_other_kernel, stud),
        "students_other_core",
        [shape((chips, 2 * stud, LANES), bf16), shape((chips, 1, LANES), f32)],
        scratch_shapes=[
            rows_scratch,
            pltpu.VMEM((own_students, width), f32),
            pltpu.VMEM((own_students, LANES), f32),
        ],
        **work,
    )(own_rows, other_protos, acc, tot)
    own_glob = chips * glob
    other_exps = call(
        functools.partial(other_core_kernel, stud, glob),
        "teacher_other_core",
        pltpu.VMEM((own_glob, protos), bf16),
        flops=2 * own_glob * protos * width,
        nbytes=2 * protos * width,
        exps=own_glob * protos,
    )(own_rows, other_protos)
    got_sums, attract, total, other_exps = lax.optimization_barrier(
        (got_sums, attract, total, other_exps)
    )
    other_exps = in_vmem(other_exps)
    row_parts = call(pair_kernel, "add_halves", shape((half, protos // LANES, LANES), f32))(row_parts, got_sums)
    halves = [list(range(half)), list(range(half, parts))]
    row_parts = exchange(row_parts, "dp", axis_index_groups=halves)

    for iteration in range(SINK_ITERS - 1):
        col_parts = call(
            col_kernel,
            "sum_over_prototypes",
            shape((groups, 1, teach_rows), f32),
            flops=2 * teach_rows * protos,
            nbytes=2 * teach_rows * protos,
        )(row_parts, exps)
        col_parts = exchange(col_parts, "proto")
        row_parts = call(
            row_kernel,
            "sum_over_rows",
            shape((parts, protos // LANES, LANES), bf16),
            scratch_shapes=[pltpu.VMEM((protos // LANES, LANES), f32)],
            flops=2 * teach_rows * protos,
            nbytes=2 * teach_rows * protos,
        )(col_parts, exps)
        row_parts = exchange(row_parts, "dp")

    other_parts = swap(row_parts)
    work = dict(flops=2 * own_glob * protos * width, nbytes=4 * protos * width)
    repel, mass = call(
        repel_own_kernel,
        "repel_own_core",
        [shape((own_glob, width), f32), shape((own_glob, LANES), f32)],
        in_specs=[scalar] + [vmem] * 3,
        **work,
    )(core, row_parts, exps, unit_protos)
    back = call(
        functools.partial(repel_other_kernel, stud),
        "repel_other_core",
        shape((chips, 2 * stud + 2 * glob + 8, LANES), bf16),
        **work,
    )(other_parts, other_exps, other_protos, repel, mass, attract, total)
    back = exchange(back, "proto", axis_index_groups=same_core)

    grad, loss = call(
        final_kernel,
        "gradients",
        [shape((crops, images, width), f32), shape((images, crops), f32)],
        scratch_shapes=[pltpu.VMEM((stud, width), f32)],
    )(back, student)
    return jnp.transpose(grad, (1, 0, 2)), loss


def solution(mesh):
    in_specs = (
        P(("dp", "proto"), None, None),
        P(("dp", "proto"), None),
        P(("dp", "proto"), None, None),
        P("proto", None),
    )
    out_specs = (P(("dp", "proto"), None, None), P(("dp", "proto"), None))
    return jax.shard_map(body, mesh=mesh, in_specs=in_specs, out_specs=out_specs, check_vma=False)
```

```python
import functools
import math

import jax
import jax.numpy as jnp
from jax import lax
from jax.experimental import pallas as pl
from jax.experimental.pallas import tpu as pltpu
from jax.sharding import PartitionSpec as P

SINK_ITERS = 3
TEACHER_SOFTNESS = 0.07
STUDENT_SOFTNESS = 0.1
NORM_EPSILON = 1e-06
TEACHER_EXP2 = math.log2(math.e) / TEACHER_SOFTNESS
STUDENT_EXP2 = math.log2(math.e) / STUDENT_SOFTNESS

LANES = 128
MIB = 1024 * 1024

f32 = jnp.float32
bf16 = jnp.bfloat16
shape = jax.ShapeDtypeStruct


def iota(shape, dim):
    return lax.broadcasted_iota(jnp.int32, shape, dim)


def unit(values):
    return values * lax.rsqrt(jnp.sum(values * values, axis=-1, keepdims=True) + NORM_EPSILON)


def nt_dot(a, b):
    return lax.dot_general(a, b, (((1,), (1,)), ((), ())), preferred_element_type=f32)


def call(kernel, name, out_shape, flops=0, nbytes=0, exps=0, vmem=16, **kw):
    return pl.pallas_call(
        kernel,
        out_shape=out_shape,
        compiler_params=pltpu.CompilerParams(vmem_limit_bytes=vmem * MIB),
        cost_estimate=pl.CostEstimate(flops=flops, bytes_accessed=nbytes, transcendentals=exps),
        name=name,
        **kw,
    )


def in_vmem(array):
    return pltpu.with_memory_space_constraint(array, pltpu.VMEM)


def in_hbm(array):
    return pltpu.with_memory_space_constraint(array, pltpu.HBM)


def pack_kernel(student_ref, teacher_ref, queue_ref, out_ref, rows_ref):
    crops, images, width = student_ref.shape
    stud, glob = crops * images, 2 * images
    half = width // 2

    def put(at, rows, height, values):
        rows_ref[at + rows : at + rows + values.shape[0], :] = values[:, :half]
        rows_ref[at + height + rows : at + height + rows + values.shape[0], :] = values[:, half:]

    for c in range(crops):
        put(0, c * images, stud, unit(student_ref[c].astype(f32)))
    at = 2 * stud
    for i in range(images):
        views = unit(teacher_ref[i].astype(f32))
        put(at, i, glob, views[1:2])
        put(at, images + i, glob, views[0:1])
    units = unit(queue_ref[...].astype(f32))
    at = at + 2 * glob
    put(at, 0, 8, units[:8])
    put(at + 16, 0, 4, units[8:])
    packed = rows_ref[...].astype(bf16)
    for j in range(out_ref.shape[0]):
        out_ref[j] = packed


def wide(low, high):
    return jnp.concatenate([low, high], axis=-1)


def unit_kernel(protos_ref, out_ref, raw_ref, sems):
    parts = sems.shape[0]
    rows = raw_ref.shape[0] // parts
    copies = []
    for j in range(parts):
        here = pl.ds(j * rows, rows)
        copies.append(pltpu.make_async_copy(protos_ref.at[here], raw_ref.at[here], sems.at[j]))
        copies[j].start()
    for j in range(parts):
        copies[j].wait()
        here = slice(j * rows, (j + 1) * rows)
        out_ref[here, :] = unit(raw_ref[here, :].astype(f32)).astype(bf16)


def by_core(core_ref, own, other):
    is_first = core_ref[0] == 0
    return jnp.where(is_first, own, other), jnp.where(is_first, other, own)


def teacher_kernel(stud, glob, core_ref, own_ref, other_ref, unit_ref, exp_ref, sums_ref):
    chips, _, half = own_ref.shape
    width = 2 * half
    at = 2 * stud
    blocks = by_core(core_ref, own_ref[...].astype(f32)[:, at:], other_ref[...].astype(f32)[:, at:])
    block = jnp.concatenate(blocks, axis=0)
    groups = 2 * chips
    at = 2 * glob
    g = wide(block[:, :glob], block[:, glob:at]).reshape(groups * glob, width)
    q = wide(block[:, at : at + 8], block[:, at + 8 : at + 16]).reshape(groups * 8, width)
    r = block[:, at + 16 :].reshape(chips, 2, 8, half)
    turned = jnp.concatenate([r[:, :, 4:], r[:, :, :4]], axis=2)
    top = iota((chips, 8, half), 1) < 4
    r = wide(jnp.where(top, r[:, 0], turned[:, 1]), jnp.where(top, turned[:, 0], r[:, 1]))
    r = r.reshape(groups * 4, width)
    teach = jnp.concatenate([g, q, r], axis=0).astype(bf16)
    step = 256
    for start in range(0, unit_ref.shape[0], step):
        here = slice(start, start + step)
        exps = jnp.exp2(nt_dot(teach, unit_ref[here, :]) * TEACHER_EXP2)
        exp_ref[:, here] = exps.astype(bf16)
        sums = jnp.sum(exps, axis=0, keepdims=True)
        for k in range(step // LANES):
            at = start // LANES + k
            sums_ref[at : at + 1, :] = sums[:, k * LANES : (k + 1) * LANES]


def other_core_kernel(stud, glob, own_ref, unit_ref, exp_ref):
    chips, _, half = own_ref.shape
    at = 2 * stud
    block = own_ref[...].astype(f32)[:, at : at + 2 * glob]
    teach = wide(block[:, :glob], block[:, glob:]).reshape(chips * glob, 2 * half).astype(bf16)
    step = 512
    for start in range(0, unit_ref.shape[0], step):
        here = slice(start, start + step)
        exp_ref[:, here] = jnp.exp2(nt_dot(teach, unit_ref[here, :]) * TEACHER_EXP2).astype(bf16)


def add_students(stud, own_ref, unit_ref, stud_ref, acc_ref, tot_ref, start_acc, start_tot):
    chips, _, half = own_ref.shape
    block = own_ref[...].astype(f32)[:, : 2 * stud]
    block = wide(block[:, :stud], block[:, stud:])
    stud_ref[...] = block.reshape(chips * stud, 2 * half).astype(bf16)
    step = 512
    for start in range(0, unit_ref.shape[0], step):
        protos = unit_ref[start : start + step, :]
        weights = jnp.exp2(nt_dot(stud_ref[...], protos) * STUDENT_EXP2)
        part = weights[:, :LANES]
        for k in range(1, step // LANES):
            part = part + weights[:, k * LANES : (k + 1) * LANES]
        term = jnp.dot(weights.astype(bf16), protos, preferred_element_type=f32)
        if start == 0 and start_acc is None:
            tot_ref[...] = part
            acc_ref[...] = term
        elif start == 0:
            tot_ref[...] = start_tot[...] + part
            acc_ref[...] = start_acc[...] + term
        else:
            tot_ref[...] += part
            acc_ref[...] += term


def student_own_kernel(stud, own_ref, unit_ref, acc_ref, tot_ref, stud_ref):
    add_students(stud, own_ref, unit_ref, stud_ref, acc_ref, tot_ref, None, None)


def student_other_kernel(
    stud, own_ref, unit_ref, start_acc, start_tot, attract_ref, total_ref, stud_ref, acc_ref, tot_ref
):
    add_students(stud, own_ref, unit_ref, stud_ref, acc_ref, tot_ref, start_acc, start_tot)
    chips = own_ref.shape[0]
    attract = acc_ref[...].reshape(chips, stud, 2 * LANES)
    attract = jnp.concatenate([attract[:, :, :LANES], attract[:, :, LANES:]], axis=1)
    attract_ref[...] = attract.astype(bf16)
    total = jnp.sum(tot_ref[...], axis=1, keepdims=True).reshape(chips, stud, 1)
    eye = iota((chips, stud, LANES), 1) == iota((chips, stud, LANES), 2)
    total_ref[...] = jnp.sum(
        jnp.where(eye, jnp.broadcast_to(total, (chips, stud, LANES)), 0.0), axis=1, keepdims=True
    )


def pair_kernel(mine_ref, got_ref, out_ref):
    total = (mine_ref[...] + got_ref[...]).astype(bf16)
    for j in range(out_ref.shape[0]):
        out_ref[j] = total


def proto_scale_of(parts_ref):
    total = parts_ref[0].astype(f32)
    for j in range(1, parts_ref.shape[0]):
        total = total + parts_ref[j].astype(f32)
    scale = 1.0 / total
    return jnp.concatenate([scale[k : k + 1, :] for k in range(scale.shape[0])], axis=1)


def col_kernel(parts_ref, exp_ref, out_ref):
    scale = proto_scale_of(parts_ref)
    rows, cols = exp_ref.shape
    lines = []
    for g in range(rows // LANES):
        acc = None
        for k in range(cols // LANES):
            lanes = slice(k * LANES, (k + 1) * LANES)
            term = exp_ref[g * LANES : (g + 1) * LANES, lanes].astype(f32) * scale[:, lanes]
            acc = term if acc is None else acc + term
        lines.append(jnp.sum(acc.T, axis=0, keepdims=True))
    out = jnp.concatenate(lines, axis=1)
    for j in range(out_ref.shape[0]):
        out_ref[j] = out


def row_kernel(parts_ref, exp_ref, out_ref, line_ref):
    rows, cols = exp_ref.shape
    scale = 1.0 / jnp.sum(parts_ref[...], axis=0)
    acc = None
    for g in range(rows // LANES):
        tall = jnp.broadcast_to(scale[:, g * LANES : (g + 1) * LANES], (LANES, LANES)).T
        for t in range(0, LANES, 16):
            scales = jnp.concatenate([tall[t : t + 16]] * (cols // LANES), axis=1)
            term = exp_ref[g * LANES + t : g * LANES + t + 16, :].astype(f32) * scales
            term = term[:8] + term[8:]
            acc = term if acc is None else acc + term
    line = jnp.sum(acc, axis=0, keepdims=True)
    for k in range(cols // LANES):
        line_ref[k : k + 1, :] = line[:, k * LANES : (k + 1) * LANES]
    sums = line_ref[...].astype(bf16)
    for j in range(out_ref.shape[0]):
        out_ref[j] = sums


def add_repel(parts_ref, exps_of, unit_ref, repel, mass):
    scale = proto_scale_of(parts_ref)
    step = 512
    for start in range(0, unit_ref.shape[0], step):
        here = slice(start, start + step)
        terms = exps_of(here).astype(f32) * scale[:, here]
        for k in range(step // LANES):
            mass = mass + terms[:, k * LANES : (k + 1) * LANES]
        repel = repel + jnp.dot(terms.astype(bf16), unit_ref[here, :], preferred_element_type=f32)
    return repel, mass


def repel_own_kernel(core_ref, parts_ref, exp_ref, unit_ref, repel_ref, mass_ref):
    rows = repel_ref.shape[0]
    mine = pl.ds(pl.multiple_of(core_ref[0] * rows, rows), rows)
    repel_ref[...], mass_ref[...] = add_repel(
        parts_ref,
        lambda here: exp_ref[mine, here],
        unit_ref,
        jnp.zeros(repel_ref.shape, f32),
        jnp.zeros(mass_ref.shape, f32),
    )


def repel_other_kernel(
    stud, parts_ref, exp_ref, unit_ref, repel_ref, mass_ref, attract_ref, total_ref, out_ref
):
    repel, mass = add_repel(
        parts_ref, lambda here: exp_ref[:, here], unit_ref, repel_ref[...], mass_ref[...]
    )
    chips = attract_ref.shape[0]
    glob = repel.shape[0] // chips
    repel = repel.reshape(chips, glob, 2 * LANES)
    dims = (chips, glob, LANES)
    place = iota(dims, 1) + stud == iota(dims, 2)
    mass = jnp.sum(mass, axis=1, keepdims=True).reshape(chips, glob, 1)
    mass = jnp.where(place, jnp.broadcast_to(mass, dims), 0.0)
    scalars = total_ref[...] + jnp.sum(mass, axis=1, keepdims=True)
    high = scalars.astype(bf16).astype(f32)
    scalars = jnp.where(iota(dims, 1) == 0, high, scalars - high)
    parts = [attract_ref[...].astype(f32), repel[:, :, :LANES], repel[:, :, LANES:], scalars]
    out_ref[...] = jnp.concatenate(parts, axis=1).astype(bf16)


def final_kernel(back_ref, student_ref, grad_ref, loss_ref, rows_ref):
    crops, images, width = student_ref.shape
    stud = crops * images
    for c in range(crops):
        rows_ref[c * images : (c + 1) * images, :] = student_ref[c].astype(f32)
    values = rows_ref[...]
    back = jnp.sum(back_ref[...].astype(f32), axis=0)
    attract = wide(back[:stud], back[stud : 2 * stud])
    back = back[2 * stud :]
    line = back[16:17] + back[17:18]
    sub, lane = iota((stud, LANES), 0), iota((stud, LANES), 1)
    lines = jnp.broadcast_to(line, (stud, LANES))
    total = jnp.sum(jnp.where(lane == sub, lines, 0.0), axis=1, keepdims=True)
    mass = jnp.sum(jnp.where(lane == sub + stud, lines, 0.0)[:8], axis=1, keepdims=True)
    views = wide(back[:8], back[8:16]) / mass
    both = views + jnp.concatenate([views[images:], views[:images]], axis=0)
    repel = jnp.concatenate([views] + [both] * (stud // 8 - 1), axis=0)
    pairs = jnp.where(iota((stud, 1), 0) < 2 * images, 1.0, 2.0)
    inv_norm = lax.rsqrt(jnp.sum(values * values, axis=1, keepdims=True) + NORM_EPSILON)
    own = values * inv_norm
    low = own.astype(bf16).astype(f32)
    grad_unit = (pairs * attract / total - repel) / STUDENT_SOFTNESS
    cross = jnp.sum(low * repel, axis=1, keepdims=True) / STUDENT_SOFTNESS
    loss = pairs * jnp.log(total) - cross
    inner = jnp.sum(own * grad_unit, axis=1, keepdims=True)
    grad = inv_norm * (grad_unit - own * inner)
    for c in range(crops):
        grad_ref[c] = grad[c * images : (c + 1) * images]
    spreads = jnp.broadcast_to(loss, (stud, LANES))
    for i in range(images):
        spread = jnp.where(sub == lane * images + i, spreads, 0.0)
        loss_ref[i : i + 1, :] = jnp.sum(spread, axis=0, keepdims=True)[:, :crops]


def exchange(array, axis, **kw):
    return lax.all_to_all(array, axis, 0, 0, tiled=True, **kw)


def body(teacher_global, queue, student, prototypes):
    images, crops, width = student.shape
    queue_rows = queue.shape[0]
    groups, parts = lax.axis_size("proto"), lax.axis_size("dp")
    chips = groups // 2
    stud, glob = images * crops, images * 2
    teach_rows = groups * (glob + queue_rows)
    protos = prototypes.shape[0]
    student = jnp.transpose(student, (1, 0, 2))
    core = jnp.reshape(lax.axis_index("proto") & 1, (1,))
    core, student = lax.optimization_barrier((core, student))
    scalar = pl.BlockSpec(memory_space=pltpu.SMEM)
    vmem = pl.BlockSpec(memory_space=pltpu.VMEM)

    def swap(array):
        return lax.ppermute(array, "proto", [(j, j ^ 1) for j in range(groups)])

    send_rows = 2 * (stud + glob + queue_rows)
    packed = call(
        pack_kernel,
        "pack_rows",
        shape((chips, send_rows, LANES), bf16),
        scratch_shapes=[pltpu.VMEM((send_rows, LANES), f32)],
    )(*map(in_hbm, (student, teacher_global, queue)))
    same_core = [list(range(c, groups, 2)) for c in range(2)]
    own_rows = exchange(packed, "proto", axis_index_groups=same_core)
    other_rows = swap(own_rows)
    own_rows, prototypes = lax.optimization_barrier((own_rows, prototypes))
    unit_protos = call(
        unit_kernel,
        "unit_prototypes",
        shape((protos, width), bf16),
        in_specs=[pl.BlockSpec(memory_space=pl.ANY)],
        scratch_shapes=[pltpu.VMEM((protos, width), bf16), pltpu.SemaphoreType.DMA((8,))],
        flops=3 * protos * width,
        nbytes=4 * protos * width,
    )(in_hbm(prototypes))

    other_rows, unit_protos = lax.optimization_barrier((other_rows, unit_protos))
    other_protos = swap(unit_protos)
    exps, row_parts = call(
        functools.partial(teacher_kernel, stud, glob),
        "teacher_exponentials",
        [pltpu.VMEM((teach_rows, protos), bf16), shape((protos // LANES, LANES), f32)],
        in_specs=[scalar, vmem, vmem, vmem],
        flops=2 * teach_rows * protos * width,
        nbytes=2 * teach_rows * protos,
        exps=teach_rows * protos,
    )(core, own_rows, other_rows, unit_protos)
    exps = in_vmem(exps)

    row_parts, own_rows = lax.optimization_barrier((row_parts, own_rows))
    half = parts // 2
    got_sums = lax.ppermute(row_parts, "dp", [(j, (j + half) % parts) for j in range(parts)])
    own_students = chips * stud
    work = dict(
        flops=4 * own_students * protos * width,
        nbytes=2 * protos * width,
        exps=own_students * protos,
    )
    rows_scratch = pltpu.VMEM((own_students, width), bf16)
    acc, tot = call(
        functools.partial(student_own_kernel, stud),
        "students_own_core",
        [shape((own_students, width), f32), shape((own_students, LANES), f32)],
        scratch_shapes=[rows_scratch],
        **work,
    )(own_rows, unit_protos)
    attract, total = call(
        functools.partial(student_other_kernel, stud),
        "students_other_core",
        [shape((chips, 2 * stud, LANES), bf16), shape((chips, 1, LANES), f32)],
        scratch_shapes=[
            rows_scratch,
            pltpu.VMEM((own_students, width), f32),
            pltpu.VMEM((own_students, LANES), f32),
        ],
        **work,
    )(own_rows, other_protos, acc, tot)
    got_sums, attract, total = lax.optimization_barrier((got_sums, attract, total))
    row_parts = call(pair_kernel, "add_halves", shape((half, protos // LANES, LANES), bf16))(row_parts, got_sums)
    halves = [list(range(half)), list(range(half, parts))]
    row_parts = exchange(row_parts, "dp", axis_index_groups=halves)

    for iteration in range(SINK_ITERS - 1):
        col_parts = call(
            col_kernel,
            "sum_over_prototypes",
            shape((groups, 1, teach_rows), f32),
            flops=2 * teach_rows * protos,
            nbytes=2 * teach_rows * protos,
        )(row_parts, exps)
        col_parts = exchange(col_parts, "proto")
        row_parts = call(
            row_kernel,
            "sum_over_rows",
            shape((parts, protos // LANES, LANES), bf16),
            scratch_shapes=[pltpu.VMEM((protos // LANES, LANES), f32)],
            flops=2 * teach_rows * protos,
            nbytes=2 * teach_rows * protos,
        )(col_parts, exps)
        row_parts = exchange(row_parts, "dp")

    row_parts, own_rows = lax.optimization_barrier((row_parts, own_rows))
    other_parts = swap(row_parts)
    own_glob = chips * glob
    other_exps = call(
        functools.partial(other_core_kernel, stud, glob),
        "teacher_other_core",
        pltpu.VMEM((own_glob, protos), bf16),
        flops=2 * own_glob * protos * width,
        nbytes=2 * protos * width,
        exps=own_glob * protos,
    )(own_rows, other_protos)
    other_exps = in_vmem(other_exps)
    work = dict(flops=2 * own_glob * protos * width, nbytes=4 * protos * width)
    repel, mass = call(
        repel_own_kernel,
        "repel_own_core",
        [shape((own_glob, width), f32), shape((own_glob, LANES), f32)],
        in_specs=[scalar] + [vmem] * 3,
        **work,
    )(core, row_parts, exps, unit_protos)
    back = call(
        functools.partial(repel_other_kernel, stud),
        "repel_other_core",
        shape((chips, 2 * stud + 2 * glob + 8, LANES), bf16),
        **work,
    )(other_parts, other_exps, other_protos, repel, mass, attract, total)
    back = exchange(back, "proto", axis_index_groups=same_core)

    grad, loss = call(
        final_kernel,
        "gradients",
        [shape((crops, images, width), f32), shape((images, crops), f32)],
        scratch_shapes=[pltpu.VMEM((stud, width), f32)],
    )(back, student)
    return jnp.transpose(grad, (1, 0, 2)), loss


def solution(mesh):
    in_specs = (
        P(("dp", "proto"), None, None),
        P(("dp", "proto"), None),
        P(("dp", "proto"), None, None),
        P("proto", None),
    )
    out_specs = (P(("dp", "proto"), None, None), P(("dp", "proto"), None))
    return jax.shard_map(body, mesh=mesh, in_specs=in_specs, out_specs=out_specs, check_vma=False)
```

```python
import functools
import math

import jax
import jax.numpy as jnp
from jax import lax
from jax.experimental import pallas as pl
from jax.experimental.pallas import tpu as pltpu
from jax.sharding import PartitionSpec as P

SINK_ITERS = 3
TEACHER_SOFTNESS = 0.07
STUDENT_SOFTNESS = 0.1
NORM_EPSILON = 1e-06
TEACHER_EXP2 = math.log2(math.e) / TEACHER_SOFTNESS
STUDENT_EXP2 = math.log2(math.e) / STUDENT_SOFTNESS

LANES = 128
MIB = 1024 * 1024

f32 = jnp.float32
bf16 = jnp.bfloat16
shape = jax.ShapeDtypeStruct


def iota(shape, dim):
    return lax.broadcasted_iota(jnp.int32, shape, dim)


def unit(values):
    return values * lax.rsqrt(jnp.sum(values * values, axis=-1, keepdims=True) + NORM_EPSILON)


def nt_dot(a, b):
    return lax.dot_general(a, b, (((1,), (1,)), ((), ())), preferred_element_type=f32)


def call(kernel, name, out_shape, flops=0, nbytes=0, exps=0, vmem=16, **kw):
    return pl.pallas_call(
        kernel,
        out_shape=out_shape,
        compiler_params=pltpu.CompilerParams(vmem_limit_bytes=vmem * MIB),
        cost_estimate=pl.CostEstimate(flops=flops, bytes_accessed=nbytes, transcendentals=exps),
        name=name,
        **kw,
    )


def in_vmem(array):
    return pltpu.with_memory_space_constraint(array, pltpu.VMEM)


def in_hbm(array):
    return pltpu.with_memory_space_constraint(array, pltpu.HBM)


def pack_kernel(student_ref, teacher_ref, queue_ref, out_ref, rows_ref):
    crops, images, width = student_ref.shape
    stud, glob = crops * images, 2 * images
    half = width // 2

    def put(at, rows, height, values):
        rows_ref[at + rows : at + rows + values.shape[0], :] = values[:, :half]
        rows_ref[at + height + rows : at + height + rows + values.shape[0], :] = values[:, half:]

    for c in range(crops):
        put(0, c * images, stud, unit(student_ref[c].astype(f32)))
    at = 2 * stud
    for i in range(images):
        views = unit(teacher_ref[i].astype(f32))
        put(at, i, glob, views[1:2])
        put(at, images + i, glob, views[0:1])
    units = unit(queue_ref[...].astype(f32))
    at = at + 2 * glob
    put(at, 0, 8, units[:8])
    put(at + 16, 0, 4, units[8:])
    packed = rows_ref[...].astype(bf16)
    for j in range(out_ref.shape[0]):
        out_ref[j] = packed


def wide(low, high):
    return jnp.concatenate([low, high], axis=-1)


def unit_kernel(protos_ref, out_ref, raw_ref, sems):
    parts = sems.shape[0]
    rows = raw_ref.shape[0] // parts
    copies = []
    for j in range(parts):
        here = pl.ds(j * rows, rows)
        copies.append(pltpu.make_async_copy(protos_ref.at[here], raw_ref.at[here], sems.at[j]))
        copies[j].start()
    for j in range(parts):
        copies[j].wait()
        here = slice(j * rows, (j + 1) * rows)
        out_ref[here, :] = unit(raw_ref[here, :].astype(f32)).astype(bf16)


def by_core(core_ref, own, other):
    is_first = core_ref[0] == 0
    return jnp.where(is_first, own, other), jnp.where(is_first, other, own)


def teacher_kernel(stud, glob, core_ref, own_ref, other_ref, unit_ref, exp_ref, sums_ref, line_ref):
    chips, _, half = own_ref.shape
    width = 2 * half
    at = 2 * stud
    blocks = by_core(core_ref, own_ref[...].astype(f32)[:, at:], other_ref[...].astype(f32)[:, at:])
    block = jnp.concatenate(blocks, axis=0)
    groups = 2 * chips
    at = 2 * glob
    g = wide(block[:, :glob], block[:, glob:at]).reshape(groups * glob, width)
    q = wide(block[:, at : at + 8], block[:, at + 8 : at + 16]).reshape(groups * 8, width)
    r = block[:, at + 16 :].reshape(chips, 2, 8, half)
    turned = jnp.concatenate([r[:, :, 4:], r[:, :, :4]], axis=2)
    top = iota((chips, 8, half), 1) < 4
    r = wide(jnp.where(top, r[:, 0], turned[:, 1]), jnp.where(top, turned[:, 0], r[:, 1]))
    r = r.reshape(groups * 4, width)
    teach = jnp.concatenate([g, q, r], axis=0).astype(bf16)
    step = 256
    for start in range(0, unit_ref.shape[0], step):
        here = slice(start, start + step)
        exps = jnp.exp2(nt_dot(teach, unit_ref[here, :]) * TEACHER_EXP2)
        exp_ref[:, here] = exps.astype(bf16)
        sums = jnp.sum(exps, axis=0, keepdims=True)
        for k in range(step // LANES):
            at = start // LANES + k
            line_ref[at : at + 1, :] = sums[:, k * LANES : (k + 1) * LANES]
    sums = line_ref[...].astype(bf16)
    for j in range(sums_ref.shape[0]):
        sums_ref[j] = sums


def other_core_kernel(stud, glob, own_ref, unit_ref, exp_ref):
    chips, _, half = own_ref.shape
    at = 2 * stud
    block = own_ref[...].astype(f32)[:, at : at + 2 * glob]
    teach = wide(block[:, :glob], block[:, glob:]).reshape(chips * glob, 2 * half).astype(bf16)
    step = 512
    for start in range(0, unit_ref.shape[0], step):
        here = slice(start, start + step)
        exp_ref[:, here] = jnp.exp2(nt_dot(teach, unit_ref[here, :]) * TEACHER_EXP2).astype(bf16)


def add_students(stud, own_ref, unit_ref, stud_ref, acc_ref, tot_ref, start_acc, start_tot):
    chips, _, half = own_ref.shape
    block = own_ref[...].astype(f32)[:, : 2 * stud]
    block = wide(block[:, :stud], block[:, stud:])
    stud_ref[...] = block.reshape(chips * stud, 2 * half).astype(bf16)
    step = 512
    for start in range(0, unit_ref.shape[0], step):
        protos = unit_ref[start : start + step, :]
        weights = jnp.exp2(nt_dot(stud_ref[...], protos) * STUDENT_EXP2)
        part = weights[:, :LANES]
        for k in range(1, step // LANES):
            part = part + weights[:, k * LANES : (k + 1) * LANES]
        term = jnp.dot(weights.astype(bf16), protos, preferred_element_type=f32)
        if start == 0 and start_acc is None:
            tot_ref[...] = part
            acc_ref[...] = term
        elif start == 0:
            tot_ref[...] = start_tot[...] + part
            acc_ref[...] = start_acc[...] + term
        else:
            tot_ref[...] += part
            acc_ref[...] += term


def student_own_kernel(stud, own_ref, unit_ref, acc_ref, tot_ref, stud_ref):
    add_students(stud, own_ref, unit_ref, stud_ref, acc_ref, tot_ref, None, None)


def student_other_kernel(
    stud, own_ref, unit_ref, start_acc, start_tot, attract_ref, total_ref, stud_ref, acc_ref, tot_ref
):
    add_students(stud, own_ref, unit_ref, stud_ref, acc_ref, tot_ref, start_acc, start_tot)
    chips = own_ref.shape[0]
    attract = acc_ref[...].reshape(chips, stud, 2 * LANES)
    attract = jnp.concatenate([attract[:, :, :LANES], attract[:, :, LANES:]], axis=1)
    attract_ref[...] = attract.astype(bf16)
    total = jnp.sum(tot_ref[...], axis=1, keepdims=True).reshape(chips, stud, 1)
    eye = iota((chips, stud, LANES), 1) == iota((chips, stud, LANES), 2)
    total_ref[...] = jnp.sum(
        jnp.where(eye, jnp.broadcast_to(total, (chips, stud, LANES)), 0.0), axis=1, keepdims=True
    )


def proto_scale_of(*parts_refs):
    parts = [ref[j].astype(f32) for ref in parts_refs for j in range(ref.shape[0])]
    total = sum(parts[1:], parts[0])
    scale = 1.0 / total
    return jnp.concatenate([scale[k : k + 1, :] for k in range(scale.shape[0])], axis=1)


def col_kernel(*refs):
    *parts_refs, exp_ref, out_ref = refs
    scale = proto_scale_of(*parts_refs)
    rows, cols = exp_ref.shape
    lines = []
    for g in range(rows // LANES):
        acc = None
        for k in range(cols // LANES):
            lanes = slice(k * LANES, (k + 1) * LANES)
            term = exp_ref[g * LANES : (g + 1) * LANES, lanes].astype(f32) * scale[:, lanes]
            acc = term if acc is None else acc + term
        lines.append(jnp.sum(acc.T, axis=0, keepdims=True))
    out = jnp.concatenate(lines, axis=1)
    for j in range(out_ref.shape[0]):
        out_ref[j] = out


def row_kernel(parts_ref, exp_ref, out_ref, line_ref):
    rows, cols = exp_ref.shape
    scale = 1.0 / jnp.sum(parts_ref[...], axis=0)
    acc = None
    for g in range(rows // LANES):
        tall = jnp.broadcast_to(scale[:, g * LANES : (g + 1) * LANES], (LANES, LANES)).T
        for t in range(0, LANES, 16):
            scales = jnp.concatenate([tall[t : t + 16]] * (cols // LANES), axis=1)
            term = exp_ref[g * LANES + t : g * LANES + t + 16, :].astype(f32) * scales
            term = term[:8] + term[8:]
            acc = term if acc is None else acc + term
    line = jnp.sum(acc, axis=0, keepdims=True)
    for k in range(cols // LANES):
        line_ref[k : k + 1, :] = line[:, k * LANES : (k + 1) * LANES]
    sums = line_ref[...].astype(bf16)
    for j in range(out_ref.shape[0]):
        out_ref[j] = sums


def add_repel(parts_ref, exps_of, unit_ref, repel, mass):
    scale = proto_scale_of(parts_ref)
    step = 512
    for start in range(0, unit_ref.shape[0], step):
        here = slice(start, start + step)
        terms = exps_of(here).astype(f32) * scale[:, here]
        for k in range(step // LANES):
            mass = mass + terms[:, k * LANES : (k + 1) * LANES]
        repel = repel + jnp.dot(terms.astype(bf16), unit_ref[here, :], preferred_element_type=f32)
    return repel, mass


def repel_own_kernel(core_ref, parts_ref, exp_ref, unit_ref, repel_ref, mass_ref):
    rows = repel_ref.shape[0]
    mine = pl.ds(pl.multiple_of(core_ref[0] * rows, rows), rows)
    repel_ref[...], mass_ref[...] = add_repel(
        parts_ref,
        lambda here: exp_ref[mine, here],
        unit_ref,
        jnp.zeros(repel_ref.shape, f32),
        jnp.zeros(mass_ref.shape, f32),
    )


def repel_other_kernel(
    stud, parts_ref, exp_ref, unit_ref, repel_ref, mass_ref, attract_ref, total_ref, out_ref
):
    repel, mass = add_repel(
        parts_ref, lambda here: exp_ref[:, here], unit_ref, repel_ref[...], mass_ref[...]
    )
    chips = attract_ref.shape[0]
    glob = repel.shape[0] // chips
    repel = repel.reshape(chips, glob, 2 * LANES)
    dims = (chips, glob, LANES)
    place = iota(dims, 1) + stud == iota(dims, 2)
    mass = jnp.sum(mass, axis=1, keepdims=True).reshape(chips, glob, 1)
    mass = jnp.where(place, jnp.broadcast_to(mass, dims), 0.0)
    scalars = total_ref[...] + jnp.sum(mass, axis=1, keepdims=True)
    high = scalars.astype(bf16).astype(f32)
    scalars = jnp.where(iota(dims, 1) == 0, high, scalars - high)
    parts = [attract_ref[...].astype(f32), repel[:, :, :LANES], repel[:, :, LANES:], scalars]
    out_ref[...] = jnp.concatenate(parts, axis=1).astype(bf16)


def final_kernel(back_ref, student_ref, grad_ref, loss_ref, rows_ref):
    crops, images, width = student_ref.shape
    stud = crops * images
    for c in range(crops):
        rows_ref[c * images : (c + 1) * images, :] = student_ref[c].astype(f32)
    values = rows_ref[...]
    back = jnp.sum(back_ref[...].astype(f32), axis=0)
    attract = wide(back[:stud], back[stud : 2 * stud])
    back = back[2 * stud :]
    line = back[16:17] + back[17:18]
    sub, lane = iota((stud, LANES), 0), iota((stud, LANES), 1)
    lines = jnp.broadcast_to(line, (stud, LANES))
    total = jnp.sum(jnp.where(lane == sub, lines, 0.0), axis=1, keepdims=True)
    mass = jnp.sum(jnp.where(lane == sub + stud, lines, 0.0)[:8], axis=1, keepdims=True)
    views = wide(back[:8], back[8:16]) / mass
    both = views + jnp.concatenate([views[images:], views[:images]], axis=0)
    repel = jnp.concatenate([views] + [both] * (stud // 8 - 1), axis=0)
    pairs = jnp.where(iota((stud, 1), 0) < 2 * images, 1.0, 2.0)
    inv_norm = lax.rsqrt(jnp.sum(values * values, axis=1, keepdims=True) + NORM_EPSILON)
    own = values * inv_norm
    low = own.astype(bf16).astype(f32)
    grad_unit = (pairs * attract / total - repel) / STUDENT_SOFTNESS
    cross = jnp.sum(low * repel, axis=1, keepdims=True) / STUDENT_SOFTNESS
    loss = pairs * jnp.log(total) - cross
    inner = jnp.sum(own * grad_unit, axis=1, keepdims=True)
    grad = inv_norm * (grad_unit - own * inner)
    for c in range(crops):
        grad_ref[c] = grad[c * images : (c + 1) * images]
    spreads = jnp.broadcast_to(loss, (stud, LANES))
    for i in range(images):
        spread = jnp.where(sub == lane * images + i, spreads, 0.0)
        loss_ref[i : i + 1, :] = jnp.sum(spread, axis=0, keepdims=True)[:, :crops]


def exchange(array, axis, **kw):
    return lax.all_to_all(array, axis, 0, 0, tiled=True, **kw)


def body(teacher_global, queue, student, prototypes):
    images, crops, width = student.shape
    queue_rows = queue.shape[0]
    groups, parts = lax.axis_size("proto"), lax.axis_size("dp")
    chips = groups // 2
    stud, glob = images * crops, images * 2
    teach_rows = groups * (glob + queue_rows)
    protos = prototypes.shape[0]
    student = jnp.transpose(student, (1, 0, 2))
    core = jnp.reshape(lax.axis_index("proto") & 1, (1,))
    core, student = lax.optimization_barrier((core, student))
    scalar = pl.BlockSpec(memory_space=pltpu.SMEM)
    vmem = pl.BlockSpec(memory_space=pltpu.VMEM)

    def swap(array):
        return lax.ppermute(array, "proto", [(j, j ^ 1) for j in range(groups)])

    send_rows = 2 * (stud + glob + queue_rows)
    packed = call(
        pack_kernel,
        "pack_rows",
        shape((chips, send_rows, LANES), bf16),
        scratch_shapes=[pltpu.VMEM((send_rows, LANES), f32)],
    )(*map(in_hbm, (student, teacher_global, queue)))
    same_core = [list(range(c, groups, 2)) for c in range(2)]
    own_rows = exchange(packed, "proto", axis_index_groups=same_core)
    other_rows = swap(own_rows)
    own_rows, prototypes = lax.optimization_barrier((own_rows, prototypes))
    unit_protos = call(
        unit_kernel,
        "unit_prototypes",
        shape((protos, width), bf16),
        in_specs=[pl.BlockSpec(memory_space=pl.ANY)],
        scratch_shapes=[pltpu.VMEM((protos, width), bf16), pltpu.SemaphoreType.DMA((8,))],
        flops=3 * protos * width,
        nbytes=4 * protos * width,
    )(in_hbm(prototypes))

    other_rows, unit_protos = lax.optimization_barrier((other_rows, unit_protos))
    other_protos = swap(unit_protos)
    half = parts // 2
    exps, row_parts = call(
        functools.partial(teacher_kernel, stud, glob),
        "teacher_exponentials",
        [pltpu.VMEM((teach_rows, protos), bf16), shape((half, protos // LANES, LANES), bf16)],
        in_specs=[scalar, vmem, vmem, vmem],
        scratch_shapes=[pltpu.VMEM((protos // LANES, LANES), f32)],
        flops=2 * teach_rows * protos * width,
        nbytes=2 * teach_rows * protos,
        exps=teach_rows * protos,
    )(core, own_rows, other_rows, unit_protos)
    exps = in_vmem(exps)

    halves = [list(range(half)), list(range(half, parts))]
    row_parts = exchange(row_parts, "dp", axis_index_groups=halves)
    row_parts, own_rows = lax.optimization_barrier((row_parts, own_rows))
    got_sums = lax.ppermute(row_parts, "dp", [(j, (j + half) % parts) for j in range(parts)])
    own_students = chips * stud
    work = dict(
        flops=4 * own_students * protos * width,
        nbytes=2 * protos * width,
        exps=own_students * protos,
    )
    rows_scratch = pltpu.VMEM((own_students, width), bf16)
    acc, tot = call(
        functools.partial(student_own_kernel, stud),
        "students_own_core",
        [shape((own_students, width), f32), shape((own_students, LANES), f32)],
        scratch_shapes=[rows_scratch],
        **work,
    )(own_rows, unit_protos)
    attract, total = call(
        functools.partial(student_other_kernel, stud),
        "students_other_core",
        [shape((chips, 2 * stud, LANES), bf16), shape((chips, 1, LANES), f32)],
        scratch_shapes=[
            rows_scratch,
            pltpu.VMEM((own_students, width), f32),
            pltpu.VMEM((own_students, LANES), f32),
        ],
        **work,
    )(own_rows, other_protos, acc, tot)
    got_sums, attract, total = lax.optimization_barrier((got_sums, attract, total))
    row_parts = (row_parts, got_sums)

    for iteration in range(SINK_ITERS - 1):
        col_parts = call(
            col_kernel,
            "sum_over_prototypes",
            shape((groups, 1, teach_rows), f32),
            flops=2 * teach_rows * protos,
            nbytes=2 * teach_rows * protos,
        )(*row_parts, exps)
        col_parts = exchange(col_parts, "proto")
        row_parts = call(
            row_kernel,
            "sum_over_rows",
            shape((parts, protos // LANES, LANES), bf16),
            scratch_shapes=[pltpu.VMEM((protos // LANES, LANES), f32)],
            flops=2 * teach_rows * protos,
            nbytes=2 * teach_rows * protos,
        )(col_parts, exps)
        row_parts = (exchange(row_parts, "dp"),)

    (row_parts,) = row_parts
    row_parts, own_rows = lax.optimization_barrier((row_parts, own_rows))
    other_parts = swap(row_parts)
    own_glob = chips * glob
    other_exps = call(
        functools.partial(other_core_kernel, stud, glob),
        "teacher_other_core",
        pltpu.VMEM((own_glob, protos), bf16),
        flops=2 * own_glob * protos * width,
        nbytes=2 * protos * width,
        exps=own_glob * protos,
    )(own_rows, other_protos)
    other_exps = in_vmem(other_exps)
    work = dict(flops=2 * own_glob * protos * width, nbytes=4 * protos * width)
    repel, mass = call(
        repel_own_kernel,
        "repel_own_core",
        [shape((own_glob, width), f32), shape((own_glob, LANES), f32)],
        in_specs=[scalar] + [vmem] * 3,
        **work,
    )(core, row_parts, exps, unit_protos)
    back = call(
        functools.partial(repel_other_kernel, stud),
        "repel_other_core",
        shape((chips, 2 * stud + 2 * glob + 8, LANES), bf16),
        **work,
    )(other_parts, other_exps, other_protos, repel, mass, attract, total)
    back = exchange(back, "proto", axis_index_groups=same_core)

    grad, loss = call(
        final_kernel,
        "gradients",
        [shape((crops, images, width), f32), shape((images, crops), f32)],
        scratch_shapes=[pltpu.VMEM((stud, width), f32)],
    )(back, student)
    return jnp.transpose(grad, (1, 0, 2)), loss


def solution(mesh):
    in_specs = (
        P(("dp", "proto"), None, None),
        P(("dp", "proto"), None),
        P(("dp", "proto"), None, None),
        P("proto", None),
    )
    out_specs = (P(("dp", "proto"), None, None), P(("dp", "proto"), None))
    return jax.shard_map(body, mesh=mesh, in_specs=in_specs, out_specs=out_specs, check_vma=False)
```

```python
import functools
import math

import jax
import jax.numpy as jnp
from jax import lax
from jax.experimental import pallas as pl
from jax.experimental.pallas import tpu as pltpu
from jax.sharding import PartitionSpec as P

SINK_ITERS = 3
TEACHER_SOFTNESS = 0.07
STUDENT_SOFTNESS = 0.1
NORM_EPSILON = 1e-06
TEACHER_EXP2 = math.log2(math.e) / TEACHER_SOFTNESS
STUDENT_EXP2 = math.log2(math.e) / STUDENT_SOFTNESS

LANES = 128
MIB = 1024 * 1024

f32 = jnp.float32
bf16 = jnp.bfloat16
shape = jax.ShapeDtypeStruct


def iota(shape, dim):
    return lax.broadcasted_iota(jnp.int32, shape, dim)


def unit(values):
    return values * lax.rsqrt(jnp.sum(values * values, axis=-1, keepdims=True) + NORM_EPSILON)


def nt_dot(a, b):
    return lax.dot_general(a, b, (((1,), (1,)), ((), ())), preferred_element_type=f32)


def call(kernel, name, out_shape, flops=0, nbytes=0, exps=0, vmem=16, **kw):
    return pl.pallas_call(
        kernel,
        out_shape=out_shape,
        compiler_params=pltpu.CompilerParams(vmem_limit_bytes=vmem * MIB),
        cost_estimate=pl.CostEstimate(flops=flops, bytes_accessed=nbytes, transcendentals=exps),
        name=name,
        **kw,
    )


def in_vmem(array):
    return pltpu.with_memory_space_constraint(array, pltpu.VMEM)


def in_hbm(array):
    return pltpu.with_memory_space_constraint(array, pltpu.HBM)


def pack_kernel(student_ref, teacher_ref, queue_ref, out_ref, rows_ref):
    crops, images, width = student_ref.shape
    stud, glob = crops * images, 2 * images
    half = width // 2

    def put(at, rows, height, values):
        rows_ref[at + rows : at + rows + values.shape[0], :] = values[:, :half]
        rows_ref[at + height + rows : at + height + rows + values.shape[0], :] = values[:, half:]

    for c in range(crops):
        put(0, c * images, stud, unit(student_ref[c].astype(f32)))
    at = 2 * stud
    for i in range(images):
        views = unit(teacher_ref[i].astype(f32))
        put(at, i, glob, views[1:2])
        put(at, images + i, glob, views[0:1])
    units = unit(queue_ref[...].astype(f32))
    at = at + 2 * glob
    put(at, 0, 8, units[:8])
    put(at + 16, 0, 4, units[8:])
    packed = rows_ref[...].astype(bf16)
    for j in range(out_ref.shape[0]):
        out_ref[j] = packed


def wide(low, high):
    return jnp.concatenate([low, high], axis=-1)


def unit_kernel(protos_ref, out_ref, raw_ref, sems):
    parts = sems.shape[0]
    rows = raw_ref.shape[0] // parts
    copies = []
    for j in range(parts):
        here = pl.ds(j * rows, rows)
        copies.append(pltpu.make_async_copy(protos_ref.at[here], raw_ref.at[here], sems.at[j]))
    for copy in copies[:3]:
        copy.start()
    for j in range(parts):
        copies[j].wait()
        if j + 3 < parts:
            copies[j + 3].start()
        here = slice(j * rows, (j + 1) * rows)
        out_ref[here, :] = unit(raw_ref[here, :].astype(f32)).astype(bf16)


def by_core(core_ref, own, other):
    is_first = core_ref[0] == 0
    return jnp.where(is_first, own, other), jnp.where(is_first, other, own)


def teacher_kernel(stud, glob, core_ref, own_ref, other_ref, unit_ref, exp_ref, sums_ref):
    chips, _, half = own_ref.shape
    width = 2 * half
    at = 2 * stud
    blocks = by_core(core_ref, own_ref[...].astype(f32)[:, at:], other_ref[...].astype(f32)[:, at:])
    block = jnp.concatenate(blocks, axis=0)
    groups = 2 * chips
    at = 2 * glob
    g = wide(block[:, :glob], block[:, glob:at]).reshape(groups * glob, width)
    q = wide(block[:, at : at + 8], block[:, at + 8 : at + 16]).reshape(groups * 8, width)
    r = block[:, at + 16 :].reshape(chips, 2, 8, half)
    turned = jnp.concatenate([r[:, :, 4:], r[:, :, :4]], axis=2)
    top = iota((chips, 8, half), 1) < 4
    r = wide(jnp.where(top, r[:, 0], turned[:, 1]), jnp.where(top, turned[:, 0], r[:, 1]))
    r = r.reshape(groups * 4, width)
    teach = jnp.concatenate([g, q, r], axis=0).astype(bf16)
    step = 256
    for start in range(0, unit_ref.shape[0], step):
        here = slice(start, start + step)
        exps = jnp.exp2(nt_dot(teach, unit_ref[here, :]) * TEACHER_EXP2)
        exp_ref[:, here] = exps.astype(bf16)
        sums = jnp.sum(exps, axis=0, keepdims=True)
        for k in range(step // LANES):
            at = start // LANES + k
            sums_ref[at : at + 1, :] = sums[:, k * LANES : (k + 1) * LANES]


def other_core_kernel(stud, glob, own_ref, unit_ref, exp_ref):
    chips, _, half = own_ref.shape
    at = 2 * stud
    block = own_ref[...].astype(f32)[:, at : at + 2 * glob]
    teach = wide(block[:, :glob], block[:, glob:]).reshape(chips * glob, 2 * half).astype(bf16)
    step = 512
    for start in range(0, unit_ref.shape[0], step):
        here = slice(start, start + step)
        exp_ref[:, here] = jnp.exp2(nt_dot(teach, unit_ref[here, :]) * TEACHER_EXP2).astype(bf16)


def add_students(stud, own_ref, unit_ref, stud_ref, acc_ref, tot_ref, start_acc, start_tot):
    chips, _, half = own_ref.shape
    block = own_ref[...].astype(f32)[:, : 2 * stud]
    block = wide(block[:, :stud], block[:, stud:])
    stud_ref[...] = block.reshape(chips * stud, 2 * half).astype(bf16)
    step = 512
    for start in range(0, unit_ref.shape[0], step):
        protos = unit_ref[start : start + step, :]
        weights = jnp.exp2(nt_dot(stud_ref[...], protos) * STUDENT_EXP2)
        part = weights[:, :LANES]
        for k in range(1, step // LANES):
            part = part + weights[:, k * LANES : (k + 1) * LANES]
        term = jnp.dot(weights.astype(bf16), protos, preferred_element_type=f32)
        if start == 0 and start_acc is None:
            tot_ref[...] = part
            acc_ref[...] = term
        elif start == 0:
            tot_ref[...] = start_tot[...] + part
            acc_ref[...] = start_acc[...] + term
        else:
            tot_ref[...] += part
            acc_ref[...] += term


def student_own_kernel(stud, own_ref, unit_ref, acc_ref, tot_ref, stud_ref):
    add_students(stud, own_ref, unit_ref, stud_ref, acc_ref, tot_ref, None, None)


def student_other_kernel(
    stud, own_ref, unit_ref, start_acc, start_tot, attract_ref, total_ref, stud_ref, acc_ref, tot_ref
):
    add_students(stud, own_ref, unit_ref, stud_ref, acc_ref, tot_ref, start_acc, start_tot)
    chips = own_ref.shape[0]
    attract = acc_ref[...].reshape(chips, stud, 2 * LANES)
    attract = jnp.concatenate([attract[:, :, :LANES], attract[:, :, LANES:]], axis=1)
    attract_ref[...] = attract.astype(bf16)
    total = jnp.sum(tot_ref[...], axis=1, keepdims=True).reshape(chips, stud, 1)
    eye = iota((chips, stud, LANES), 1) == iota((chips, stud, LANES), 2)
    total_ref[...] = jnp.sum(
        jnp.where(eye, jnp.broadcast_to(total, (chips, stud, LANES)), 0.0), axis=1, keepdims=True
    )


def pair_kernel(mine_ref, got_ref, out_ref):
    total = (mine_ref[...] + got_ref[...]).astype(bf16)
    for j in range(out_ref.shape[0]):
        out_ref[j] = total


def proto_scale_of(parts_ref):
    total = parts_ref[0].astype(f32)
    for j in range(1, parts_ref.shape[0]):
        total = total + parts_ref[j].astype(f32)
    scale = 1.0 / total
    return jnp.concatenate([scale[k : k + 1, :] for k in range(scale.shape[0])], axis=1)


def col_kernel(parts_ref, exp_ref, out_ref):
    scale = proto_scale_of(parts_ref)
    rows, cols = exp_ref.shape
    lines = []
    for g in range(rows // LANES):
        acc = None
        for k in range(cols // LANES):
            lanes = slice(k * LANES, (k + 1) * LANES)
            term = exp_ref[g * LANES : (g + 1) * LANES, lanes].astype(f32) * scale[:, lanes]
            acc = term if acc is None else acc + term
        lines.append(jnp.sum(acc.T, axis=0, keepdims=True))
    out = jnp.concatenate(lines, axis=1)
    for j in range(out_ref.shape[0]):
        out_ref[j] = out


def row_kernel(parts_ref, exp_ref, out_ref, line_ref):
    rows, cols = exp_ref.shape
    scale = 1.0 / jnp.sum(parts_ref[...], axis=0)
    acc = None
    for g in range(rows // LANES):
        tall = jnp.broadcast_to(scale[:, g * LANES : (g + 1) * LANES], (LANES, LANES)).T
        for t in range(0, LANES, 16):
            scales = jnp.concatenate([tall[t : t + 16]] * (cols // LANES), axis=1)
            term = exp_ref[g * LANES + t : g * LANES + t + 16, :].astype(f32) * scales
            term = term[:8] + term[8:]
            acc = term if acc is None else acc + term
    line = jnp.sum(acc, axis=0, keepdims=True)
    for k in range(cols // LANES):
        line_ref[k : k + 1, :] = line[:, k * LANES : (k + 1) * LANES]
    sums = line_ref[...].astype(bf16)
    for j in range(out_ref.shape[0]):
        out_ref[j] = sums


def add_repel(parts_ref, exps_of, unit_ref, repel, mass):
    scale = proto_scale_of(parts_ref)
    step = 512
    for start in range(0, unit_ref.shape[0], step):
        here = slice(start, start + step)
        terms = exps_of(here).astype(f32) * scale[:, here]
        for k in range(step // LANES):
            mass = mass + terms[:, k * LANES : (k + 1) * LANES]
        repel = repel + jnp.dot(terms.astype(bf16), unit_ref[here, :], preferred_element_type=f32)
    return repel, mass


def repel_own_kernel(core_ref, parts_ref, exp_ref, unit_ref, repel_ref, mass_ref):
    rows = repel_ref.shape[0]
    mine = pl.ds(pl.multiple_of(core_ref[0] * rows, rows), rows)
    repel_ref[...], mass_ref[...] = add_repel(
        parts_ref,
        lambda here: exp_ref[mine, here],
        unit_ref,
        jnp.zeros(repel_ref.shape, f32),
        jnp.zeros(mass_ref.shape, f32),
    )


def repel_other_kernel(
    stud, parts_ref, exp_ref, unit_ref, repel_ref, mass_ref, attract_ref, total_ref, out_ref
):
    repel, mass = add_repel(
        parts_ref, lambda here: exp_ref[:, here], unit_ref, repel_ref[...], mass_ref[...]
    )
    chips = attract_ref.shape[0]
    glob = repel.shape[0] // chips
    repel = repel.reshape(chips, glob, 2 * LANES)
    dims = (chips, glob, LANES)
    place = iota(dims, 1) + stud == iota(dims, 2)
    mass = jnp.sum(mass, axis=1, keepdims=True).reshape(chips, glob, 1)
    mass = jnp.where(place, jnp.broadcast_to(mass, dims), 0.0)
    scalars = total_ref[...] + jnp.sum(mass, axis=1, keepdims=True)
    high = scalars.astype(bf16).astype(f32)
    scalars = jnp.where(iota(dims, 1) == 0, high, scalars - high)
    parts = [attract_ref[...].astype(f32), repel[:, :, :LANES], repel[:, :, LANES:], scalars]
    out_ref[...] = jnp.concatenate(parts, axis=1).astype(bf16)


def final_kernel(back_ref, student_ref, grad_ref, loss_ref, rows_ref):
    crops, images, width = student_ref.shape
    stud = crops * images
    for c in range(crops):
        rows_ref[c * images : (c + 1) * images, :] = student_ref[c].astype(f32)
    values = rows_ref[...]
    back = jnp.sum(back_ref[...].astype(f32), axis=0)
    attract = wide(back[:stud], back[stud : 2 * stud])
    back = back[2 * stud :]
    line = back[16:17] + back[17:18]
    sub, lane = iota((stud, LANES), 0), iota((stud, LANES), 1)
    lines = jnp.broadcast_to(line, (stud, LANES))
    total = jnp.sum(jnp.where(lane == sub, lines, 0.0), axis=1, keepdims=True)
    mass = jnp.sum(jnp.where(lane == sub + stud, lines, 0.0)[:8], axis=1, keepdims=True)
    views = wide(back[:8], back[8:16]) / mass
    both = views + jnp.concatenate([views[images:], views[:images]], axis=0)
    repel = jnp.concatenate([views] + [both] * (stud // 8 - 1), axis=0)
    pairs = jnp.where(iota((stud, 1), 0) < 2 * images, 1.0, 2.0)
    inv_norm = lax.rsqrt(jnp.sum(values * values, axis=1, keepdims=True) + NORM_EPSILON)
    own = values * inv_norm
    low = own.astype(bf16).astype(f32)
    grad_unit = (pairs * attract / total - repel) / STUDENT_SOFTNESS
    cross = jnp.sum(low * repel, axis=1, keepdims=True) / STUDENT_SOFTNESS
    loss = pairs * jnp.log(total) - cross
    inner = jnp.sum(own * grad_unit, axis=1, keepdims=True)
    grad = inv_norm * (grad_unit - own * inner)
    for c in range(crops):
        grad_ref[c] = grad[c * images : (c + 1) * images]
    spreads = jnp.broadcast_to(loss, (stud, LANES))
    for i in range(images):
        spread = jnp.where(sub == lane * images + i, spreads, 0.0)
        loss_ref[i : i + 1, :] = jnp.sum(spread, axis=0, keepdims=True)[:, :crops]


def exchange(array, axis, **kw):
    return lax.all_to_all(array, axis, 0, 0, tiled=True, **kw)


def body(teacher_global, queue, student, prototypes):
    images, crops, width = student.shape
    queue_rows = queue.shape[0]
    groups, parts = lax.axis_size("proto"), lax.axis_size("dp")
    chips = groups // 2
    stud, glob = images * crops, images * 2
    teach_rows = groups * (glob + queue_rows)
    protos = prototypes.shape[0]
    student = jnp.transpose(student, (1, 0, 2))
    core = jnp.reshape(lax.axis_index("proto") & 1, (1,))
    core, student = lax.optimization_barrier((core, student))
    scalar = pl.BlockSpec(memory_space=pltpu.SMEM)
    vmem = pl.BlockSpec(memory_space=pltpu.VMEM)

    def swap(array):
        return lax.ppermute(array, "proto", [(j, j ^ 1) for j in range(groups)])

    send_rows = 2 * (stud + glob + queue_rows)
    packed = call(
        pack_kernel,
        "pack_rows",
        shape((chips, send_rows, LANES), bf16),
        scratch_shapes=[pltpu.VMEM((send_rows, LANES), f32)],
    )(*map(in_hbm, (student, teacher_global, queue)))
    same_core = [list(range(c, groups, 2)) for c in range(2)]
    own_rows = exchange(packed, "proto", axis_index_groups=same_core)
    other_rows = swap(own_rows)
    own_rows, prototypes = lax.optimization_barrier((own_rows, prototypes))
    unit_protos = call(
        unit_kernel,
        "unit_prototypes",
        shape((protos, width), bf16),
        in_specs=[pl.BlockSpec(memory_space=pl.ANY)],
        scratch_shapes=[pltpu.VMEM((protos, width), bf16), pltpu.SemaphoreType.DMA((8,))],
        flops=3 * protos * width,
        nbytes=4 * protos * width,
    )(in_hbm(prototypes))

    other_rows, unit_protos = lax.optimization_barrier((other_rows, unit_protos))
    other_protos = swap(unit_protos)
    exps, row_parts = call(
        functools.partial(teacher_kernel, stud, glob),
        "teacher_exponentials",
        [pltpu.VMEM((teach_rows, protos), bf16), shape((protos // LANES, LANES), f32)],
        in_specs=[scalar, vmem, vmem, vmem],
        flops=2 * teach_rows * protos * width,
        nbytes=2 * teach_rows * protos,
        exps=teach_rows * protos,
    )(core, own_rows, other_rows, unit_protos)
    exps = in_vmem(exps)

    row_parts, own_rows = lax.optimization_barrier((row_parts, own_rows))
    half = parts // 2
    got_sums = lax.ppermute(row_parts, "dp", [(j, (j + half) % parts) for j in range(parts)])
    own_students = chips * stud
    work = dict(
        flops=4 * own_students * protos * width,
        nbytes=2 * protos * width,
        exps=own_students * protos,
    )
    rows_scratch = pltpu.VMEM((own_students, width), bf16)
    acc, tot = call(
        functools.partial(student_own_kernel, stud),
        "students_own_core",
        [shape((own_students, width), f32), shape((own_students, LANES), f32)],
        scratch_shapes=[rows_scratch],
        **work,
    )(own_rows, unit_protos)
    attract, total = call(
        functools.partial(student_other_kernel, stud),
        "students_other_core",
        [shape((chips, 2 * stud, LANES), bf16), shape((chips, 1, LANES), f32)],
        scratch_shapes=[
            rows_scratch,
            pltpu.VMEM((own_students, width), f32),
            pltpu.VMEM((own_students, LANES), f32),
        ],
        **work,
    )(own_rows, other_protos, acc, tot)
    got_sums, attract, total = lax.optimization_barrier((got_sums, attract, total))
    row_parts = call(pair_kernel, "add_halves", shape((half, protos // LANES, LANES), bf16))(row_parts, got_sums)
    halves = [list(range(half)), list(range(half, parts))]
    row_parts = exchange(row_parts, "dp", axis_index_groups=halves)

    for iteration in range(SINK_ITERS - 1):
        col_parts = call(
            col_kernel,
            "sum_over_prototypes",
            shape((groups, 1, teach_rows), f32),
            flops=2 * teach_rows * protos,
            nbytes=2 * teach_rows * protos,
        )(row_parts, exps)
        col_parts = exchange(col_parts, "proto")
        row_parts = call(
            row_kernel,
            "sum_over_rows",
            shape((parts, protos // LANES, LANES), bf16),
            scratch_shapes=[pltpu.VMEM((protos // LANES, LANES), f32)],
            flops=2 * teach_rows * protos,
            nbytes=2 * teach_rows * protos,
        )(col_parts, exps)
        row_parts = exchange(row_parts, "dp")

    row_parts, own_rows = lax.optimization_barrier((row_parts, own_rows))
    other_parts = swap(row_parts)
    own_glob = chips * glob
    other_exps = call(
        functools.partial(other_core_kernel, stud, glob),
        "teacher_other_core",
        pltpu.VMEM((own_glob, protos), bf16),
        flops=2 * own_glob * protos * width,
        nbytes=2 * protos * width,
        exps=own_glob * protos,
    )(own_rows, other_protos)
    other_exps = in_vmem(other_exps)
    work = dict(flops=2 * own_glob * protos * width, nbytes=4 * protos * width)
    repel, mass = call(
        repel_own_kernel,
        "repel_own_core",
        [shape((own_glob, width), f32), shape((own_glob, LANES), f32)],
        in_specs=[scalar] + [vmem] * 3,
        **work,
    )(core, row_parts, exps, unit_protos)
    back = call(
        functools.partial(repel_other_kernel, stud),
        "repel_other_core",
        shape((chips, 2 * stud + 2 * glob + 8, LANES), bf16),
        **work,
    )(other_parts, other_exps, other_protos, repel, mass, attract, total)
    back = exchange(back, "proto", axis_index_groups=same_core)

    grad, loss = call(
        final_kernel,
        "gradients",
        [shape((crops, images, width), f32), shape((images, crops), f32)],
        scratch_shapes=[pltpu.VMEM((stud, width), f32)],
    )(back, student)
    return jnp.transpose(grad, (1, 0, 2)), loss


def solution(mesh):
    in_specs = (
        P(("dp", "proto"), None, None),
        P(("dp", "proto"), None),
        P(("dp", "proto"), None, None),
        P("proto", None),
    )
    out_specs = (P(("dp", "proto"), None, None), P(("dp", "proto"), None))
    return jax.shard_map(body, mesh=mesh, in_specs=in_specs, out_specs=out_specs, check_vma=False)
```
